128 devices in a mesh: seq: 8 (over x, z_lo), tp: 16 (over z_hi, y, core).
Axes of the slice: x: 4, y: 4, z: 4 (z_hi: 2, z_lo: 2; z = z_hi * 2 + z_lo), core: 2. Of those that a mesh axis runs over, the one named last changes fastest.
Arguments:
- tokens: bfloat16 [16384, 2048], P('seq', 'tp'), may hold values from -6 to 6
- gain_first: bfloat16 [2048], P('tp'), may hold values from 0.5 to 1.5
- gain_second: bfloat16 [2048], P('tp'), may hold values from 0.5 to 1.5
- w_in: bfloat16 [2048, 3, 2048], P('seq', None, 'tp'), may hold values from -0.125 to 0.125
- conv_w: bfloat16 [3, 3, 2048], P(None, None, 'tp'), may hold values from -4 to 4
- log_rate: bfloat16 [16, 2048], P(None, 'tp')
- residue: bfloat16 [16, 2048], P(None, 'tp')
- skip: bfloat16 [2048], P('tp'), may hold values from -3 to 3
- w_out: bfloat16 [2048, 2048], P('tp', 'seq'), may hold values from -0.125 to 0.125
- w_gate: bfloat16 [2048, 5632], P('seq', 'tp'), may hold values from -0.125 to 0.125
- w_up: bfloat16 [2048, 5632], P('seq', 'tp'), may hold values from -0.125 to 0.125
- w_down: bfloat16 [5632, 2048], P('tp', 'seq'), may hold values from -0.078125 to 0.078125
- cotangent: bfloat16 [16384, 2048], P('seq', 'tp'), may hold values from -6 to 6
- lengths: int32 [8], replicated, may hold values from 1 to 14337, 16384 in all
Outputs:
- mixed: bfloat16 [16384, 2048], P('seq', 'tp')
- grad_tokens: float32 [16384, 2048], P('seq', 'tp')
- grad_gain_first: float32 [2048], P('tp')
- grad_gain_second: float32 [2048], P('tp')
- grad_w_in: float32 [2048, 3, 2048], P('seq', None, 'tp')
- grad_conv: float32 [3, 3, 2048], P(None, None, 'tp')
- grad_rate: float32 [16, 2048], P(None, 'tp')
- grad_residue: float32 [16, 2048], P(None, 'tp')
- grad_skip: float32 [2048], P('tp')
- grad_w_out: float32 [2048, 2048], P('tp', 'seq')
- grad_w_gate: float32 [2048, 5632], P('seq', 'tp')
- grad_w_up: float32 [2048, 5632], P('seq', 'tp')
- grad_w_down: float32 [5632, 2048], P('tp', 'seq')
The draws below stay inside these ranges and needn't reach their ends.
Inputs may be any that keep to these rules, and one draw needn't show every extreme that they name: The lengths sum to 16384; exactly one document has the largest length 14337.
All inputs are finite; a program needn't handle non-finite values.
Results may differ from the reference program's by a relative error of at most 0.025.
Values may be sent and summed in bfloat16 or wider, within the bound.
A program may use at most 256 MiB of HBM per device.

```python
import math
import jax
import jax.numpy as jnp
import numpy as np
from jax import lax

D = 2048
FF = 5632
POLES = 16
DOCS = 8
TOK_DEV = 2048
TOKENS = 16384


def pole_rates(key, share):
    slow_key, fast_key, pick_key = jax.random.split(key, 3)
    slow = jnp.exp(jax.random.uniform(slow_key, (POLES, D), jnp.float32, jnp.log(0.1 / TOKENS), jnp.log(2.0 / TOKENS)))
    fast = jnp.exp(jax.random.uniform(fast_key, (POLES, D), jnp.float32, jnp.log(0.04), jnp.log(0.15)))
    pick = jax.random.uniform(pick_key, (POLES, D), jnp.float32) < share
    return jnp.where(pick, slow, fast)


def draw_log_rate(key, part):
    share = 0.5
    rates = pole_rates(key, share)
    return jnp.log(rates).astype(jnp.bfloat16)


def draw_residue(key, part):
    share = 0.5
    rates = pole_rates(key, share)
    key = jax.random.fold_in(key, 2)
    return (0.35 * jnp.sqrt(2.0 * rates) * jax.random.normal(key, (POLES, D), jnp.float32)).astype(jnp.bfloat16)


def steps_of(stream_key, dims, cuts, least, top_value):
    level = 1.0
    for dim, shards_of in cuts:
        heights = jax.random.uniform(jax.random.fold_in(jax.random.fold_in(stream_key, 6), dim), (shards_of,), jnp.float32, least / len(cuts), top_value / len(cuts))
        level = level * jnp.repeat(jnp.exp(heights), dims[dim] // shards_of).reshape((-1,) + (1,) * (len(dims) - 1 - dim))
    return level


def split_up(count, total, bound, skew):
    loads = [(1 << 20) // math.isqrt(grade ** skew) + 1 for grade in range(2, count + 1)]
    spare, holding = total - bound - (count - 1), [1] * (count - 1)
    while spare > 0:
        free = [i for i in range(count - 1) if holding[i] < bound]
        mass, remaining = sum([loads[i] for i in free]), spare
        for i in free:
            addition = min(bound - holding[i], max(1, remaining * loads[i] // mass), spare)
            holding[i] = holding[i] + addition
            spare = spare - addition
    return np.array([bound] + holding)


def ragged_sizes(own_key, count, total, reach, slope):
    if count == 2:
        one = jax.random.randint(own_key, (), max(1, total - reach), min(reach, total - 1) + 1)
        return jnp.stack([one, total - one])
    tallies = jnp.asarray(split_up(count, total, reach, slope), jnp.int32)
    twos = (count - 1) // 2
    source_of, taker = tallies[1:1 + 2 * twos:2], tallies[2:2 + 2 * twos:2]
    slack = jnp.minimum(source_of - 1, reach - taker)
    moved = jax.random.randint(jax.random.fold_in(own_key, 1), (twos,), 0, 1 << 20) % (slack + 1)
    tallies = tallies.at[1:1 + 2 * twos:2].set(source_of - moved).at[2:2 + 2 * twos:2].set(taker + moved)
    return tallies[jax.random.permutation(jax.random.fold_in(own_key, 2), count)]


def noise(key, dims, spread, limit, cuts=(), held_as=jnp.bfloat16):
    entries = spread * jax.random.normal(key, dims, jnp.float32)
    if cuts:
        entries = entries * steps_of(key, dims, cuts, -0.22, 0.18)
    return jnp.clip(entries, -limit, limit).astype(held_as)


def setup_inputs(seed: int = 0) -> dict:
    streams_of = jax.random.split(jax.random.key(seed), 15)
    return {
        "tokens": noise(streams_of[0], (TOKENS, D), 1.0, 6.0, ((0, 8), (1, 16))),
        "gain_first": jnp.clip(1.0 + 0.1 * jax.random.normal(streams_of[1], (D,), jnp.float32), 0.5, 1.5).astype(jnp.bfloat16),
        "gain_second": jnp.clip(1.0 + 0.1 * jax.random.normal(streams_of[2], (D,), jnp.float32), 0.5, 1.5).astype(jnp.bfloat16),
        "w_in": noise(streams_of[3], (D, 3, D), D ** -0.5, 0.125, ((0, 8), (2, 16))),
        "conv_w": noise(streams_of[4], (3, 3, D), 0.6, 4.0, ((2, 16),)),
        "log_rate": draw_log_rate(jax.random.fold_in(streams_of[14], 71), 0),
        "residue": draw_residue(jax.random.fold_in(streams_of[14], 71), 0),
        "skip": noise(streams_of[7], (D,), 0.5, 3.0, ((0, 16),)),
        "w_out": noise(streams_of[8], (D, D), D ** -0.5, 0.125, ((0, 16), (1, 8))),
        "w_gate": noise(streams_of[9], (D, FF), D ** -0.5, 0.125, ((0, 8), (1, 16))),
        "w_up": noise(streams_of[10], (D, FF), D ** -0.5, 0.125, ((0, 8), (1, 16))),
        "w_down": noise(streams_of[11], (FF, D), FF ** -0.5, 0.078125, ((0, 16), (1, 8))),
        "cotangent": noise(streams_of[12], (TOKENS, D), 1.0, 6.0, ((0, 8), (1, 16))),
        "lengths": ragged_sizes(streams_of[13], DOCS, TOKENS, TOKENS - TOK_DEV + 1, 2).astype(jnp.int32),
    }


EPS = 1e-06
HIGH = lax.Precision.HIGHEST

@jax.custom_vjp
def low(v):
    return lax.optimization_barrier(v.astype(jnp.bfloat16)).astype(jnp.float32)

@jax.custom_vjp
def low_back(v):
    return v

def low_keep(v):
    return (low(v), None)

def low_pass(kept, grad):
    return (grad,)

def back_keep(v):
    return (v, None)

def back_low(kept, grad):
    return (low(grad),)
low.defvjp(low_keep, low_pass)
low_back.defvjp(back_keep, back_low)

def doc_ids(lengths, first, count):
    ends = jnp.cumsum(lengths.astype(jnp.int32))[:-1]
    places = first + jnp.arange(count, dtype=jnp.int32)
    ids = lax.optimization_barrier(jnp.sum((places[:, None] >= ends[None, :]).astype(jnp.int32), axis=1))
    return jnp.where(places >= 0, ids, -1).astype(jnp.int32)

def modal_blocks(z, log_rate, residue, docs, prev_doc):
    total, chans = z.shape
    block = min(128, total)
    count = total // block
    rate = jnp.exp(log_rate)
    steps = jnp.arange(block, dtype=jnp.float32)
    fall = jnp.exp(-rate[:, None, :] * steps[None, :, None])
    lift = jnp.exp(rate[:, None, :] * steps[None, :, None])
    entry = fall * jnp.exp(-rate)[:, None, :] * residue[:, None, :]
    tail = jnp.exp(-rate[:, None, :] * (block - 1.0 - steps)[None, :, None])
    whole = jnp.exp(-rate * block)
    causal = (steps[:, None] >= steps[None, :]).astype(jnp.float32)
    kernel = jnp.einsum('ntc,nsc->cts', fall * residue[:, None, :], lift, precision=HIGH) * causal[None]
    z_blocks = z.reshape(count, block, chans)
    d_blocks = docs.reshape(count, block)
    prior = jnp.concatenate([jnp.reshape(prev_doc, (1,)).astype(jnp.int32), docs[block - 1::block][:-1].astype(jnp.int32)])

    def step(state, item):
        z_here, d_here, d_prior = item
        same = (d_here[:, None] == d_here[None, :]).astype(jnp.float32)
        local = jnp.einsum('cts,sc->tc', kernel * same[None], z_here, precision=HIGH)
        keep = (d_here == d_prior).astype(jnp.float32)
        carried = jnp.einsum('ntc,nc->tc', entry * keep[None, :, None], state, precision=HIGH)
        final_doc = (d_here == d_here[block - 1]).astype(jnp.float32)
        fresh = jnp.einsum('nsc,sc->nc', tail, z_here * final_doc[:, None], precision=HIGH)
        state = whole * keep[block - 1] * state + fresh
        return (state, local + carried)
    start = jnp.zeros(rate.shape, jnp.float32)
    final, outs = lax.scan(jax.checkpoint(step), start, (z_blocks, d_blocks, prior))
    return (outs.reshape(total, chans), final)

def forward(tokens, gain_first, gain_second, w_in, conv_w, log_rate, residue, skip, w_out, w_gate, w_up, w_down, docs):
    r1 = lax.rsqrt(lax.optimization_barrier(jnp.mean(tokens * tokens, axis=1, keepdims=True)) + EPS)
    xn = low(tokens * r1 * gain_first)
    proj = low_back(jnp.einsum('td,djc->tjc', xn, w_in, precision=HIGH))
    same1 = jnp.concatenate([jnp.zeros((1,), jnp.float32), (docs[1:] == docs[:-1]).astype(jnp.float32)])
    same2 = jnp.concatenate([jnp.zeros((2,), jnp.float32), (docs[2:] == docs[:-2]).astype(jnp.float32)])
    back1 = jnp.concatenate([jnp.zeros_like(proj[:1]), proj[:-1]])
    back2 = jnp.concatenate([jnp.zeros_like(proj[:2]), proj[:-2]])
    short = conv_w[0] * proj + conv_w[1] * same1[:, None, None] * back1 + conv_w[2] * same2[:, None, None] * back2
    query, key_part, value = (short[:, 0], short[:, 1], short[:, 2])
    z = key_part * value
    filtered, ignored = modal_blocks(z, log_rate, residue, docs, jnp.int32(-1))
    u = filtered + skip * z
    gated = low(query * u)
    mixer = low_back(jnp.dot(gated, w_out, precision=HIGH))
    hidden = tokens + mixer
    r2 = lax.rsqrt(lax.optimization_barrier(jnp.mean(hidden * hidden, axis=1, keepdims=True)) + EPS)
    hn = low(hidden * r2 * gain_second)
    gate = low_back(jnp.dot(hn, w_gate, precision=HIGH))
    upper = low_back(jnp.dot(hn, w_up, precision=HIGH))
    act = low(jax.nn.silu(gate) * upper)
    return hidden + jnp.dot(act, w_down, precision=HIGH)

def reference(tokens, gain_first, gain_second, w_in, conv_w, log_rate, residue, skip, w_out, w_gate, w_up, w_down, cotangent, lengths):
    docs = doc_ids(lengths, jnp.int32(0), TOKENS)
    floats = [a.astype(jnp.float32) for a in (tokens, gain_first, gain_second, w_in, conv_w, log_rate, residue, skip, w_out, w_gate, w_up, w_down)]

    def whole_block(*params):
        return forward(*params, docs)
    out, pull = jax.vjp(whole_block, *floats)
    grads = pull(cotangent.astype(jnp.float32))
    return (out.astype(jnp.bfloat16), grads[0], grads[1], grads[2], grads[3], grads[4], grads[5], grads[6], grads[7], grads[8], grads[9], grads[10], grads[11])
```

```python
import functools

import jax
import jax.numpy as jnp
from jax import lax
from jax.experimental import pallas as pl
from jax.experimental.pallas import tpu as pltpu
from jax.sharding import Mesh
from jax.sharding import PartitionSpec as P

EPS = 1e-06
DOCS = 8
ROW_AXES = ("x", "zl", "zh")
COL_AXES = ("y", "c")
F32 = jnp.float32
BF16 = jnp.bfloat16
VMEM_LIMIT = 60 * 1024 * 1024
SEGS = 8
LANES = 128


def spread(row):
    return jnp.broadcast_to(row, (SEGS, LANES))


def seg_rows():
    return lax.broadcasted_iota(jnp.int32, (SEGS, LANES), 0)


def tile(i):
    return pl.ds(pl.multiple_of(i * SEGS, SEGS), SEGS)


def lanes_of(b, j=0):
    return slice(LANES * (b + j), LANES * (b + j + 1))


def add_all(terms):
    while len(terms) > 1:
        terms = [sum(terms[i + 1 : i + 2], terms[i]) for i in range(0, len(terms), 2)]
    return terms[0]


def scan_up(ends, factor):
    rows = seg_rows()
    for by in (1, 2, 4):
        held = rows >= by
        ends = ends + factor * jnp.where(held, pltpu.roll(ends, by, 0), 0.0)
        factor = factor * jnp.where(held, pltpu.roll(factor, by, 0), 1.0)
    return ends


def scan_down(ends, factor):
    rows = seg_rows()
    for by in (1, 2, 4):
        held = rows < SEGS - by
        ends = ends + factor * jnp.where(held, pltpu.roll(ends, SEGS - by, 0), 0.0)
        factor = factor * jnp.where(held, pltpu.roll(factor, SEGS - by, 0), 1.0)
    return ends


def entering_up(ends, factor, enter):
    first = seg_rows() == 0
    whole = scan_up(ends + jnp.where(first, factor * enter, 0.0), factor)
    return jnp.where(first, enter, pltpu.roll(whole, 1, 0))


def entering_down(ends, factor, enter):
    last = seg_rows() == SEGS - 1
    whole = scan_down(ends + jnp.where(last, factor * enter, 0.0), factor)
    return jnp.where(last, enter, pltpu.roll(whole, SEGS - 1, 0))


def rows_of(ref, count, lanes):
    return [spread(ref[n : n + 1, lanes]) for n in range(count)]


def tap_rows(taps, lanes):
    return [[spread(taps[3 * i + j : 3 * i + j + 1, lanes]) for j in range(3)] for i in range(3)]


def conv_first(b, p, halo, taps, m1, m2, dec, dec_seg, q_out, z_out, k_out, v_out, ends_out, open_out, last_out):
    seg = p.shape[0] // SEGS
    poles = dec.shape[0]
    own = lanes_of(b)
    cols = [lanes_of(3 * b, j) for j in range(3)]
    first = seg_rows() == 0
    d = rows_of(dec, poles, own)
    c = tap_rows(taps, own)

    def before(j, back):
        mine = pltpu.roll(p[SEGS * (seg - back) : SEGS * (seg - back + 1), cols[j]], 1, 0)
        theirs = pltpu.roll(halo[SEGS * (2 - back) : SEGS * (3 - back), cols[j]], 1, 0)
        return jnp.where(first, theirs, mine)

    def step(i, carry):
        state, prev1, prev2, free = carry
        place = tile(i)
        one, two = m1[place, :], m2[place, :]
        cur = [p[place, cols[j]] for j in range(3)]
        q, k, v = [
            c[0][j] * cur[j] + c[1][j] * (one * prev1[j]) + c[2][j] * (two * prev2[j])
            for j in range(3)
        ]
        z = k * v
        q_out[place, own] = q
        k_out[place, own] = k
        v_out[place, own] = v
        z_out[place, own] = z
        state = [d[n] * (one * state[n]) + z for n in range(poles)]
        return (state, cur, prev1, free * one)

    zero = jnp.zeros((SEGS, LANES), F32)
    start = (
        [zero] * poles,
        [before(j, 1) for j in range(3)],
        [before(j, 2) for j in range(3)],
        zero + 1.0,
    )
    state, _, _, free = lax.fori_loop(0, seg, step, start)
    open_out[:, own] = free
    for n in range(poles):
        ends_out[SEGS * n : SEGS * (n + 1), own] = state[n]
        whole = scan_up(state[n], spread(dec_seg[n : n + 1, own]) * free)
        last_out[n : n + 1, own] = whole[SEGS - 1 :, :]


def conv_second(b, q_in, z_in, m1, ends, free, enter, dec, dec_seg, res, skip, u_out, gated_out):
    rows = q_in.shape[0]
    seg = rows // SEGS
    poles = dec.shape[0]
    own = lanes_of(b)
    d = rows_of(dec, poles, own)
    r = rows_of(res, poles, own)
    sk = spread(skip[0:1, own])
    start = [
        entering_up(
            ends[SEGS * n : SEGS * (n + 1), own],
            spread(dec_seg[n : n + 1, own]) * free[:, own],
            spread(enter[n : n + 1, own]),
        )
        for n in range(poles)
    ]

    def step(i, state):
        place = tile(i)
        one, z = m1[place, :], z_in[place, own]
        state = [d[n] * (one * state[n]) + z for n in range(poles)]
        u_out[place, own] = add_all([r[n] * state[n] for n in range(poles)] + [sk * z])
        return state

    lax.fori_loop(0, seg, step, start)

    def rounded(i, _):
        place = pl.ds(pl.multiple_of(i * 64, 64), 64)
        gated_out[place, own] = (q_in[place, own] * u_out[place, own]).astype(BF16)
        return 0

    lax.fori_loop(0, rows // 64, rounded, 0)


def back_first(b, gg_in, q_in, m1, free, dec, dec_seg, ends_out, last_out):
    seg = q_in.shape[0] // SEGS
    poles = dec.shape[0]
    own = lanes_of(b)
    d = rows_of(dec, poles, own)

    def step(t, carry):
        place = tile(seg - 1 - t)
        gu = gg_in[place, own] * q_in[place, own]
        one = m1[place, :]
        return [d[n] * (one * (carry[n] + gu)) for n in range(poles)]

    zero = jnp.zeros((SEGS, LANES), F32)
    carry = lax.fori_loop(0, seg, step, [zero] * poles)
    for n in range(poles):
        ends_out[SEGS * n : SEGS * (n + 1), own] = carry[n]
        whole = scan_down(carry[n], spread(dec_seg[n : n + 1, own]) * free[:, own])
        last_out[n : n + 1, own] = whole[:1, :]


def keep_states(b, part, z_in, m1, ends, enter, free, dec, dec_seg, kept):
    seg = z_in.shape[0] // SEGS
    half = dec.shape[0] // 2
    own = lanes_of(b)
    these = range(half * part, half * (part + 1))
    d = [spread(dec[n : n + 1, own]) for n in these]
    start = [
        entering_up(
            ends[SEGS * n : SEGS * (n + 1), own],
            spread(dec_seg[n : n + 1, own]) * free[:, own],
            spread(enter[n : n + 1, own]),
        )
        for n in these
    ]

    def forward(i, state):
        place = tile(i)
        one, z = m1[place, :], z_in[place, own]
        state = [d[n] * (one * state[n]) + z for n in range(half)]
        for n in range(half):
            kept[i, n] = state[n]
        return state

    lax.fori_loop(0, seg, forward, start)


def back_poles(
    b, part, gg_in, u_in, q_in, z_in, m1, back_ends, back_enter, free, dec, dec_seg, res, skip,
    res_out, rate_out, skip_out, kept, gq, gz,
):
    seg = q_in.shape[0] // SEGS
    half = dec.shape[0] // 2
    own = lanes_of(b)
    zero = jnp.zeros((SEGS, LANES), F32)
    sk = spread(skip[0:1, own])
    these = range(half * part, half * (part + 1))
    d = [spread(dec[n : n + 1, own]) for n in these]
    r = [spread(res[n : n + 1, own]) for n in these]
    carry = [
        entering_down(
            back_ends[SEGS * n : SEGS * (n + 1), own],
            spread(dec_seg[n : n + 1, own]) * free[:, own],
            spread(back_enter[n : n + 1, own]),
        )
        for n in these
    ]

    def backward(t, held):
        carry, by_res, by_rate, by_skip = held
        i = seg - 1 - t
        place = tile(i)
        gg, one = gg_in[place, own], m1[place, :]
        gu = gg * q_in[place, own]
        s = [kept[i, n] for n in range(half)]
        lam = [carry[n] + gu for n in range(half)]
        terms = [r[n] * lam[n] for n in range(half)]
        if part == 0:
            terms.append(sk * gu)
            by_skip = by_skip + gu * z_in[place, own]
            gq[place, :] = gg * u_in[place, own]
        else:
            terms.append(gz[place, :])
        gz[place, :] = add_all(terms)
        by_res = [by_res[n] + gu * s[n] for n in range(half)]
        by_rate = [by_rate[n] + carry[n] * s[n] for n in range(half)]
        carry = [d[n] * (one * lam[n]) for n in range(half)]
        return (carry, by_res, by_rate, by_skip)

    _, by_res, by_rate, by_skip = lax.fori_loop(
        0, seg, backward, (carry, [zero] * half, [zero] * half, zero)
    )
    for k, n in enumerate(these):
        res_out[n : n + 1, own] = jnp.sum(by_res[k], axis=0, keepdims=True)
        rate_out[n : n + 1, own] = jnp.sum(by_rate[k], axis=0, keepdims=True)
    if part == 0:
        skip_out[:, own] = by_skip


def back_taps(b, v_in, k_in, p, halo, taps, m1, m2, gp_out, edge_out, conv_out, gq, gz):
    seg = p.shape[0] // SEGS
    own = lanes_of(b)
    cols = [lanes_of(3 * b, j) for j in range(3)]
    zero = jnp.zeros((SEGS, LANES), F32)
    c = tap_rows(taps, own)
    last = seg_rows() == SEGS - 1

    def short_grads(place):
        g = gz[place, :]
        return [gq[place, :], g * v_in[place, own], g * k_in[place, own]]

    def next_seg(value):
        return jnp.where(last, 0.0, pltpu.roll(value, SEGS - 1, 0))

    g0, g1 = short_grads(tile(0)), short_grads(tile(1))
    a1 = [m1[tile(0), :] * g for g in g0]
    b1 = [m2[tile(0), :] * g for g in g0]
    b2 = [m2[tile(1), :] * g for g in g1]
    for j in range(3):
        edge_out[0:8, cols[j]] = a1[j]
        edge_out[8:16, cols[j]] = b1[j]
        edge_out[16:24, cols[j]] = b2[j]

    def taps_back(t, held):
        late1, late2, later2, sums = held
        place = tile(seg - 1 - t)
        one, two = m1[place, :], m2[place, :]
        g = short_grads(place)
        new = []
        for j in range(3):
            value = p[place, cols[j]]
            gp_out[place, cols[j]] = c[0][j] * g[j] + c[1][j] * late1[j] + c[2][j] * later2[j]
            new += [
                sums[3 * j] + g[j] * value,
                sums[3 * j + 1] + late1[j] * value,
                sums[3 * j + 2] + later2[j] * value,
            ]
        return ([one * x for x in g], [two * x for x in g], late2, new)

    start = (
        [next_seg(x) for x in a1],
        [next_seg(x) for x in b1],
        [next_seg(x) for x in b2],
        [zero] * 9,
    )
    _, _, _, sums = lax.fori_loop(0, seg, taps_back, start)
    for j in range(3):
        old1, old2 = halo[15:16, cols[j]], halo[7:8, cols[j]]
        conv_out[j : j + 1, own] = jnp.sum(sums[3 * j], axis=0, keepdims=True)
        conv_out[3 + j : 4 + j, own] = jnp.sum(sums[3 * j + 1], axis=0, keepdims=True) + a1[j][:1] * old1
        conv_out[6 + j : 7 + j, own] = (
            jnp.sum(sums[3 * j + 2], axis=0, keepdims=True) + b1[j][:1] * old2 + b2[j][:1] * old1
        )


def mend_edges(b, taps, edge_in, gp_out):
    rows = gp_out.shape[0]
    own = lanes_of(b)
    cols = [lanes_of(3 * b, j) for j in range(3)]
    c = tap_rows(taps, own)
    last = seg_rows() == SEGS - 1
    for j in range(3):
        one = pltpu.roll(edge_in[0:8, cols[j]], SEGS - 1, 0)
        two = pltpu.roll(edge_in[8:16, cols[j]], SEGS - 1, 0)
        three = pltpu.roll(edge_in[16:24, cols[j]], SEGS - 1, 0)
        near, far = slice(rows - 8, rows), slice(rows - 16, rows - 8)
        gp_out[near, cols[j]] = gp_out[near, cols[j]] + jnp.where(last, c[1][j] * one + c[2][j] * three, 0.0)
        gp_out[far, cols[j]] = gp_out[far, cols[j]] + jnp.where(last, c[2][j] * two, 0.0)


class Links:
    def __init__(self, sends, recvs):
        self.sends, self.recvs, self.used, self.open = sends, recvs, 0, []
        self.x, self.y, self.c = lax.axis_index("x"), lax.axis_index("y"), lax.axis_index("c")
        self.zl, self.zh = lax.axis_index("zl"), lax.axis_index("zh")
        self.z = 2 * self.zh + self.zl

    def at_y(self, by):
        return lax.rem(self.y + by + 4, 4)

    def at_x(self, by):
        return lax.rem(self.x + by + 4, 4)

    def at_z(self, by):
        return lax.rem(self.z + by + 4, 4)

    def to_y(self, by):
        return {"y": self.at_y(by)}

    def to_x(self, by):
        return {"x": self.at_x(by)}

    def to_z(self, by):
        z = self.at_z(by)
        return {"zh": lax.div(z, 2), "zl": lax.rem(z, 2)}

    def sibling(self):
        return {"c": 1 - self.c}

    def send(self, src, dst, device):
        i = self.used
        self.used += 1
        copy = pltpu.make_async_remote_copy(
            src_ref=src,
            dst_ref=dst,
            send_sem=self.sends.at[i],
            recv_sem=self.recvs.at[i],
            device_id=device,
            device_id_type=pl.DeviceIdType.MESH,
        )
        copy.start()
        self.open.append(copy)
        return copy

    def local(self, src, dst):
        i = self.used
        self.used += 1
        copy = pltpu.make_async_copy(src, dst, self.sends.at[i])
        copy.start()
        return copy

    def greet(self, devices):
        barrier = pltpu.get_barrier_semaphore()
        for device in devices:
            pl.semaphore_signal(
                barrier, inc=1, device_id=device, device_id_type=pl.DeviceIdType.MESH
            )
        pl.semaphore_wait(barrier, len(devices))

    def settle(self):
        for copy in self.open:
            copy.wait_send()
        self.open = []


def arrived(copies):
    for copy in copies:
        copy.wait_recv()


def interleave(parts, order):
    for letter in order:
        next(parts[ord(letter) - ord("a")], None)
    finish(*parts)


def cut(count):
    upper = (count // 2 + 15) // 16 * 16
    return upper, count - upper


def owner_cols(y, c, b):
    return pl.ds(pl.multiple_of(b * 1024 + (2 * y + c) * LANES, LANES), LANES)


def gather_yc(links, src, dst):
    rows = src.shape[0]
    top, low = cut(rows)
    h0, h1 = pl.ds(0, top), pl.ds(top, low)
    full = pl.ds(0, rows)

    def mine(part, b):
        return src.at[part, pl.ds(b * LANES, LANES)]

    def slot(y, c, part, b):
        return dst.at[part, owner_cols(y, c, b)]

    def push(y, part, device, own=False):
        c = links.c
        return [
            links.send(mine(part, b) if own else slot(y, c, part, b), slot(y, c, part, b), device)
            for b in range(2)
        ]

    y, up, down, far = links.y, links.at_y(1), links.at_y(-1), links.at_y(2)
    fwd, bwd, sib = links.to_y(1), links.to_y(-1), links.sibling()
    a0 = push(y, h0, fwd, True)
    b1 = push(y, h1, bwd, True)
    a1 = push(y, h1, fwd, True)
    b0 = push(y, h0, bwd, True)
    s = push(y, full, sib, True)
    keep = [links.local(mine(full, b), slot(y, links.c, full, b)) for b in range(2)]
    yield
    arrived(a0)
    f0 = push(down, h0, fwd)
    arrived(b1)
    f1 = push(up, h1, bwd)
    yield
    arrived(a1)
    s += push(down, full, sib)
    arrived(b0)
    s += push(up, full, sib)
    yield
    arrived(f0)
    s += push(far, h0, sib)
    arrived(f1)
    s += push(far, h1, sib)
    yield
    arrived(s)
    for copy in keep:
        copy.wait()


def fill(pairs, dst, cols):
    value = None
    for left, right in pairs:
        term = jnp.dot(left[...], right[:, cols], preferred_element_type=F32)
        value = term if value is None else value + term
    dst[:, cols] = value.astype(BF16)


def scatter_yc(links, pairs, out, src, sib_buf, half_buf, full_buf):
    rows = src.shape[0]
    top, low = cut(rows)
    step = 64
    order = [links.at_y(2), links.at_y(1), links.at_y(-1), links.y]
    fwd, bwd, sib = links.to_y(1), links.to_y(-1), links.sibling()
    mine, other = links.c, 1 - links.c
    got = []

    def produce(k):
        for b in range(2):
            fill(pairs, src, pl.ds(pl.multiple_of(b * 1024 + order[k] * 256, 256), 256))
        got.append(
            [
                links.send(
                    src.at[:, owner_cols(order[k], other, b)], sib_buf.at[k, :, pl.ds(b * LANES, LANES)], sib
                )
                for b in range(2)
            ]
        )

    def total(k, place, b):
        lanes = slice(b * LANES, (b + 1) * LANES)
        return src[place, owner_cols(order[k], mine, b)].astype(F32) + sib_buf[k, place, lanes].astype(F32)

    def over(first, count, body):
        def run(i, _):
            body(pl.multiple_of(first + i * step, 16))
            return 0

        assert count % step == 0
        lax.fori_loop(0, count // step, run, 0)

    def put(k, first, count, more=None, more_first=0):
        def body(at):
            place = pl.ds(at, step)
            for b in range(2):
                lanes = slice(b * LANES, (b + 1) * LANES)
                value = total(k, place, b)
                if more is not None:
                    value = value + more[pl.ds(pl.multiple_of(at - more_first, 16), step), lanes].astype(F32)
                sib_buf[k, place, lanes] = value.astype(BF16)

        over(first, count, body)

    t, l = pl.ds(0, top), pl.ds(top, low)
    produce(0)
    yield
    produce(1)
    arrived(got[0])
    put(0, 0, top)
    h0 = links.send(sib_buf.at[0, t, :], half_buf.at[0, t, :], fwd)
    put(0, top, low)
    h1 = links.send(sib_buf.at[0, l, :], half_buf.at[1, pl.ds(0, low), :], bwd)
    yield
    produce(2)
    arrived(got[1])
    put(1, top, low)
    p1 = links.send(sib_buf.at[1, l, :], full_buf.at[0, l, :], fwd)
    yield
    produce(3)
    arrived(got[2])
    put(2, 0, top)
    m1 = links.send(sib_buf.at[2, t, :], full_buf.at[1, t, :], bwd)
    yield
    h0.wait_recv()
    put(1, 0, top, half_buf.at[0], 0)
    p0 = links.send(sib_buf.at[1, t, :], full_buf.at[0, t, :], fwd)
    h1.wait_recv()
    put(2, top, low, half_buf.at[1], top)
    m0 = links.send(sib_buf.at[2, l, :], full_buf.at[1, l, :], bwd)
    yield
    yield
    arrived(got[3])
    arrived([p1, m1, p0, m0])

    def last(at):
        place = pl.ds(at, step)
        for b in range(2):
            lanes = slice(b * LANES, (b + 1) * LANES)
            out[place, lanes] = (
                total(3, place, b)
                + full_buf[0, place, lanes].astype(F32)
                + full_buf[1, place, lanes].astype(F32)
            )

    over(0, rows, last)


def scatter_yc_scratch(rows):
    top, _ = cut(rows)
    return [
        pltpu.VMEM((rows, 2048), BF16),
        pltpu.VMEM((4, rows, 256), BF16),
        pltpu.VMEM((2, top, 256), BF16),
        pltpu.VMEM((2, rows, 256), BF16),
    ]


def yc_peers(links):
    return [
        {"y": links.at_y(dy), "c": lax.rem(links.c + dc, 2)}
        for dy in range(4)
        for dc in range(2)
        if (dy, dc) != (0, 0)
    ]


def sum_dots(links, src, out, buf):
    me = 2 * links.y + links.c
    copies = [links.send(src, buf.at[me], device) for device in yc_peers(links)]
    yield
    yield
    arrived(copies)
    total = src[...]
    for dy in range(4):
        for dc in range(2):
            if (dy, dc) != (0, 0):
                total = total + buf[2 * links.at_y(dy) + lax.rem(links.c + dc, 2)]
    out[...] = total


def xz_slot(dst, x, z, part):
    zh, zl = lax.div(z, 2), lax.rem(z, 2)
    rows = pl.ds(pl.multiple_of(zh * (dst.shape[0] // 2) + part.start, 16), part.size)
    return dst.at[rows, pl.ds(pl.multiple_of((2 * x + zl) * 256, 256), 256)]


AROUND = (2, 1, 3)


def xz_peers(links):
    return [links.to_x(by) for by in AROUND] + [links.to_z(by) for by in AROUND]


def gather_xz(links, src, dst, first=0):
    rows = src.shape[0]
    a, b = (first, rows - first) if first else cut(rows)
    keep = links.local(src, xz_slot(dst, links.x, links.z, pl.ds(0, rows)))
    upper, lower = pl.ds(0, a), pl.ds(a, b)

    def own(part, device):
        return links.send(src.at[part, :], xz_slot(dst, links.x, links.z, part), device)

    along_x = [(own(upper, links.to_x(by)), own(lower, links.to_x(by))) for by in AROUND]
    yield
    along_z = [(own(lower, links.to_z(by)), own(upper, links.to_z(by))) for by in AROUND]
    yield
    far = [pair[1] for pair in along_x + along_z]
    for by, (copy, _) in zip(AROUND, along_x):
        copy.wait_recv()
        piece = xz_slot(dst, links.at_x(-by), links.z, upper)
        far.extend(links.send(piece, piece, links.to_z(on)) for on in AROUND)
    for by, (copy, _) in zip(AROUND, along_z):
        copy.wait_recv()
        piece = xz_slot(dst, links.x, links.at_z(-by), lower)
        far.extend(links.send(piece, piece, links.to_x(on)) for on in AROUND)
    yield
    arrived(far)
    keep.wait()


def add_rows(count, terms, into):
    step = 16
    for size in (32, 48, 64, 80, 88, 96):
        if size % 16 == 0 and count % size == 0:
            step = size
    width = into[0].shape[-1]

    def pick(ref, first, lane, i):
        place = pl.ds(pl.multiple_of(first + i * step, 16), step)
        lanes = pl.ds(0 if lane is None else pl.multiple_of(lane, LANES), width)
        return place, lanes

    def body(i, _):
        value = None
        for ref, first, lane in terms:
            place, lanes = pick(ref, first, lane, i)
            term = ref[place, lanes].astype(F32)
            value = term if value is None else value + term
        ref, first, lane = into
        place, lanes = pick(ref, first, lane, i)
        ref[place, lanes] = value.astype(ref.dtype)
        return 0

    lax.fori_loop(0, count // step, body, 0)


def scatter_xz(links, src, out, near, near2):
    rows = out.shape[0]
    a, b = cut(rows)

    def by_xz(x, z):
        z = jnp.int32(z) if isinstance(z, int) else z
        return lax.div(z, 2), (2 * x + lax.rem(z, 2)) * 256

    halves = [
        (0, a, links.at_x, links.to_x, links.at_z, links.to_z, by_xz),
        (a, b, links.at_z, links.to_z, links.at_x, links.to_x, lambda z, x: by_xz(x, z)),
    ]
    came = []
    for which, (first, count, at1, to1, at2, to2, place_of) in enumerate(halves):
        copies = []
        for by in AROUND:
            for q in range(4):
                zh, lane = place_of(at1(by), q)
                part = src.at[
                    pl.ds(pl.multiple_of(zh * rows + first, 16), count), pl.ds(pl.multiple_of(lane, 256), 256)
                ]
                copies.append(links.send(part, near.at[which, by - 1, q, pl.ds(0, count), :], to1(by)))
        came.append(copies)
    yield
    last = []
    for which, (first, count, at1, to1, at2, to2, place_of) in enumerate(halves):
        arrived(came[which])
        for q in range(4):
            zh, lane = place_of(at1(0), q)
            add_rows(
                count,
                [(src, zh * rows + first, lane), *[(near.at[which, k, q], 0, None) for k in range(3)]],
                (near.at[which, 0, q], 0, None),
            )
        last.append(
            [
                links.send(
                    near.at[which, 0, at2(by), pl.ds(0, count), :], near2.at[which, by - 1, pl.ds(0, count), :], to2(by)
                )
                for by in AROUND
            ]
        )
    yield
    for which, (first, count, at1, to1, at2, to2, place_of) in enumerate(halves):
        arrived(last[which])
        add_rows(
            count,
            [(near.at[which, 0, at2(0)], 0, None), *[(near2.at[which, k], 0, None) for k in range(3)]],
            (out, first, None),
        )


def scatter_xz_scratch(rows):
    a, _ = cut(rows)
    return [pltpu.VMEM((2, 3, 4, a, 256), BF16), pltpu.VMEM((2, 3, a, 256), BF16)]


def scatter_grad(links, left, right, out, src, near, near2):
    rows = 2 * out.shape[0]
    for i in range(4):
        cols = slice(512 * i, 512 * (i + 1))
        value = lax.dot_general(
            left[...], right[:, cols], (((0,), (0,)), ((), ())), preferred_element_type=F32
        ).astype(BF16)
        src[0:rows, cols] = value
        yield
    yield from scatter_xz(links, src, out, near, near2)


def row_peers(links):
    peers = []
    for dx in range(4):
        for dz in range(4):
            if (dx, dz) != (0, 0):
                peers.append({"x": links.at_x(dx), **links.to_z(dz)})
    return peers


def block_of(links, dx, dz):
    z = links.at_z(dz)
    return links.at_x(dx) * 4 + lax.rem(z, 2) * 2 + lax.div(z, 2)


def exchange_rows(links, src, out):
    me = block_of(links, 0, 0)
    keep = links.local(src, out.at[me])
    copies = [links.send(src, out.at[me], device) for device in row_peers(links)]
    yield
    arrived(copies)
    keep.wait()


def sum_rows(links, src, out, buf):
    me = block_of(links, 0, 0)
    copies = []
    for dx in range(4):
        for dz in range(4):
            if (dx, dz) != (0, 0):
                device = {"x": links.at_x(dx), **links.to_z(dz)}
                lanes = pl.ds(pl.multiple_of(device["zh"] * LANES, LANES), LANES)
                copies.append(links.send(src.at[:, lanes], buf.at[me], device))
    yield
    arrived(copies)
    total = src[:, pl.ds(pl.multiple_of(links.zh * LANES, LANES), LANES)]
    for dx in range(4):
        for dz in range(4):
            if (dx, dz) != (0, 0):
                total = total + buf[block_of(links, dx, dz)]
    out[...] = total


def swap_pairs(links, ins, outs):
    lanes = pl.ds(pl.multiple_of(links.zh * LANES, LANES), LANES)
    keep, got = [], []
    for src, dst in zip(ins, outs):
        place = dst.at[pl.ds(0, src.shape[1]), lanes]
        got.append(links.send(src.at[1 - links.zh], place, links.to_z(2)))
    for src, dst in zip(ins, outs):
        place = dst.at[pl.ds(0, src.shape[1]), lanes]
        keep.append(links.local(src.at[links.zh], place))
    return got, keep


def unswap_pair(links, src, dst):
    mine = pl.ds(pl.multiple_of(links.zh * LANES, LANES), LANES)
    theirs = pl.ds(pl.multiple_of((1 - links.zh) * LANES, LANES), LANES)
    got = links.send(src.at[:, theirs], dst.at[links.zh], links.to_z(2))
    keep = links.local(src.at[:, mine], dst.at[links.zh])
    yield
    got.wait_recv()
    keep.wait()


def swap_only(links, src, dst):
    got, keep = swap_pairs(links, (src,), (dst,))
    for _ in range(4):
        yield
    arrived(got)
    for copy in keep:
        copy.wait()


def block_device(block):
    block = lax.rem(block + 16, 16)
    return {"x": lax.div(block, 4), "zl": lax.rem(lax.div(block, 2), 2), "zh": lax.rem(block, 2)}


def conv_backward(
    links, gg, u, q, z, k, v, p, halo, taps, m1, m2, ends, enter, free, dec, dec_seg, res, skip, rates, starts,
    gp, res_out, rate_out, skip_out, conv_out, edge, edge_in, back_ends, last, lasts, back_enter, kept, gq, gz,
):
    me = block_of(links, 0, 0)
    for b in range(2):
        back_first(b, gg, q, m1, free, dec, dec_seg, back_ends, last)
        if b == 0:
            yield
    going = exchange_rows(links, last, lasts)
    next(going)
    yield
    finish(going)
    total = jnp.zeros(last.shape, F32)
    for j in range(lasts.shape[0]):
        apart = (jnp.maximum(j - me - 1, 0) * p.shape[0]).astype(F32)
        after = (me < j).astype(F32)
        still = open_between(starts, (me + 1) * p.shape[0], j * p.shape[0])
        total = total + lasts[j] * (after * still * jnp.exp(-rates[...] * apart))
    back_enter[...] = total
    for b in range(2):
        for part in range(2):
            if (b, part) != (0, 0):
                keep_states(b, part, z, m1, ends, enter, free, dec, dec_seg, kept)
                yield
            back_poles(
                b, part, gg, u, q, z, m1, back_ends, back_enter, free, dec, dec_seg, res, skip,
                res_out, rate_out, skip_out, kept, gq, gz,
            )
            yield
        back_taps(b, v, k, p, halo, taps, m1, m2, gp, edge, conv_out, gq, gz)
        yield
    got = links.send(edge, edge_in, block_device(me - 1))
    yield
    got.wait_recv()
    for b in range(2):
        mend_edges(b, taps, edge_in, gp)


def shape(*dims, dtype=F32):
    return jax.ShapeDtypeStruct(dims, dtype)


def finish(*parts):
    for part in parts:
        for _ in part:
            pass


NT = (((1,), (1,)), ((), ()))


def feed_forward(
    links, gated, wout, g2, inv_g2, cot, wgate, tok, up_t, down,
    hidden, xs, acts, gg, gu, hg_out, wdown_out, gh, dots, r2, sum_down,
    shard, wup, wdown, mixer, hg, own_dots, dots_buf, *held,
):
    rows = gated.shape[0]
    width = hg.shape[1]
    one, two, held = held[:4], held[4:8], held[8:]
    swap = swap_only(links, tok, xs)
    beside = [gather_xz(links, up_t, wup), gather_xz(links, down, wdown)]
    next(swap)
    for part in beside:
        next(part)
    mixed_in = scatter_yc(links, [(gated, wout)], mixer, *one)
    next(mixed_in)
    next(mixed_in)
    for part in beside:
        next(part)
    finish(mixed_in)
    finish(swap)
    staged = links.local(xs, shard)
    staged.wait()

    def residual(i, _):
        place = pl.ds(pl.multiple_of(i * 64, 64), 64)
        value = shard[place, :].astype(F32) + mixer[place, :]
        hidden[place, :] = value
        shard[place, :] = (value * g2[0:1, :]).astype(BF16)
        return 0

    lax.fori_loop(0, rows // 64, residual, 0)
    columns = gather_yc(links, shard, hg)
    next(columns)
    for part in beside:
        next(part)
    finish(columns)
    finish(*beside)
    links.settle()
    kept = [links.local(hg, hg_out), links.local(wdown, wdown_out)]
    step = 256

    def block(i, _):
        place = pl.ds(pl.multiple_of(i * step, step), step)
        r = rows_scale(hg, inv_g2, place, width)
        r2[place, :] = jnp.broadcast_to(r, (step, LANES))
        h = hg[place, :]
        gate = r * lax.dot_general(h, wgate[...], NT, preferred_element_type=F32)
        upper = r * lax.dot_general(h, wup[...], NT, preferred_element_type=F32)
        g_act = lax.dot_general(cot[place, :], wdown[...], NT, preferred_element_type=F32)
        sig = jax.nn.sigmoid(gate)
        acts[place, :] = (gate * sig * upper).astype(BF16)
        g_gate = g_act * upper * (sig * (1.0 + gate * (1.0 - sig)))
        g_upper = g_act * gate * sig
        gg[place, :] = (r * g_gate).astype(BF16)
        gu[place, :] = (r * g_upper).astype(BF16)
        both = (g_gate * gate + g_upper * upper).astype(BF16)
        own_dots[:, place] = lax.dot_general(
            jnp.ones((8, both.shape[1]), BF16), both, NT, preferred_element_type=F32
        )
        return 0

    lax.fori_loop(0, rows // step, block, 0)
    parts = [
        scatter_yc(links, [(gg, wgate), (gu, wup)], gh, *two),
        scatter_grad(links, acts, cot, sum_down, *held),
        sum_dots(links, own_dots, dots, dots_buf),
    ]
    interleave(parts, "caabbbbbaaabaab")
    for copy in kept:
        copy.wait()


def rows_scale(x, gain, place, width):
    square = jnp.zeros((place.size, LANES), F32)
    for k in range(width // LANES):
        lanes = slice(LANES * k, LANES * (k + 1))
        plain = x[place, lanes].astype(F32) * gain[0:1, lanes]
        square = square + plain * plain
    return lax.rsqrt(jnp.sum(square, axis=1, keepdims=True) / width + EPS)


def open_between(starts, low, high):
    at = starts[...]
    hit = jnp.where((at >= low) & (at < high), 1.0, 0.0)
    return 1.0 - jnp.max(hit, axis=0, keepdims=True)


def write_masks(block, starts, m1, m2):
    rows = m1.shape[0]
    seg = rows // SEGS
    firsts = [jnp.broadcast_to(starts[j : j + 1, 0:LANES], (SEGS, LANES)) for j in range(DOCS)]
    base = block * rows + seg_rows() * seg

    def carries_on(place):
        hit = place == firsts[0]
        for first in firsts[1:]:
            hit = hit | (place == first)
        return jnp.where(hit, 0.0, 1.0)

    def step(i, earlier):
        one = carries_on(base + i)
        m1[tile(i), :] = one
        m2[tile(i), :] = one * earlier
        return one

    lax.fori_loop(0, seg, step, carries_on(base - 1))


def mixer_input(
    links, scaled, small, cot, win_t, wout, wgate_t, starts,
    xg_out, win_out, wout_out, wgate_out, cs, cot_out, p_out, q_out, z_out, k_out, v_out,
    u, gated, halo, ends, free, enter, params, inv_g2, r1, m1, m2,
    xs, sm, xg, gains, inv, win, p, q, z, k, v, dec, dec_seg, taps, res, skip, last, lasts,
):
    rows, width = xg.shape
    poles = dec.shape[0]
    me = block_of(links, 0, 0)
    got, keep = swap_pairs(links, (small, scaled), (sm, xs))
    win_in = gather_xz(links, win_t, win, win_t.shape[0] // 4)
    next(win_in)
    cot_swap = swap_only(links, cot, cs)
    wout_in = gather_xz(links, wout, wout_out)
    wgate_in = gather_xz(links, wgate_t, wgate_out)
    write_masks(me, starts, m1, m2)
    arrived(got[:1])
    keep[0].wait()
    gain_rows = gather_yc(links, sm.at[pl.ds(0, 32), :], gains)
    next(gain_rows)
    values = sm[...].astype(F32)
    rate = jnp.exp(values[32:48])
    dec[...] = jnp.exp(-rate)
    dec_seg[...] = jnp.exp(-rate * (rows // SEGS))
    taps[...] = values[16:32]
    res[...] = values[48:64]
    skip[...] = jnp.broadcast_to(values[2:3], (SEGS, 2 * LANES))
    params[0:16, :] = values[0:16]
    params[16:32, :] = values[16:32]
    params[32:48, :] = rate
    params[48:64, :] = values[48:64]
    arrived(got[1:])
    keep[1].wait()
    columns = gather_yc(links, xs, xg)
    next(columns)
    next(win_in)
    next(cot_swap)
    next(gain_rows)
    next(gain_rows)
    next(columns)
    next(win_in)
    next(columns)
    next(gain_rows)
    finish(columns)
    finish(gain_rows, win_in)
    inv[...] = 1.0 / gains[0:16, :].astype(F32)
    inv_g2[...] = inv[1:2, :]
    stores = [links.local(xg, xg_out), links.local(win, win_out)]
    step = 256

    def project(i, _):
        place = pl.ds(pl.multiple_of(i * step, step), step)
        r = rows_scale(xg, inv, place, width)
        r1[place, :] = jnp.broadcast_to(r, (step, LANES))
        p[place, :] = r * lax.dot_general(xg[place, :], win[...], NT, preferred_element_type=F32)
        return 0

    lax.fori_loop(0, rows // step, project, 0)
    stores.append(links.local(p, p_out))
    tail = links.send(p.at[pl.ds(rows - 16, 16), :], halo, block_device(me + 1))
    for part in (wgate_in, wout_in):
        next(part)
        next(part)
    finish(cot_swap)
    cot_in = gather_yc(links, cs, cot_out)
    next(cot_in)
    tail.wait_recv()
    for b in range(2):
        conv_first(b, p, halo, taps, m1, m2, dec, dec_seg, q, z, k, v, ends, free, last)
    going = exchange_rows(links, last, lasts)
    next(going)
    next(cot_in)
    next(wgate_in)
    next(wout_in)
    stores += [links.local(q, q_out), links.local(z, z_out), links.local(k, k_out), links.local(v, v_out)]
    finish(going)
    rates = params[32:48, :]
    total = jnp.zeros((poles, 2 * LANES), F32)
    for j in range(lasts.shape[0]):
        apart = (jnp.maximum(me - 1 - j, 0) * rows).astype(F32)
        before = (me > j).astype(F32)
        total = total + lasts[j] * (before * open_between(starts, (j + 1) * rows, me * rows) * jnp.exp(-rates * apart))
    enter[...] = total
    conv_second(0, q, z, m1, ends, free, enter, dec, dec_seg, res, skip, u, gated)
    next(cot_in)
    conv_second(1, q, z, m1, ends, free, enter, dec, dec_seg, res, skip, u, gated)
    finish(cot_in)
    finish(wgate_in, wout_in)
    for copy in stores:
        copy.wait()


def mixer_back(
    links, g_o, wout, gated, acts, wdown, gg_low, gu_low, hg, hidden, u, q, z, k, v, p, halo, taps, m1, m2,
    ends, enter, free, dec, dec_seg, res, skip, rates, starts,
    gp, res_out, rate_out, skip_out, conv_out, mixed, sum_gate, sum_up, sum_out,
    g_mix, gg, mlp, mixed_half, edge, edge_in, back_ends, last, lasts, back_enter, kept, gq, gz, *held,
):
    rows = gg.shape[0]
    columns = gather_yc(links, g_o, g_mix)
    gate = scatter_grad(links, gg_low, hg, sum_gate, *held[4:7])
    up = scatter_grad(links, gu_low, hg, sum_up, *held[7:10])
    out = scatter_grad(links, gated, g_mix, sum_out, *held[10:13])
    down = scatter_yc(links, [(acts, wdown)], mlp, *held[:4])
    steps = lambda part, count: [next(part, None) for _ in range(count)]
    steps(columns, 1)
    steps(gate, 5)
    steps(columns, 1)
    steps(up, 5)
    steps(columns, 2)
    steps(down, 2)
    keep_states(0, 0, z, m1, ends, enter, free, dec, dec_seg, kept)
    finish(columns)
    gg[...] = lax.dot_general(g_mix[...], wout[...], NT, preferred_element_type=F32)
    back = conv_backward(
        links, gg, u, q, z, k, v, p, halo, taps, m1, m2, ends, enter, free, dec, dec_seg, res, skip, rates, starts,
        gp, res_out, rate_out, skip_out, conv_out, edge, edge_in, back_ends, last, lasts, back_enter, kept, gq, gz,
    )
    steps(back, 2)
    steps(down, 2)
    steps(gate, 1)
    steps(up, 1)
    steps(back, 1)
    steps(down, 1)
    steps(out, 5)
    steps(back, 1)
    finish(gate)
    steps(back, 1)
    steps(down, 1)
    steps(out, 1)
    steps(back, 1)
    finish(up)
    steps(back, 1)
    finish(down)

    def mix(i, _):
        place = pl.ds(pl.multiple_of(i * 64, 64), 64)
        mixed_half[place, :] = (hidden[place, :] + mlp[place, :]).astype(BF16)
        return 0

    lax.fori_loop(0, rows // 64, mix, 0)
    swapped = unswap_pair(links, mixed_half, mixed)
    steps(swapped, 1)
    finish(back, out, swapped)


def input_back(
    links, gp, p, r1, xg, win, g_hidden, xs, g1, conv, rate_raw, res_raw, skip_raw, rate, res, gain2,
    sum_in, grad, tiny_out,
    gp_low, own_dots, dots, dots_buf, gx, grad_half, tiny, tiny_buf, *held,
):
    rows = gp.shape[0]
    width = xg.shape[1]
    step = 256

    def scale(i, _):
        place = pl.ds(pl.multiple_of(i * step, step), step)
        value = gp[place, :]
        both = (value * p[place, :]).astype(BF16)
        own_dots[:, place] = lax.dot_general(
            jnp.ones((8, both.shape[1]), BF16), both, NT, preferred_element_type=F32
        )
        gp_low[place, :] = (r1[place, 0:1] * value).astype(BF16)
        return 0

    lax.fori_loop(0, rows // step, scale, 0)
    parts = [
        scatter_yc(links, [(gp_low, win)], gx, *held[:4]),
        sum_dots(links, own_dots, dots, dots_buf),
        scatter_grad(links, gp_low, xg, sum_in, *held[4:]),
    ]
    for letter in "baacccccaaaacba":
        next(parts[ord(letter) - ord("a")], None)
    finish(parts[0], parts[1])
    line = lax.broadcasted_iota(jnp.int32, dots.shape, 0)
    value = dots[...]
    high = value.astype(BF16).astype(F32)
    pair = jnp.where(line == 0, high, jnp.where(line == 1, value - high, 0.0)).astype(BF16)
    column = lax.dot_general(
        pair, jnp.ones((8, LANES), BF16), (((0,), (0,)), ((), ())), preferred_element_type=F32
    )
    tiny[...] = jnp.zeros_like(tiny)
    pull = r1[...] * r1[...] * column / width
    for b in range(2):
        lanes = lanes_of(b)
        x = xs[:, lanes].astype(F32)
        got = gx[:, lanes]
        grad_half[:, lanes] = (g_hidden[:, lanes] + g1[0:1, lanes] * got - x * pull).astype(BF16)
        tiny[0:1, lanes] = jnp.sum(got * x, axis=0, keepdims=True)
    tiny[1:2, :] = gain2[...]
    tiny[2:3, :] = jnp.sum(skip_raw[...], axis=0, keepdims=True)
    tiny[8:24, :] = conv[...]
    tiny[24:40, :] = -rate[...] * res[...] * rate_raw[...]
    tiny[40:56, :] = res_raw[...]
    swapped = unswap_pair(links, grad_half, grad)
    summed = sum_rows(links, tiny, tiny_out, tiny_buf)
    next(swapped)
    next(summed)
    finish(parts[2], summed, swapped)


def fused(number, maker, peers, inputs, outs, scratch, copies):
    vmem = pl.BlockSpec(memory_space=pltpu.VMEM)
    hbm = pl.BlockSpec(memory_space=pl.ANY)
    staged = [i for i, (_, kind) in enumerate(inputs) if kind == "s"]
    n_in, n_out = len(inputs), len(outs)

    def kernel(*refs):
        ins, results = list(refs[:n_in]), refs[n_in : n_in + n_out]
        held = refs[n_in + n_out : -2]
        links = Links(refs[-2], refs[-1])
        moves = []
        for i, buf in zip(staged, held):
            moves.append(links.local(ins[i], buf))
            ins[i] = buf
        met = []
        if "Y" in peers:
            met += yc_peers(links)
        elif "y" in peers:
            met += [links.to_y(1), links.to_y(-1), links.sibling()]
        if "r" in peers:
            met += row_peers(links)
        elif "x" in peers:
            met += xz_peers(links)
        links.greet(met)
        for move in moves:
            move.wait()
        maker(links, *ins, *results, *held[len(staged) :])
        links.settle()

    return pl.pallas_call(
        kernel,
        in_specs=[vmem if kind == "v" else hbm for _, kind in inputs],
        out_specs=[vmem if kind == "v" else hbm for _, kind in outs],
        out_shape=[kept for kept, _ in outs],
        scratch_shapes=[
            *[pltpu.VMEM(inputs[i][0].shape, inputs[i][0].dtype) for i in staged],
            *scratch,
            pltpu.SemaphoreType.DMA((copies,)),
            pltpu.SemaphoreType.DMA((copies,)),
        ],
        compiler_params=pltpu.CompilerParams(
            collective_id=number, has_side_effects=True, vmem_limit_bytes=VMEM_LIMIT
        ),
    )(*[array for array, _ in inputs])


def grad_scratch(rows):
    return [pltpu.VMEM((2 * rows, 2048), BF16), *scatter_xz_scratch(rows)]


def shards(
    tokens, gain_first, gain_second, w_in, conv_w, log_rate, residue, skip,
    w_out, w_gate, w_up, w_down, cotangent, lengths,
):
    rows = tokens.shape[0] // 2
    width = 16 * LANES
    seg = rows // SEGS

    def stepped(value):
        return value.reshape(2, SEGS, seg, LANES).transpose(0, 2, 1, 3).reshape(2, rows, LANES)

    def unstepped(value):
        return value.reshape(2, seg, SEGS, LANES).transpose(0, 2, 1, 3).reshape(2 * rows, LANES)

    before = jnp.arange(DOCS)[:, None] < jnp.arange(DOCS)[None, :]
    starts = jnp.sum(jnp.where(before, lengths[:, None], 0), axis=0)
    starts = jnp.broadcast_to(starts[:, None], (DOCS, 2 * LANES))

    tok = stepped(tokens)
    scaled = stepped((tokens.astype(F32) * gain_first.astype(F32)).astype(BF16))
    line = lax.broadcasted_iota(jnp.int32, (16, LANES), 0)
    singles = jnp.where(line == 0, gain_first, jnp.where(line == 1, gain_second, jnp.where(line == 2, skip, 0)))
    taps_own = jnp.pad(conv_w.reshape(9, LANES), ((0, 7), (0, 0)))
    small = jnp.concatenate([singles.astype(BF16), taps_own, log_rate, residue])
    hidden_units = w_gate.shape[1]
    half = (rows, 2 * LANES)
    weight = (2 * hidden_units, width)
    act = shape(*half)
    low = shape(*half, dtype=BF16)
    proj_shape = shape(rows, 6 * LANES)
    (
        xg, win, wout, wgate, cs, cot, proj, q, z, k, v, u, gated, halo, seg_ends, free, enter, params, inv_g2, r1,
        mask1, mask2,
    ) = fused(
        1,
        mixer_input,
        "yr",
        [
            (scaled, "h"), (jnp.broadcast_to(small[None], (2, 64, LANES)), "h"), (stepped(cotangent), "h"),
            (w_in.transpose(1, 2, 0).reshape(3 * LANES, 256), "h"), (w_out, "h"), (w_gate.T, "h"),
            (starts, "v"),
        ],
        [
            (shape(rows, width, dtype=BF16), "h"), (shape(6 * LANES, width, dtype=BF16), "h"),
            (shape(2 * LANES, width, dtype=BF16), "h"), (shape(*weight, dtype=BF16), "h"), (low, "h"),
            (shape(rows, width, dtype=BF16), "h"), (proj_shape, "h"), (act, "h"), (act, "h"), (act, "h"), (act, "h"),
            (act, "v"), (low, "v"), (shape(16, 768), "v"), (shape(128, 256), "v"), (shape(8, 256), "v"),
            (shape(16, 256), "v"), (shape(64, 256), "v"), (shape(1, width), "v"), (shape(rows, LANES), "v"),
            (shape(rows, LANES), "v"), (shape(rows, LANES), "v"),
        ],
        [
            pltpu.VMEM(half, BF16), pltpu.VMEM((64, 256), BF16), pltpu.VMEM((rows, width), BF16),
            pltpu.VMEM((32, width), BF16), pltpu.VMEM((16, width), F32), pltpu.VMEM((6 * LANES, width), BF16),
            pltpu.VMEM((rows, 6 * LANES), F32), *([pltpu.VMEM(half, F32)] * 4),
            pltpu.VMEM((16, 256), F32), pltpu.VMEM((16, 256), F32), pltpu.VMEM((16, 256), F32),
            pltpu.VMEM((16, 256), F32), pltpu.VMEM((8, 256), F32), pltpu.VMEM((16, 256), F32),
            pltpu.VMEM((16, 16, 256), F32),
        ],
        220,
    )
    g1, g2 = params[0:1], params[1:2]
    skip8 = jnp.broadcast_to(params[2:3], (8, 2 * LANES))
    taps, rate, res = params[16:32], params[32:48], params[48:64]
    dec = jnp.exp(-rate)
    dec_seg = jnp.exp(-rate * seg)

    units = shape(rows, 2 * hidden_units, dtype=BF16)
    hidden, xs, acts, gg_low, gu_low, hg, wdown, gh, dot2, r2, sums_down = fused(
        3,
        feed_forward,
        "Yx",
        [
            (gated, "s"), (wout, "s"), (g2, "v"), (inv_g2, "v"), (cot, "s"), (wgate, "s"),
            (tok, "h"), (w_up.T, "h"), (w_down, "h"),
        ],
        [
            (shape(*half), "v"), (shape(*half, dtype=BF16), "h"), (units, "v"), (units, "v"), (units, "v"),
            (shape(rows, width, dtype=BF16), "h"), (shape(*weight, dtype=BF16), "h"), (shape(*half), "v"),
            (shape(8, rows), "v"), (shape(rows, LANES), "v"), (shape(hidden_units, 2 * LANES), "v"),
        ],
        [
            pltpu.VMEM(half, BF16), pltpu.VMEM(weight, BF16), pltpu.VMEM(weight, BF16), pltpu.VMEM(half, F32),
            pltpu.VMEM((rows, width), BF16), pltpu.VMEM((8, rows), F32), pltpu.VMEM((8, 8, rows), F32),
            *scatter_yc_scratch(rows), *scatter_yc_scratch(rows), *grad_scratch(hidden_units),
        ],
        200,
    )
    r2 = r2[:, :1]
    dot2 = dot2[0][:, None]
    g_hidden = cs.astype(F32) + g2 * gh - hidden * (r2 * r2 * dot2 / width)
    grad_gain2 = jnp.sum(gh * hidden, axis=0)
    sixteen = shape(16, 2 * LANES)
    g_proj, res_raw, rate_raw, skip_raw, conv_raw, mixed, sums_gate, sums_up, sums_out = fused(
        4,
        mixer_back,
        "yr",
        [
            (g_hidden.astype(BF16), "h"), (wout, "s"), (gated, "s"), (acts, "s"), (wdown, "s"), (gg_low, "s"),
            (gu_low, "s"), (hg, "s"), (hidden, "s"), (u, "s"), (q, "s"), (z, "s"), (k, "s"), (v, "s"), (proj, "s"),
            (halo, "v"), (taps, "v"), (mask1, "s"), (mask2, "s"), (seg_ends, "v"), (enter, "v"), (free, "v"),
            (dec, "v"), (dec_seg, "v"), (res, "v"), (skip8, "v"), (rate, "v"), (starts, "v"),
        ],
        [
            (proj_shape, "v"), (sixteen, "v"), (sixteen, "v"), (shape(8, 2 * LANES), "v"), (sixteen, "v"),
            (shape(2, rows, LANES, dtype=BF16), "h"), *[(shape(hidden_units, 2 * LANES), "v")] * 2,
            (shape(LANES, 2 * LANES), "v"),
        ],
        [
            pltpu.VMEM((rows, width), BF16), pltpu.VMEM(half, F32), pltpu.VMEM(half, F32), pltpu.VMEM(half, BF16),
            pltpu.VMEM((24, 6 * LANES), F32), pltpu.VMEM((24, 6 * LANES), F32), pltpu.VMEM((128, 256), F32),
            pltpu.VMEM((16, 256), F32), pltpu.VMEM((16, 16, 256), F32), pltpu.VMEM((16, 256), F32),
            pltpu.VMEM((seg, 8, SEGS, LANES), F32), pltpu.VMEM((rows, LANES), F32), pltpu.VMEM((rows, LANES), F32),
            *scatter_yc_scratch(rows), *(grad_scratch(hidden_units) * 2), *grad_scratch(LANES),
        ],
        220,
    )
    sums_in, grad_tok, tiny = fused(
        5,
        input_back,
        "Yr",
        [
            (g_proj, "s"), (proj, "s"), (r1, "s"), (xg, "s"), (win, "s"), (g_hidden, "s"), (xs, "s"), (g1, "v"),
            (conv_raw, "v"), (rate_raw, "v"), (res_raw, "v"), (skip_raw, "v"), (rate, "v"), (res, "v"),
            (grad_gain2[None], "v"),
        ],
        [
            (shape(3 * LANES, 2 * LANES), "v"), (shape(2, rows, LANES, dtype=BF16), "h"), (shape(56, LANES), "v"),
        ],
        [
            pltpu.VMEM((rows, 6 * LANES), BF16), pltpu.VMEM((8, rows), F32), pltpu.VMEM((8, rows), F32),
            pltpu.VMEM((8, 8, rows), F32), pltpu.VMEM(half, F32), pltpu.VMEM(half, BF16), pltpu.VMEM((56, 256), F32),
            pltpu.VMEM((16, 56, LANES), F32), *scatter_yc_scratch(rows), *grad_scratch(3 * LANES),
        ],
        120,
    )
    return (
        unstepped(mixed),
        unstepped(grad_tok).astype(F32),
        tiny[0],
        tiny[1],
        sums_in.reshape(3, LANES, 256).transpose(2, 0, 1),
        tiny[8:17].reshape(3, 3, LANES),
        tiny[24:40],
        tiny[40:56],
        tiny[2],
        sums_out,
        sums_gate.T,
        sums_up.T,
        sums_down,
    )


def solution(mesh):
    cube = Mesh(mesh.devices.reshape(4, 2, 2, 4, 2), ("x", "zl", "zh", "y", "c"))
    seq, tp = ("x", "zl"), ("zh", "y", "c")
    return jax.shard_map(
        shards,
        mesh=cube,
        in_specs=(
            P(seq, tp), P(tp), P(tp), P(seq, None, tp), P(None, None, tp), P(None, tp), P(None, tp), P(tp),
            P(tp, seq), P(seq, tp), P(seq, tp), P(tp, seq), P(seq, tp), P(),
        ),
        out_specs=(
            P(seq, tp), P(seq, tp), P(tp), P(tp), P(seq, None, tp), P(None, None, tp), P(None, tp), P(None, tp), P(tp),
            P(tp, seq), P(seq, tp), P(seq, tp), P(tp, seq),
        ),
        check_vma=False,
    )
```

```python
import functools

import jax
import jax.numpy as jnp
from jax import lax
from jax.experimental import pallas as pl
from jax.experimental.pallas import tpu as pltpu
from jax.sharding import Mesh
from jax.sharding import PartitionSpec as P

EPS = 1e-06
DOCS = 8
ROW_AXES = ("x", "zl", "zh")
COL_AXES = ("y", "c")
F32 = jnp.float32
BF16 = jnp.bfloat16
VMEM_LIMIT = 60 * 1024 * 1024
SEGS = 8
LANES = 128


def spread(row):
    return jnp.broadcast_to(row, (SEGS, LANES))


def seg_rows():
    return lax.broadcasted_iota(jnp.int32, (SEGS, LANES), 0)


def tile(i):
    return pl.ds(pl.multiple_of(i * SEGS, SEGS), SEGS)


def lanes_of(b, j=0):
    return slice(LANES * (b + j), LANES * (b + j + 1))


def add_all(terms):
    while len(terms) > 1:
        terms = [sum(terms[i + 1 : i + 2], terms[i]) for i in range(0, len(terms), 2)]
    return terms[0]


def scan_up(ends, factor):
    rows = seg_rows()
    for by in (1, 2, 4):
        held = rows >= by
        ends = ends + factor * jnp.where(held, pltpu.roll(ends, by, 0), 0.0)
        factor = factor * jnp.where(held, pltpu.roll(factor, by, 0), 1.0)
    return ends


def scan_down(ends, factor):
    rows = seg_rows()
    for by in (1, 2, 4):
        held = rows < SEGS - by
        ends = ends + factor * jnp.where(held, pltpu.roll(ends, SEGS - by, 0), 0.0)
        factor = factor * jnp.where(held, pltpu.roll(factor, SEGS - by, 0), 1.0)
    return ends


def entering_up(ends, factor, enter):
    first = seg_rows() == 0
    whole = scan_up(ends + jnp.where(first, factor * enter, 0.0), factor)
    return jnp.where(first, enter, pltpu.roll(whole, 1, 0))


def entering_down(ends, factor, enter):
    last = seg_rows() == SEGS - 1
    whole = scan_down(ends + jnp.where(last, factor * enter, 0.0), factor)
    return jnp.where(last, enter, pltpu.roll(whole, SEGS - 1, 0))


def rows_of(ref, count, lanes):
    return [spread(ref[n : n + 1, lanes]) for n in range(count)]


def tap_rows(taps, lanes):
    return [[spread(taps[3 * i + j : 3 * i + j + 1, lanes]) for j in range(3)] for i in range(3)]


def conv_first(b, p, halo, taps, m1, m2, dec, dec_seg, q_out, z_out, k_out, v_out, ends_out, open_out, last_out):
    seg = p.shape[0] // SEGS
    poles = dec.shape[0]
    own = lanes_of(b)
    cols = [lanes_of(3 * b, j) for j in range(3)]
    first = seg_rows() == 0
    d = rows_of(dec, poles, own)
    c = tap_rows(taps, own)

    def before(j, back):
        mine = pltpu.roll(p[SEGS * (seg - back) : SEGS * (seg - back + 1), cols[j]], 1, 0)
        theirs = pltpu.roll(halo[SEGS * (2 - back) : SEGS * (3 - back), cols[j]], 1, 0)
        return jnp.where(first, theirs, mine)

    def step(i, carry):
        state, prev1, prev2, free = carry
        place = tile(i)
        one, two = m1[place, :], m2[place, :]
        cur = [p[place, cols[j]] for j in range(3)]
        q, k, v = [
            c[0][j] * cur[j] + c[1][j] * (one * prev1[j]) + c[2][j] * (two * prev2[j])
            for j in range(3)
        ]
        z = k * v
        q_out[place, own] = q
        k_out[place, own] = k
        v_out[place, own] = v
        z_out[place, own] = z
        state = [d[n] * (one * state[n]) + z for n in range(poles)]
        return (state, cur, prev1, free * one)

    zero = jnp.zeros((SEGS, LANES), F32)
    start = (
        [zero] * poles,
        [before(j, 1) for j in range(3)],
        [before(j, 2) for j in range(3)],
        zero + 1.0,
    )
    state, _, _, free = lax.fori_loop(0, seg, step, start)
    open_out[:, own] = free
    for n in range(poles):
        ends_out[SEGS * n : SEGS * (n + 1), own] = state[n]
        whole = scan_up(state[n], spread(dec_seg[n : n + 1, own]) * free)
        last_out[n : n + 1, own] = whole[SEGS - 1 :, :]


def conv_second(b, q_in, z_in, m1, ends, free, enter, dec, dec_seg, res, skip, u_out, gated_out):
    rows = q_in.shape[0]
    seg = rows // SEGS
    poles = dec.shape[0]
    own = lanes_of(b)
    d = rows_of(dec, poles, own)
    r = rows_of(res, poles, own)
    sk = spread(skip[0:1, own])
    start = [
        entering_up(
            ends[SEGS * n : SEGS * (n + 1), own],
            spread(dec_seg[n : n + 1, own]) * free[:, own],
            spread(enter[n : n + 1, own]),
        )
        for n in range(poles)
    ]

    def step(i, state):
        place = tile(i)
        one, z = m1[place, :], z_in[place, own]
        state = [d[n] * (one * state[n]) + z for n in range(poles)]
        u_out[place, own] = add_all([r[n] * state[n] for n in range(poles)] + [sk * z])
        return state

    lax.fori_loop(0, seg, step, start)

    def rounded(i, _):
        place = pl.ds(pl.multiple_of(i * 64, 64), 64)
        gated_out[place, own] = (q_in[place, own] * u_out[place, own]).astype(BF16)
        return 0

    lax.fori_loop(0, rows // 64, rounded, 0)


def back_first(b, gg_in, q_in, m1, free, dec, dec_seg, ends_out, last_out):
    seg = q_in.shape[0] // SEGS
    poles = dec.shape[0]
    own = lanes_of(b)
    d = rows_of(dec, poles, own)

    def step(t, carry):
        place = tile(seg - 1 - t)
        gu = gg_in[place, own] * q_in[place, own]
        one = m1[place, :]
        return [d[n] * (one * (carry[n] + gu)) for n in range(poles)]

    zero = jnp.zeros((SEGS, LANES), F32)
    carry = lax.fori_loop(0, seg, step, [zero] * poles)
    for n in range(poles):
        ends_out[SEGS * n : SEGS * (n + 1), own] = carry[n]
        whole = scan_down(carry[n], spread(dec_seg[n : n + 1, own]) * free[:, own])
        last_out[n : n + 1, own] = whole[:1, :]


def keep_states(b, part, z_in, m1, ends, enter, free, dec, dec_seg, kept):
    seg = z_in.shape[0] // SEGS
    half = dec.shape[0] // 2
    own = lanes_of(b)
    these = range(half * part, half * (part + 1))
    d = [spread(dec[n : n + 1, own]) for n in these]
    start = [
        entering_up(
            ends[SEGS * n : SEGS * (n + 1), own],
            spread(dec_seg[n : n + 1, own]) * free[:, own],
            spread(enter[n : n + 1, own]),
        )
        for n in these
    ]

    def forward(i, state):
        place = tile(i)
        one, z = m1[place, :], z_in[place, own]
        state = [d[n] * (one * state[n]) + z for n in range(half)]
        for n in range(half):
            kept[i, n] = state[n]
        return state

    lax.fori_loop(0, seg, forward, start)


def back_poles(
    b, part, gg_in, u_in, q_in, z_in, m1, back_ends, back_enter, free, dec, dec_seg, res, skip,
    res_out, rate_out, skip_out, kept, gq, gz,
):
    seg = q_in.shape[0] // SEGS
    half = dec.shape[0] // 2
    own = lanes_of(b)
    zero = jnp.zeros((SEGS, LANES), F32)
    sk = spread(skip[0:1, own])
    these = range(half * part, half * (part + 1))
    d = [spread(dec[n : n + 1, own]) for n in these]
    r = [spread(res[n : n + 1, own]) for n in these]
    carry = [
        entering_down(
            back_ends[SEGS * n : SEGS * (n + 1), own],
            spread(dec_seg[n : n + 1, own]) * free[:, own],
            spread(back_enter[n : n + 1, own]),
        )
        for n in these
    ]

    def backward(t, held):
        carry, by_res, by_rate, by_skip = held
        i = seg - 1 - t
        place = tile(i)
        gg, one = gg_in[place, own], m1[place, :]
        gu = gg * q_in[place, own]
        s = [kept[i, n] for n in range(half)]
        lam = [carry[n] + gu for n in range(half)]
        terms = [r[n] * lam[n] for n in range(half)]
        if part == 0:
            terms.append(sk * gu)
            by_skip = by_skip + gu * z_in[place, own]
            gq[place, :] = gg * u_in[place, own]
        else:
            terms.append(gz[place, :])
        gz[place, :] = add_all(terms)
        by_res = [by_res[n] + gu * s[n] for n in range(half)]
        by_rate = [by_rate[n] + carry[n] * s[n] for n in range(half)]
        carry = [d[n] * (one * lam[n]) for n in range(half)]
        return (carry, by_res, by_rate, by_skip)

    _, by_res, by_rate, by_skip = lax.fori_loop(
        0, seg, backward, (carry, [zero] * half, [zero] * half, zero)
    )
    for k, n in enumerate(these):
        res_out[n : n + 1, own] = jnp.sum(by_res[k], axis=0, keepdims=True)
        rate_out[n : n + 1, own] = jnp.sum(by_rate[k], axis=0, keepdims=True)
    if part == 0:
        skip_out[:, own] = by_skip


def back_taps(b, v_in, k_in, p, halo, taps, m1, m2, gp_out, edge_out, conv_out, gq, gz):
    seg = p.shape[0] // SEGS
    own = lanes_of(b)
    cols = [lanes_of(3 * b, j) for j in range(3)]
    zero = jnp.zeros((SEGS, LANES), F32)
    c = tap_rows(taps, own)
    last = seg_rows() == SEGS - 1

    def short_grads(place):
        g = gz[place, :]
        return [gq[place, :], g * v_in[place, own], g * k_in[place, own]]

    def next_seg(value):
        return jnp.where(last, 0.0, pltpu.roll(value, SEGS - 1, 0))

    g0, g1 = short_grads(tile(0)), short_grads(tile(1))
    a1 = [m1[tile(0), :] * g for g in g0]
    b1 = [m2[tile(0), :] * g for g in g0]
    b2 = [m2[tile(1), :] * g for g in g1]
    for j in range(3):
        edge_out[0:8, cols[j]] = a1[j]
        edge_out[8:16, cols[j]] = b1[j]
        edge_out[16:24, cols[j]] = b2[j]

    def taps_back(t, held):
        late1, late2, later2, sums = held
        place = tile(seg - 1 - t)
        one, two = m1[place, :], m2[place, :]
        g = short_grads(place)
        new = []
        for j in range(3):
            value = p[place, cols[j]]
            gp_out[place, cols[j]] = c[0][j] * g[j] + c[1][j] * late1[j] + c[2][j] * later2[j]
            new += [
                sums[3 * j] + g[j] * value,
                sums[3 * j + 1] + late1[j] * value,
                sums[3 * j + 2] + later2[j] * value,
            ]
        return ([one * x for x in g], [two * x for x in g], late2, new)

    start = (
        [next_seg(x) for x in a1],
        [next_seg(x) for x in b1],
        [next_seg(x) for x in b2],
        [zero] * 9,
    )
    _, _, _, sums = lax.fori_loop(0, seg, taps_back, start)
    for j in range(3):
        old1, old2 = halo[15:16, cols[j]], halo[7:8, cols[j]]
        conv_out[j : j + 1, own] = jnp.sum(sums[3 * j], axis=0, keepdims=True)
        conv_out[3 + j : 4 + j, own] = jnp.sum(sums[3 * j + 1], axis=0, keepdims=True) + a1[j][:1] * old1
        conv_out[6 + j : 7 + j, own] = (
            jnp.sum(sums[3 * j + 2], axis=0, keepdims=True) + b1[j][:1] * old2 + b2[j][:1] * old1
        )


def mend_edges(b, taps, edge_in, gp_out):
    rows = gp_out.shape[0]
    own = lanes_of(b)
    cols = [lanes_of(3 * b, j) for j in range(3)]
    c = tap_rows(taps, own)
    last = seg_rows() == SEGS - 1
    for j in range(3):
        one = pltpu.roll(edge_in[0:8, cols[j]], SEGS - 1, 0)
        two = pltpu.roll(edge_in[8:16, cols[j]], SEGS - 1, 0)
        three = pltpu.roll(edge_in[16:24, cols[j]], SEGS - 1, 0)
        near, far = slice(rows - 8, rows), slice(rows - 16, rows - 8)
        gp_out[near, cols[j]] = gp_out[near, cols[j]] + jnp.where(last, c[1][j] * one + c[2][j] * three, 0.0)
        gp_out[far, cols[j]] = gp_out[far, cols[j]] + jnp.where(last, c[2][j] * two, 0.0)


class Links:
    def __init__(self, sends, recvs):
        self.sends, self.recvs, self.used, self.open = sends, recvs, 0, []
        self.x, self.y, self.c = lax.axis_index("x"), lax.axis_index("y"), lax.axis_index("c")
        self.zl, self.zh = lax.axis_index("zl"), lax.axis_index("zh")
        self.z = 2 * self.zh + self.zl

    def at_y(self, by):
        return lax.rem(self.y + by + 4, 4)

    def at_x(self, by):
        return lax.rem(self.x + by + 4, 4)

    def at_z(self, by):
        return lax.rem(self.z + by + 4, 4)

    def to_y(self, by):
        return {"y": self.at_y(by)}

    def to_x(self, by):
        return {"x": self.at_x(by)}

    def to_z(self, by):
        z = self.at_z(by)
        return {"zh": lax.div(z, 2), "zl": lax.rem(z, 2)}

    def sibling(self):
        return {"c": 1 - self.c}

    def send(self, src, dst, device):
        i = self.used
        self.used += 1
        copy = pltpu.make_async_remote_copy(
            src_ref=src,
            dst_ref=dst,
            send_sem=self.sends.at[i],
            recv_sem=self.recvs.at[i],
            device_id=device,
            device_id_type=pl.DeviceIdType.MESH,
        )
        copy.start()
        self.open.append(copy)
        return copy

    def local(self, src, dst):
        i = self.used
        self.used += 1
        copy = pltpu.make_async_copy(src, dst, self.sends.at[i])
        copy.start()
        return copy

    def greet(self, devices):
        barrier = pltpu.get_barrier_semaphore()
        for device in devices:
            pl.semaphore_signal(
                barrier, inc=1, device_id=device, device_id_type=pl.DeviceIdType.MESH
            )
        pl.semaphore_wait(barrier, len(devices))

    def settle(self):
        for copy in self.open:
            copy.wait_send()
        self.open = []


def arrived(copies):
    for copy in copies:
        copy.wait_recv()


def interleave(parts, order):
    for letter in order:
        next(parts[ord(letter) - ord("a")], None)
    finish(*parts)


def cut(count):
    upper = (count // 2 + 15) // 16 * 16
    return upper, count - upper


def owner_cols(y, c, b):
    return pl.ds(pl.multiple_of(b * 1024 + (2 * y + c) * LANES, LANES), LANES)


def gather_yc(links, src, dst, first=0, count=0):
    count = count or src.shape[0]
    top, low = cut(count)
    h0, h1 = pl.ds(first, top), pl.ds(first + top, low)
    full = pl.ds(first, count)

    def mine(part, b):
        return src.at[part, pl.ds(b * LANES, LANES)]

    def slot(y, c, part, b):
        return dst.at[part, owner_cols(y, c, b)]

    def push(y, part, device, own=False):
        c = links.c
        return [
            links.send(mine(part, b) if own else slot(y, c, part, b), slot(y, c, part, b), device)
            for b in range(2)
        ]

    y, up, down, far = links.y, links.at_y(1), links.at_y(-1), links.at_y(2)
    fwd, bwd, sib = links.to_y(1), links.to_y(-1), links.sibling()
    a0 = push(y, h0, fwd, True)
    b1 = push(y, h1, bwd, True)
    a1 = push(y, h1, fwd, True)
    b0 = push(y, h0, bwd, True)
    s = push(y, full, sib, True)
    keep = [links.local(mine(full, b), slot(y, links.c, full, b)) for b in range(2)]
    yield
    arrived(a0)
    f0 = push(down, h0, fwd)
    arrived(b1)
    f1 = push(up, h1, bwd)
    yield
    arrived(a1)
    s += push(down, full, sib)
    arrived(b0)
    s += push(up, full, sib)
    yield
    arrived(f0)
    s += push(far, h0, sib)
    arrived(f1)
    s += push(far, h1, sib)
    yield
    arrived(s)
    for copy in keep:
        copy.wait()


def fill(pairs, dst, place, cols):
    value = None
    for left, right in pairs:
        term = jnp.dot(left[place, :], right[:, cols], preferred_element_type=F32)
        value = term if value is None else value + term
    dst[place, cols] = value.astype(BF16)


def scatter_yc(links, pairs, out, src, sib_buf, half_buf, full_buf, begin=0, rows=0):
    rows = rows or src.shape[0]
    top, low = cut(rows)
    step = 64
    whole = pl.ds(begin, rows)
    order = [links.at_y(2), links.at_y(1), links.at_y(-1), links.y]
    fwd, bwd, sib = links.to_y(1), links.to_y(-1), links.sibling()
    mine, other = links.c, 1 - links.c
    got = []

    def produce(k):
        for b in range(2):
            fill(pairs, src, whole, pl.ds(pl.multiple_of(b * 1024 + order[k] * 256, 256), 256))
        got.append(
            [
                links.send(
                    src.at[whole, owner_cols(order[k], other, b)], sib_buf.at[k, whole, pl.ds(b * LANES, LANES)], sib
                )
                for b in range(2)
            ]
        )

    def total(k, place, b):
        lanes = slice(b * LANES, (b + 1) * LANES)
        return src[place, owner_cols(order[k], mine, b)].astype(F32) + sib_buf[k, place, lanes].astype(F32)

    def over(first, count, body):
        def run(i, _):
            body(pl.multiple_of(first + i * step, 16))
            return 0

        assert count % step == 0
        lax.fori_loop(0, count // step, run, 0)

    def put(k, first, count, more=None):
        def body(at):
            place = pl.ds(at, step)
            for b in range(2):
                lanes = slice(b * LANES, (b + 1) * LANES)
                value = total(k, place, b)
                if more is not None:
                    value = value + more[place, lanes].astype(F32)
                sib_buf[k, place, lanes] = value.astype(BF16)

        over(first, count, body)

    middle = begin + top
    t, l = pl.ds(begin, top), pl.ds(middle, low)
    produce(0)
    yield
    produce(1)
    arrived(got[0])
    put(0, begin, top)
    h0 = links.send(sib_buf.at[0, t, :], half_buf.at[t, :], fwd)
    put(0, middle, low)
    h1 = links.send(sib_buf.at[0, l, :], half_buf.at[l, :], bwd)
    yield
    produce(2)
    arrived(got[1])
    put(1, middle, low)
    p1 = links.send(sib_buf.at[1, l, :], full_buf.at[0, l, :], fwd)
    yield
    produce(3)
    arrived(got[2])
    put(2, begin, top)
    m1 = links.send(sib_buf.at[2, t, :], full_buf.at[1, t, :], bwd)
    yield
    h0.wait_recv()
    put(1, begin, top, half_buf)
    p0 = links.send(sib_buf.at[1, t, :], full_buf.at[0, t, :], fwd)
    h1.wait_recv()
    put(2, middle, low, half_buf)
    m0 = links.send(sib_buf.at[2, l, :], full_buf.at[1, l, :], bwd)
    yield
    arrived(got[3])
    arrived([p1, m1, p0, m0])

    def last(at):
        place = pl.ds(at, step)
        for b in range(2):
            lanes = slice(b * LANES, (b + 1) * LANES)
            out[place, lanes] = (
                total(3, place, b)
                + full_buf[0, place, lanes].astype(F32)
                + full_buf[1, place, lanes].astype(F32)
            )

    over(begin, rows, last)


def scatter_yc_scratch(rows):
    return [
        pltpu.VMEM((rows, 2048), BF16),
        pltpu.VMEM((4, rows, 256), BF16),
        pltpu.VMEM((rows, 256), BF16),
        pltpu.VMEM((2, rows, 256), BF16),
    ]


def yc_peers(links):
    return [
        {"y": links.at_y(dy), "c": lax.rem(links.c + dc, 2)}
        for dy in range(4)
        for dc in range(2)
        if (dy, dc) != (0, 0)
    ]


def sum_dots(links, src, out, buf):
    me = 2 * links.y + links.c
    copies = [links.send(src, buf.at[me], device) for device in yc_peers(links)]
    yield
    yield
    arrived(copies)
    total = src[...]
    for dy in range(4):
        for dc in range(2):
            if (dy, dc) != (0, 0):
                total = total + buf[2 * links.at_y(dy) + lax.rem(links.c + dc, 2)]
    out[...] = total


def xz_slot(dst, x, z, part):
    zh, zl = lax.div(z, 2), lax.rem(z, 2)
    rows = pl.ds(pl.multiple_of(zh * (dst.shape[0] // 2) + part.start, 16), part.size)
    return dst.at[rows, pl.ds(pl.multiple_of((2 * x + zl) * 256, 256), 256)]


AROUND = (2, 1, 3)


def xz_peers(links):
    return [links.to_x(by) for by in AROUND] + [links.to_z(by) for by in AROUND]


def gather_xz(links, src, dst, first=0):
    rows = src.shape[0]
    a, b = (first, rows - first) if first else cut(rows)
    keep = links.local(src, xz_slot(dst, links.x, links.z, pl.ds(0, rows)))
    upper, lower = pl.ds(0, a), pl.ds(a, b)

    def own(part, device):
        return links.send(src.at[part, :], xz_slot(dst, links.x, links.z, part), device)

    along_x = [(own(upper, links.to_x(by)), own(lower, links.to_x(by))) for by in AROUND]
    yield
    along_z = [(own(lower, links.to_z(by)), own(upper, links.to_z(by))) for by in AROUND]
    yield
    far = [pair[1] for pair in along_x + along_z]
    for by, (copy, _) in zip(AROUND, along_x):
        copy.wait_recv()
        piece = xz_slot(dst, links.at_x(-by), links.z, upper)
        far.extend(links.send(piece, piece, links.to_z(on)) for on in AROUND)
    for by, (copy, _) in zip(AROUND, along_z):
        copy.wait_recv()
        piece = xz_slot(dst, links.x, links.at_z(-by), lower)
        far.extend(links.send(piece, piece, links.to_x(on)) for on in AROUND)
    yield
    arrived(far)
    keep.wait()


def add_rows(count, terms, into):
    step = 16
    for size in (32, 48, 64, 80, 88, 96):
        if size % 16 == 0 and count % size == 0:
            step = size
    width = into[0].shape[-1]

    def pick(ref, first, lane, i):
        place = pl.ds(pl.multiple_of(first + i * step, 16), step)
        lanes = pl.ds(0 if lane is None else pl.multiple_of(lane, LANES), width)
        return place, lanes

    def body(i, _):
        value = None
        for ref, first, lane in terms:
            place, lanes = pick(ref, first, lane, i)
            term = ref[place, lanes].astype(F32)
            value = term if value is None else value + term
        ref, first, lane = into
        place, lanes = pick(ref, first, lane, i)
        ref[place, lanes] = value.astype(ref.dtype)
        return 0

    lax.fori_loop(0, count // step, body, 0)


def scatter_xz(links, src, out, near, near2):
    rows = out.shape[0]
    a, b = cut(rows)

    def by_xz(x, z):
        z = jnp.int32(z) if isinstance(z, int) else z
        return lax.div(z, 2), (2 * x + lax.rem(z, 2)) * 256

    halves = [
        (0, a, links.at_x, links.to_x, links.at_z, links.to_z, by_xz),
        (a, b, links.at_z, links.to_z, links.at_x, links.to_x, lambda z, x: by_xz(x, z)),
    ]
    came = []
    for which, (first, count, at1, to1, at2, to2, place_of) in enumerate(halves):
        copies = []
        for by in AROUND:
            for q in range(4):
                zh, lane = place_of(at1(by), q)
                part = src.at[
                    pl.ds(pl.multiple_of(zh * rows + first, 16), count), pl.ds(pl.multiple_of(lane, 256), 256)
                ]
                copies.append(links.send(part, near.at[which, by - 1, q, pl.ds(0, count), :], to1(by)))
        came.append(copies)
    yield
    last = []
    for which, (first, count, at1, to1, at2, to2, place_of) in enumerate(halves):
        arrived(came[which])
        for q in range(4):
            zh, lane = place_of(at1(0), q)
            add_rows(
                count,
                [(src, zh * rows + first, lane), *[(near.at[which, k, q], 0, None) for k in range(3)]],
                (near.at[which, 0, q], 0, None),
            )
        last.append(
            [
                links.send(
                    near.at[which, 0, at2(by), pl.ds(0, count), :], near2.at[which, by - 1, pl.ds(0, count), :], to2(by)
                )
                for by in AROUND
            ]
        )
    yield
    for which, (first, count, at1, to1, at2, to2, place_of) in enumerate(halves):
        arrived(last[which])
        add_rows(
            count,
            [(near.at[which, 0, at2(0)], 0, None), *[(near2.at[which, k], 0, None) for k in range(3)]],
            (out, first, None),
        )


def scatter_xz_scratch(rows):
    a, _ = cut(rows)
    return [pltpu.VMEM((2, 3, 4, a, 256), BF16), pltpu.VMEM((2, 3, a, 256), BF16)]


def scatter_grad(links, left, right, out, src, near, near2):
    rows = 2 * out.shape[0]
    for i in range(4):
        cols = slice(512 * i, 512 * (i + 1))
        value = lax.dot_general(
            left[...], right[:, cols], (((0,), (0,)), ((), ())), preferred_element_type=F32
        ).astype(BF16)
        src[0:rows, cols] = value
        yield
    yield from scatter_xz(links, src, out, near, near2)


def row_peers(links):
    peers = []
    for dx in range(4):
        for dz in range(4):
            if (dx, dz) != (0, 0):
                peers.append({"x": links.at_x(dx), **links.to_z(dz)})
    return peers


def block_of(links, dx, dz):
    z = links.at_z(dz)
    return links.at_x(dx) * 4 + lax.rem(z, 2) * 2 + lax.div(z, 2)


def exchange_rows(links, src, out):
    me = block_of(links, 0, 0)
    keep = links.local(src, out.at[me])
    copies = [links.send(src, out.at[me], device) for device in row_peers(links)]
    yield
    arrived(copies)
    keep.wait()


def sum_rows(links, src, out, buf):
    me = block_of(links, 0, 0)
    copies = []
    for dx in range(4):
        for dz in range(4):
            if (dx, dz) != (0, 0):
                device = {"x": links.at_x(dx), **links.to_z(dz)}
                lanes = pl.ds(pl.multiple_of(device["zh"] * LANES, LANES), LANES)
                copies.append(links.send(src.at[:, lanes], buf.at[me], device))
    yield
    arrived(copies)
    total = src[:, pl.ds(pl.multiple_of(links.zh * LANES, LANES), LANES)]
    for dx in range(4):
        for dz in range(4):
            if (dx, dz) != (0, 0):
                total = total + buf[block_of(links, dx, dz)]
    out[...] = total


def swap_pairs(links, ins, outs):
    lanes = pl.ds(pl.multiple_of(links.zh * LANES, LANES), LANES)
    keep, got = [], []
    for src, dst in zip(ins, outs):
        place = dst.at[pl.ds(0, src.shape[1]), lanes]
        got.append(links.send(src.at[1 - links.zh], place, links.to_z(2)))
    for src, dst in zip(ins, outs):
        place = dst.at[pl.ds(0, src.shape[1]), lanes]
        keep.append(links.local(src.at[links.zh], place))
    return got, keep


def unswap_pair(links, src, dst):
    mine = pl.ds(pl.multiple_of(links.zh * LANES, LANES), LANES)
    theirs = pl.ds(pl.multiple_of((1 - links.zh) * LANES, LANES), LANES)
    got = links.send(src.at[:, theirs], dst.at[links.zh], links.to_z(2))
    keep = links.local(src.at[:, mine], dst.at[links.zh])
    yield
    got.wait_recv()
    keep.wait()


def swap_only(links, src, dst):
    got, keep = swap_pairs(links, (src,), (dst,))
    for _ in range(4):
        yield
    arrived(got)
    for copy in keep:
        copy.wait()


def block_device(block):
    block = lax.rem(block + 16, 16)
    return {"x": lax.div(block, 4), "zl": lax.rem(lax.div(block, 2), 2), "zh": lax.rem(block, 2)}


def conv_backward(
    links, gg, u, q, z, k, v, p, halo, taps, m1, m2, ends, enter, free, dec, dec_seg, res, skip, rates, starts,
    gp, res_out, rate_out, skip_out, conv_out, edge, edge_in, back_ends, last, lasts, back_enter, kept, gq, gz,
):
    me = block_of(links, 0, 0)
    for b in range(2):
        back_first(b, gg, q, m1, free, dec, dec_seg, back_ends, last)
        if b == 0:
            yield
    going = exchange_rows(links, last, lasts)
    next(going)
    yield
    finish(going)
    total = jnp.zeros(last.shape, F32)
    for j in range(lasts.shape[0]):
        apart = (jnp.maximum(j - me - 1, 0) * p.shape[0]).astype(F32)
        after = (me < j).astype(F32)
        still = open_between(starts, (me + 1) * p.shape[0], j * p.shape[0])
        total = total + lasts[j] * (after * still * jnp.exp(-rates[...] * apart))
    back_enter[...] = total
    for b in range(2):
        for part in range(2):
            if (b, part) != (0, 0):
                keep_states(b, part, z, m1, ends, enter, free, dec, dec_seg, kept)
                yield
            back_poles(
                b, part, gg, u, q, z, m1, back_ends, back_enter, free, dec, dec_seg, res, skip,
                res_out, rate_out, skip_out, kept, gq, gz,
            )
            yield
        back_taps(b, v, k, p, halo, taps, m1, m2, gp, edge, conv_out, gq, gz)
        yield
    got = links.send(edge, edge_in, block_device(me - 1))
    yield
    got.wait_recv()
    for b in range(2):
        mend_edges(b, taps, edge_in, gp)


def shape(*dims, dtype=F32):
    return jax.ShapeDtypeStruct(dims, dtype)


def finish(*parts):
    for part in parts:
        for _ in part:
            pass


NT = (((1,), (1,)), ((), ()))


def open_between(starts, low, high):
    at = starts[...]
    hit = jnp.where((at >= low) & (at < high), 1.0, 0.0)
    return 1.0 - jnp.max(hit, axis=0, keepdims=True)


def write_masks(block, starts, m1, m2):
    rows = m1.shape[0]
    seg = rows // SEGS
    firsts = [jnp.broadcast_to(starts[j : j + 1, 0:LANES], (SEGS, LANES)) for j in range(DOCS)]
    base = block * rows + seg_rows() * seg

    def carries_on(place):
        hit = place == firsts[0]
        for first in firsts[1:]:
            hit = hit | (place == first)
        return jnp.where(hit, 0.0, 1.0)

    def step(i, earlier):
        one = carries_on(base + i)
        m1[tile(i), :] = one
        m2[tile(i), :] = one * earlier
        return one

    lax.fori_loop(0, seg, step, carries_on(base - 1))


def forward_half(
    links, tok, small, cot_pair, win_t, wout_t, wgate_t, starts, up_t, down,
    xg_out, win_out, wout_out, cs, p_out, q_out, z_out, k_out, v_out, xs_out, hg_out, wdown_out, hidden_out, gh_out,
    u, gated, halo, ends, free, enter, params, r1, m1, m2, acts, gg, gu, dots, r2, sum_down,
    xr, xs, sm, xg, gains, inv, inv_g2, win, p, q, z, k, v, dec, dec_seg, taps, res, skip, last, lasts,
    cot, wout, wgate, wup, wdown, own_dots, dots_buf, *held,
):
    rows, width = xg.shape
    poles = dec.shape[0]
    me = block_of(links, 0, 0)
    got, keep = swap_pairs(links, (small, tok), (sm, xr))
    win_in = gather_xz(links, win_t, win, win_t.shape[0] // 4)
    next(win_in)
    cot_swap = swap_only(links, cot_pair, cs)
    wout_in = gather_xz(links, wout_t, wout)
    wgate_in = gather_xz(links, wgate_t, wgate)
    write_masks(me, starts, m1, m2)
    arrived(got[:1])
    keep[0].wait()
    gain_rows = gather_yc(links, sm.at[pl.ds(0, 32), :], gains)
    next(gain_rows)
    values = sm[...].astype(F32)
    rate = jnp.exp(values[32:48])
    dec[...] = jnp.exp(-rate)
    dec_seg[...] = jnp.exp(-rate * (rows // SEGS))
    taps[...] = values[16:32]
    res[...] = values[48:64]
    skip[...] = jnp.broadcast_to(values[2:3], (SEGS, 2 * LANES))
    params[0:16, :] = values[0:16]
    params[16:32, :] = values[16:32]
    params[32:48, :] = rate
    params[48:64, :] = values[48:64]
    arrived(got[1:])
    keep[1].wait()

    def gained(i, _):
        place = pl.ds(pl.multiple_of(i * 64, 64), 64)
        xs[place, :] = (xr[place, :].astype(F32) * params[0:1, :]).astype(BF16)
        return 0

    lax.fori_loop(0, rows // 64, gained, 0)
    columns = gather_yc(links, xs, xg)
    next(columns)
    next(win_in)
    next(cot_swap)
    next(gain_rows)
    next(gain_rows)
    next(columns)
    next(win_in)
    next(columns)
    next(gain_rows)
    finish(columns)
    finish(gain_rows, win_in)
    inv[...] = 1.0 / gains[0:16, :].astype(F32)
    inv_g2[...] = inv[1:2, :]
    stores = [links.local(xg, xg_out), links.local(win, win_out), links.local(xr, xs_out)]
    step = 256

    def project(i, _):
        place = pl.ds(pl.multiple_of(i * step, step), step)
        r = rows_scale(xg, inv, place, width)
        r1[place, :] = jnp.broadcast_to(r, (step, LANES))
        p[place, :] = r * lax.dot_general(xg[place, :], win[...], NT, preferred_element_type=F32)
        return 0

    lax.fori_loop(0, rows // step, project, 0)
    stores.append(links.local(p, p_out))
    tail = links.send(p.at[pl.ds(rows - 16, 16), :], halo, block_device(me + 1))
    for part in (wgate_in, wout_in):
        next(part)
        next(part)
    finish(cot_swap)
    cot_in = gather_yc(links, cs, cot)
    next(cot_in)
    tail.wait_recv()
    for b in range(2):
        conv_first(b, p, halo, taps, m1, m2, dec, dec_seg, q, z, k, v, ends, free, last)
    going = exchange_rows(links, last, lasts)
    next(going)
    next(cot_in)
    next(wgate_in)
    next(wout_in)
    stores += [links.local(q, q_out), links.local(z, z_out), links.local(k, k_out), links.local(v, v_out)]
    finish(going)
    rates = params[32:48, :]
    total = jnp.zeros((poles, 2 * LANES), F32)
    for j in range(lasts.shape[0]):
        apart = (jnp.maximum(me - 1 - j, 0) * rows).astype(F32)
        before = (me > j).astype(F32)
        total = total + lasts[j] * (before * open_between(starts, (j + 1) * rows, me * rows) * jnp.exp(-rates * apart))
    enter[...] = total
    conv_second(0, q, z, m1, ends, free, enter, dec, dec_seg, res, skip, u, gated)
    next(cot_in)
    conv_second(1, q, z, m1, ends, free, enter, dec, dec_seg, res, skip, u, gated)
    finish(wout_in)
    for copy in stores:
        copy.wait()
    links.settle()
    one, two, held = held[:4], held[4:7], held[7:]
    mixer, hidden, gh = z, v, k
    beside = [gather_xz(links, up_t, wup, 128), gather_xz(links, down, wdown, 128)]
    for part in beside:
        next(part)
    steps = lambda part, count: [next(part, None) for _ in range(count)]
    sums = scatter_yc(links, [(gated, wout)], mixer, *one)
    steps(sums, 2)
    for part in beside:
        next(part)
    steps(sums, 3)
    for part in beside:
        next(part)
    finish(sums, cot_in)

    def residual(i, _):
        place = pl.ds(pl.multiple_of(i * 64, 64), 64)
        value = xr[place, :].astype(F32) + mixer[place, :]
        hidden[place, :] = value
        xs[place, :] = (value * params[1:2, :]).astype(BF16)
        return 0

    lax.fori_loop(0, rows // 64, residual, 0)
    finish(gather_yc(links, xs, xg), wgate_in, *beside)
    links.settle()
    kept = [links.local(wdown, wdown_out), links.local(xg, hg_out), links.local(wout, wout_out)]
    kept.append(links.local(hidden, hidden_out))
    step = 256

    def block(i, _):
        place = pl.ds(pl.multiple_of(i * step, step), step)
        r = rows_scale(xg, inv_g2, place, width)
        r2[place, :] = jnp.broadcast_to(r, (step, LANES))
        h = xg[place, :]
        gate = r * lax.dot_general(h, wgate[...], NT, preferred_element_type=F32)
        upper = r * lax.dot_general(h, wup[...], NT, preferred_element_type=F32)
        g_act = lax.dot_general(cot[place, :], wdown[...], NT, preferred_element_type=F32)
        sig = jax.nn.sigmoid(gate)
        acts[place, :] = (gate * sig * upper).astype(BF16)
        g_gate = g_act * upper * (sig * (1.0 + gate * (1.0 - sig)))
        g_upper = g_act * gate * sig
        gg[place, :] = (r * g_gate).astype(BF16)
        gu[place, :] = (r * g_upper).astype(BF16)
        both = (g_gate * gate + g_upper * upper).astype(BF16)
        own_dots[:, place] = lax.dot_general(
            jnp.ones((8, both.shape[1]), BF16), both, NT, preferred_element_type=F32
        )
        return 0

    lax.fori_loop(0, rows // step, block, 0)
    parts = [
        scatter_yc(links, [(gg, wgate), (gu, wup)], gh, one[0], *two),
        scatter_grad(links, acts, cot, sum_down, win, *held),
        sum_dots(links, own_dots, dots, dots_buf),
    ]
    interleave(parts, "bbbbbcaaaaabaa")
    kept.append(links.local(gh, gh_out))
    for copy in kept:
        copy.wait()


def rows_scale(x, gain, place, width):
    square = jnp.zeros((place.size, LANES), F32)
    for k in range(width // LANES):
        lanes = slice(LANES * k, LANES * (k + 1))
        plain = x[place, lanes].astype(F32) * gain[0:1, lanes]
        square = square + plain * plain
    return lax.rsqrt(jnp.sum(square, axis=1, keepdims=True) / width + EPS)


def mixer_back(
    links, g_o, wout, gated, acts, wdown, gg_low, gu_low, hg, hidden, u, q, z, k, v, p, halo, taps, m1, m2,
    ends, enter, free, dec, dec_seg, res, skip, rates, starts,
    gp, res_out, rate_out, skip_out, conv_out, mixed, sum_gate, sum_up, sum_out,
    g_mix, gg, mlp, mixed_half, edge, edge_in, back_ends, last, lasts, back_enter, kept, gq, gz, *held,
):
    rows = gg.shape[0]
    columns = gather_yc(links, g_o, g_mix)
    gate = scatter_grad(links, gg_low, hg, sum_gate, *held[4:7])
    up = scatter_grad(links, gu_low, hg, sum_up, *held[7:10])
    out = scatter_grad(links, gated, g_mix, sum_out, *held[10:13])
    down = scatter_yc(links, [(acts, wdown)], mlp, *held[:4])
    steps = lambda part, count: [next(part, None) for _ in range(count)]
    steps(columns, 1)
    steps(gate, 5)
    steps(columns, 1)
    steps(up, 5)
    steps(columns, 2)
    steps(down, 2)
    keep_states(0, 0, z, m1, ends, enter, free, dec, dec_seg, kept)
    finish(columns)
    gg[...] = lax.dot_general(g_mix[...], wout[...], NT, preferred_element_type=F32)
    back = conv_backward(
        links, gg, u, q, z, k, v, p, halo, taps, m1, m2, ends, enter, free, dec, dec_seg, res, skip, rates, starts,
        gp, res_out, rate_out, skip_out, conv_out, edge, edge_in, back_ends, last, lasts, back_enter, kept, gq, gz,
    )
    steps(back, 2)
    steps(down, 2)
    steps(gate, 1)
    steps(up, 1)
    steps(back, 1)
    steps(down, 1)
    steps(out, 5)
    steps(back, 1)
    finish(gate)
    steps(back, 1)
    steps(down, 1)
    steps(out, 1)
    steps(back, 1)
    finish(up)
    steps(back, 1)
    finish(down)

    def mix(i, _):
        place = pl.ds(pl.multiple_of(i * 64, 64), 64)
        mixed_half[place, :] = (hidden[place, :] + mlp[place, :]).astype(BF16)
        return 0

    lax.fori_loop(0, rows // 64, mix, 0)
    swapped = unswap_pair(links, mixed_half, mixed)
    steps(swapped, 1)
    finish(back, out, swapped)


def input_back(
    links, gp, p, r1, xg, win, g_hidden, xs, g1, conv, rate_raw, res_raw, skip_raw, rate, res, gain2,
    sum_in, grad, tiny_out,
    gp_low, own_dots, dots, dots_buf, gx, grad_half, tiny, tiny_buf, *held,
):
    rows = gp.shape[0]
    width = xg.shape[1]
    step = 256

    def scale(i, _):
        place = pl.ds(pl.multiple_of(i * step, step), step)
        value = gp[place, :]
        both = (value * p[place, :]).astype(BF16)
        own_dots[:, place] = lax.dot_general(
            jnp.ones((8, both.shape[1]), BF16), both, NT, preferred_element_type=F32
        )
        gp_low[place, :] = (r1[place, 0:1] * value).astype(BF16)
        return 0

    lax.fori_loop(0, rows // step, scale, 0)
    parts = [
        scatter_yc(links, [(gp_low, win)], gx, *held[:4]),
        sum_dots(links, own_dots, dots, dots_buf),
        scatter_grad(links, gp_low, xg, sum_in, *held[4:]),
    ]
    for letter in "bcccccaaaaaca":
        next(parts[ord(letter) - ord("a")], None)
    finish(parts[0], parts[1])
    line = lax.broadcasted_iota(jnp.int32, dots.shape, 0)
    value = dots[...]
    high = value.astype(BF16).astype(F32)
    pair = jnp.where(line == 0, high, jnp.where(line == 1, value - high, 0.0)).astype(BF16)
    column = lax.dot_general(
        pair, jnp.ones((8, LANES), BF16), (((0,), (0,)), ((), ())), preferred_element_type=F32
    )
    tiny[...] = jnp.zeros_like(tiny)
    pull = r1[...] * r1[...] * column / width
    for b in range(2):
        lanes = lanes_of(b)
        x = xs[:, lanes].astype(F32)
        got = gx[:, lanes]
        grad_half[:, lanes] = (g_hidden[:, lanes] + g1[0:1, lanes] * got - x * pull).astype(BF16)
        tiny[0:1, lanes] = jnp.sum(got * x, axis=0, keepdims=True)
    tiny[1:2, :] = gain2[...]
    tiny[2:3, :] = jnp.sum(skip_raw[...], axis=0, keepdims=True)
    tiny[8:24, :] = conv[...]
    tiny[24:40, :] = -rate[...] * res[...] * rate_raw[...]
    tiny[40:56, :] = res_raw[...]
    swapped = unswap_pair(links, grad_half, grad)
    summed = sum_rows(links, tiny, tiny_out, tiny_buf)
    next(swapped)
    next(summed)
    finish(parts[2], summed, swapped)


def fused(number, maker, peers, inputs, outs, scratch, copies):
    vmem = pl.BlockSpec(memory_space=pltpu.VMEM)
    hbm = pl.BlockSpec(memory_space=pl.ANY)
    staged = [i for i, (_, kind) in enumerate(inputs) if kind == "s"]
    n_in, n_out = len(inputs), len(outs)

    def kernel(*refs):
        ins, results = list(refs[:n_in]), refs[n_in : n_in + n_out]
        held = refs[n_in + n_out : -2]
        links = Links(refs[-2], refs[-1])
        moves = []
        for i, buf in zip(staged, held):
            moves.append(links.local(ins[i], buf))
            ins[i] = buf
        met = []
        if "Y" in peers:
            met += yc_peers(links)
        elif "y" in peers:
            met += [links.to_y(1), links.to_y(-1), links.sibling()]
        if "r" in peers:
            met += row_peers(links)
        elif "x" in peers:
            met += xz_peers(links)
        links.greet(met)
        for move in moves:
            move.wait()
        maker(links, *ins, *results, *held[len(staged) :])
        links.settle()
        assert links.used <= copies

    return pl.pallas_call(
        kernel,
        in_specs=[vmem if kind == "v" else hbm for _, kind in inputs],
        out_specs=[vmem if kind == "v" else hbm for _, kind in outs],
        out_shape=[kept for kept, _ in outs],
        scratch_shapes=[
            *[pltpu.VMEM(inputs[i][0].shape, inputs[i][0].dtype) for i in staged],
            *scratch,
            pltpu.SemaphoreType.DMA((copies,)),
            pltpu.SemaphoreType.DMA((copies,)),
        ],
        compiler_params=pltpu.CompilerParams(
            collective_id=number, has_side_effects=True, vmem_limit_bytes=VMEM_LIMIT
        ),
    )(*[array for array, _ in inputs])


def grad_scratch(rows):
    return [pltpu.VMEM((2 * rows, 2048), BF16), *scatter_xz_scratch(rows)]


def shards(
    tokens, gain_first, gain_second, w_in, conv_w, log_rate, residue, skip,
    w_out, w_gate, w_up, w_down, cotangent, lengths,
):
    rows = tokens.shape[0] // 2
    width = 16 * LANES
    seg = rows // SEGS

    def stepped(value):
        return value.reshape(2, SEGS, seg, LANES).transpose(0, 2, 1, 3).reshape(2, rows, LANES)

    def unstepped(value):
        return value.reshape(2, seg, SEGS, LANES).transpose(0, 2, 1, 3).reshape(2 * rows, LANES)

    before = jnp.arange(DOCS)[:, None] < jnp.arange(DOCS)[None, :]
    starts = jnp.sum(jnp.where(before, lengths[:, None], 0), axis=0)
    starts = jnp.broadcast_to(starts[:, None], (DOCS, 2 * LANES))

    line = lax.broadcasted_iota(jnp.int32, (16, LANES), 0)
    singles = jnp.where(line == 0, gain_first, jnp.where(line == 1, gain_second, jnp.where(line == 2, skip, 0)))
    taps_own = jnp.pad(conv_w.reshape(9, LANES), ((0, 7), (0, 0)))
    small = jnp.concatenate([singles.astype(BF16), taps_own, log_rate, residue])
    hidden_units = w_gate.shape[1]
    half = (rows, 2 * LANES)
    weight = (2 * hidden_units, width)
    act = shape(*half)
    low = shape(*half, dtype=BF16)
    proj_shape = shape(rows, 6 * LANES)
    units = shape(rows, 2 * hidden_units, dtype=BF16)
    broad = shape(rows, width, dtype=BF16)
    sixteen = shape(16, 2 * LANES)
    vm = lambda kept: pltpu.VMEM(kept.shape, kept.dtype)
    (
        xg, win, wout, cs, proj, q, z, k, v, xs, hg, wdown, hidden, gh, u, gated, halo, seg_ends, free, enter, params,
        r1, mask1, mask2, acts, gg_low, gu_low, dot2, r2, sums_down,
    ) = fused(
        1,
        forward_half,
        "Yr",
        [
            (stepped(tokens), "h"), (jnp.broadcast_to(small[None], (2, 64, LANES)), "h"), (stepped(cotangent), "h"),
            (w_in.transpose(1, 2, 0).reshape(3 * LANES, 256), "h"), (w_out, "h"), (w_gate.T, "h"),
            (starts, "v"), (w_up.T, "h"), (w_down, "h"),
        ],
        [
            (broad, "h"), (shape(6 * LANES, width, dtype=BF16), "h"), (shape(2 * LANES, width, dtype=BF16), "h"),
            (low, "h"), (proj_shape, "h"), (act, "h"), (act, "h"), (act, "h"), (act, "h"), (low, "h"), (broad, "h"),
            (shape(*weight, dtype=BF16), "h"), (act, "h"), (act, "h"),
            (act, "v"), (low, "v"), (shape(16, 768), "v"), (shape(128, 256), "v"), (shape(8, 256), "v"),
            (sixteen, "v"), (shape(64, 256), "v"), (shape(rows, LANES), "v"), (shape(rows, LANES), "v"),
            (shape(rows, LANES), "v"), (units, "v"), (units, "v"), (units, "v"),
            (shape(8, rows), "v"), (shape(rows, LANES), "v"), (shape(hidden_units, 2 * LANES), "v"),
        ],
        [
            vm(low), vm(low), pltpu.VMEM((64, 256), BF16), vm(broad), pltpu.VMEM((32, width), BF16),
            pltpu.VMEM((16, width), F32), pltpu.VMEM((1, width), F32), pltpu.VMEM((6 * LANES, width), BF16),
            vm(proj_shape), *([vm(act)] * 4), vm(sixteen), vm(sixteen), vm(sixteen), vm(sixteen),
            pltpu.VMEM((8, 256), F32), vm(sixteen), pltpu.VMEM((16, 16, 256), F32),
            vm(broad), pltpu.VMEM((2 * LANES, width), BF16), *([pltpu.VMEM(weight, BF16)] * 3),
            pltpu.VMEM((8, rows), F32), pltpu.VMEM((8, 8, rows), F32),
            *scatter_yc_scratch(rows), *scatter_yc_scratch(rows)[1:], *scatter_xz_scratch(hidden_units),
        ],
        400,
    )
    g1, g2 = params[0:1], params[1:2]
    skip8 = jnp.broadcast_to(params[2:3], (8, 2 * LANES))
    taps, rate, res = params[16:32], params[32:48], params[48:64]
    dec = jnp.exp(-rate)
    dec_seg = jnp.exp(-rate * seg)

    r2 = r2[:, :1]
    dot2 = dot2[0][:, None]
    g_hidden = cs.astype(F32) + g2 * gh - hidden * (r2 * r2 * dot2 / width)
    grad_gain2 = jnp.sum(gh * hidden, axis=0)
    g_proj, res_raw, rate_raw, skip_raw, conv_raw, mixed, sums_gate, sums_up, sums_out = fused(
        4,
        mixer_back,
        "yr",
        [
            (g_hidden.astype(BF16), "h"), (wout, "s"), (gated, "s"), (acts, "s"), (wdown, "s"), (gg_low, "s"),
            (gu_low, "s"), (hg, "s"), (hidden, "s"), (u, "s"), (q, "s"), (z, "s"), (k, "s"), (v, "s"), (proj, "s"),
            (halo, "v"), (taps, "v"), (mask1, "s"), (mask2, "s"), (seg_ends, "v"), (enter, "v"), (free, "v"),
            (dec, "v"), (dec_seg, "v"), (res, "v"), (skip8, "v"), (rate, "v"), (starts, "v"),
        ],
        [
            (proj_shape, "v"), (sixteen, "v"), (sixteen, "v"), (shape(8, 2 * LANES), "v"), (sixteen, "v"),
            (shape(2, rows, LANES, dtype=BF16), "h"), *[(shape(hidden_units, 2 * LANES), "v")] * 2,
            (shape(LANES, 2 * LANES), "v"),
        ],
        [
            pltpu.VMEM((rows, width), BF16), pltpu.VMEM(half, F32), pltpu.VMEM(half, F32), pltpu.VMEM(half, BF16),
            pltpu.VMEM((24, 6 * LANES), F32), pltpu.VMEM((24, 6 * LANES), F32), pltpu.VMEM((128, 256), F32),
            pltpu.VMEM((16, 256), F32), pltpu.VMEM((16, 16, 256), F32), pltpu.VMEM((16, 256), F32),
            pltpu.VMEM((seg, 8, SEGS, LANES), F32), pltpu.VMEM((rows, LANES), F32), pltpu.VMEM((rows, LANES), F32),
            *scatter_yc_scratch(rows), *(grad_scratch(hidden_units) * 2), *grad_scratch(LANES),
        ],
        220,
    )
    sums_in, grad_tok, tiny = fused(
        5,
        input_back,
        "Yr",
        [
            (g_proj, "s"), (proj, "s"), (r1, "s"), (xg, "s"), (win, "s"), (g_hidden, "s"), (xs, "s"), (g1, "v"),
            (conv_raw, "v"), (rate_raw, "v"), (res_raw, "v"), (skip_raw, "v"), (rate, "v"), (res, "v"),
            (grad_gain2[None], "v"),
        ],
        [
            (shape(3 * LANES, 2 * LANES), "v"), (shape(2, rows, LANES, dtype=BF16), "h"), (shape(56, LANES), "v"),
        ],
        [
            pltpu.VMEM((rows, 6 * LANES), BF16), pltpu.VMEM((8, rows), F32), pltpu.VMEM((8, rows), F32),
            pltpu.VMEM((8, 8, rows), F32), pltpu.VMEM(half, F32), pltpu.VMEM(half, BF16), pltpu.VMEM((56, 256), F32),
            pltpu.VMEM((16, 56, LANES), F32), *scatter_yc_scratch(rows), *grad_scratch(3 * LANES),
        ],
        120,
    )
    return (
        unstepped(mixed),
        unstepped(grad_tok).astype(F32),
        tiny[0],
        tiny[1],
        sums_in.reshape(3, LANES, 256).transpose(2, 0, 1),
        tiny[8:17].reshape(3, 3, LANES),
        tiny[24:40],
        tiny[40:56],
        tiny[2],
        sums_out,
        sums_gate.T,
        sums_up.T,
        sums_down,
    )


def solution(mesh):
    cube = Mesh(mesh.devices.reshape(4, 2, 2, 4, 2), ("x", "zl", "zh", "y", "c"))
    seq, tp = ("x", "zl"), ("zh", "y", "c")
    return jax.shard_map(
        shards,
        mesh=cube,
        in_specs=(
            P(seq, tp), P(tp), P(tp), P(seq, None, tp), P(None, None, tp), P(None, tp), P(None, tp), P(tp),
            P(tp, seq), P(seq, tp), P(seq, tp), P(tp, seq), P(seq, tp), P(),
        ),
        out_specs=(
            P(seq, tp), P(seq, tp), P(tp), P(tp), P(seq, None, tp), P(None, None, tp), P(None, tp), P(None, tp), P(tp),
            P(tp, seq), P(seq, tp), P(seq, tp), P(tp, seq),
        ),
        check_vma=False,
    )
```

```python
import functools

import jax
import jax.numpy as jnp
from jax import lax
from jax.experimental import pallas as pl
from jax.experimental.pallas import tpu as pltpu
from jax.sharding import Mesh
from jax.sharding import PartitionSpec as P

EPS = 1e-06
DOCS = 8
ROW_AXES = ("x", "zl", "zh")
COL_AXES = ("y", "c")
F32 = jnp.float32
BF16 = jnp.bfloat16
VMEM_LIMIT = 61900 * 1024
SEGS = 8
LANES = 128


def spread(row):
    return jnp.broadcast_to(row, (SEGS, LANES))


def seg_rows():
    return lax.broadcasted_iota(jnp.int32, (SEGS, LANES), 0)


def tile(i):
    return pl.ds(pl.multiple_of(i * SEGS, SEGS), SEGS)


def lanes_of(b, j=0):
    return slice(LANES * (b + j), LANES * (b + j + 1))


def add_all(terms):
    while len(terms) > 1:
        terms = [sum(terms[i + 1 : i + 2], terms[i]) for i in range(0, len(terms), 2)]
    return terms[0]


def scan_up(ends, factor):
    rows = seg_rows()
    for by in (1, 2, 4):
        held = rows >= by
        ends = ends + factor * jnp.where(held, pltpu.roll(ends, by, 0), 0.0)
        factor = factor * jnp.where(held, pltpu.roll(factor, by, 0), 1.0)
    return ends


def scan_down(ends, factor):
    rows = seg_rows()
    for by in (1, 2, 4):
        held = rows < SEGS - by
        ends = ends + factor * jnp.where(held, pltpu.roll(ends, SEGS - by, 0), 0.0)
        factor = factor * jnp.where(held, pltpu.roll(factor, SEGS - by, 0), 1.0)
    return ends


def entering_up(ends, factor, enter):
    first = seg_rows() == 0
    whole = scan_up(ends + jnp.where(first, factor * enter, 0.0), factor)
    return jnp.where(first, enter, pltpu.roll(whole, 1, 0))


def entering_down(ends, factor, enter):
    last = seg_rows() == SEGS - 1
    whole = scan_down(ends + jnp.where(last, factor * enter, 0.0), factor)
    return jnp.where(last, enter, pltpu.roll(whole, SEGS - 1, 0))


def rows_of(ref, count, lanes):
    return [spread(ref[n : n + 1, lanes]) for n in range(count)]


def tap_rows(taps, lanes):
    return [[spread(taps[3 * i + j : 3 * i + j + 1, lanes]) for j in range(3)] for i in range(3)]


def conv_first(b, p, halo, taps, m1, m2, dec, dec_seg, q_out, z_out, k_out, v_out, ends_out, open_out, last_out):
    seg = p.shape[0] // SEGS
    poles = dec.shape[0]
    own = lanes_of(b)
    cols = [lanes_of(3 * b, j) for j in range(3)]
    first = seg_rows() == 0
    d = rows_of(dec, poles, own)
    c = tap_rows(taps, own)

    def before(j, back):
        mine = pltpu.roll(p[SEGS * (seg - back) : SEGS * (seg - back + 1), cols[j]], 1, 0)
        theirs = pltpu.roll(halo[SEGS * (2 - back) : SEGS * (3 - back), cols[j]], 1, 0)
        return jnp.where(first, theirs, mine)

    def step(i, carry):
        state, prev1, prev2, free = carry
        place = tile(i)
        one, two = m1[place, :], m2[place, :]
        cur = [p[place, cols[j]] for j in range(3)]
        q, k, v = [
            c[0][j] * cur[j] + c[1][j] * (one * prev1[j]) + c[2][j] * (two * prev2[j])
            for j in range(3)
        ]
        z = k * v
        q_out[place, own] = q
        k_out[place, own] = k
        v_out[place, own] = v
        z_out[place, own] = z
        state = [d[n] * (one * state[n]) + z for n in range(poles)]
        return (state, cur, prev1, free * one)

    zero = jnp.zeros((SEGS, LANES), F32)
    start = (
        [zero] * poles,
        [before(j, 1) for j in range(3)],
        [before(j, 2) for j in range(3)],
        zero + 1.0,
    )
    state, _, _, free = lax.fori_loop(0, seg, step, start)
    open_out[:, own] = free
    for n in range(poles):
        ends_out[SEGS * n : SEGS * (n + 1), own] = state[n]
        whole = scan_up(state[n], spread(dec_seg[n : n + 1, own]) * free)
        last_out[n : n + 1, own] = whole[SEGS - 1 :, :]


def conv_second(b, q_in, z_in, m1, ends, free, enter, dec, dec_seg, res, skip, u_out, gated_out):
    rows = q_in.shape[0]
    seg = rows // SEGS
    poles = dec.shape[0]
    own = lanes_of(b)
    d = rows_of(dec, poles, own)
    r = rows_of(res, poles, own)
    sk = spread(skip[0:1, own])
    start = [
        entering_up(
            ends[SEGS * n : SEGS * (n + 1), own],
            spread(dec_seg[n : n + 1, own]) * free[:, own],
            spread(enter[n : n + 1, own]),
        )
        for n in range(poles)
    ]

    def step(i, state):
        place = tile(i)
        one, z = m1[place, :], z_in[place, own]
        state = [d[n] * (one * state[n]) + z for n in range(poles)]
        u_out[place, own] = add_all([r[n] * state[n] for n in range(poles)] + [sk * z])
        return state

    lax.fori_loop(0, seg, step, start)

    def rounded(i, _):
        place = pl.ds(pl.multiple_of(i * 64, 64), 64)
        gated_out[place, own] = (q_in[place, own] * u_out[place, own]).astype(BF16)
        return 0

    lax.fori_loop(0, rows // 64, rounded, 0)


def back_first(b, gg_in, q_in, m1, free, dec, dec_seg, ends_out, last_out):
    seg = q_in.shape[0] // SEGS
    poles = dec.shape[0]
    own = lanes_of(b)
    d = rows_of(dec, poles, own)

    def step(t, carry):
        place = tile(seg - 1 - t)
        gu = gg_in[place, own] * q_in[place, own]
        one = m1[place, :]
        return [d[n] * (one * (carry[n] + gu)) for n in range(poles)]

    zero = jnp.zeros((SEGS, LANES), F32)
    carry = lax.fori_loop(0, seg, step, [zero] * poles)
    for n in range(poles):
        ends_out[SEGS * n : SEGS * (n + 1), own] = carry[n]
        whole = scan_down(carry[n], spread(dec_seg[n : n + 1, own]) * free[:, own])
        last_out[n : n + 1, own] = whole[:1, :]


def keep_states(b, part, z_in, m1, ends, enter, free, dec, dec_seg, kept):
    seg = z_in.shape[0] // SEGS
    half = dec.shape[0] // 2
    own = lanes_of(b)
    these = range(half * part, half * (part + 1))
    d = [spread(dec[n : n + 1, own]) for n in these]
    start = [
        entering_up(
            ends[SEGS * n : SEGS * (n + 1), own],
            spread(dec_seg[n : n + 1, own]) * free[:, own],
            spread(enter[n : n + 1, own]),
        )
        for n in these
    ]

    def forward(i, state):
        place = tile(i)
        one, z = m1[place, :], z_in[place, own]
        state = [d[n] * (one * state[n]) + z for n in range(half)]
        for n in range(half):
            kept[i, n] = state[n]
        return state

    lax.fori_loop(0, seg, forward, start)


def back_poles(
    b, part, gg_in, u_in, q_in, z_in, m1, back_ends, back_enter, free, dec, dec_seg, res, skip,
    res_out, rate_out, skip_out, kept, gq, gz,
):
    seg = q_in.shape[0] // SEGS
    half = dec.shape[0] // 2
    own = lanes_of(b)
    zero = jnp.zeros((SEGS, LANES), F32)
    sk = spread(skip[0:1, own])
    these = range(half * part, half * (part + 1))
    d = [spread(dec[n : n + 1, own]) for n in these]
    r = [spread(res[n : n + 1, own]) for n in these]
    carry = [
        entering_down(
            back_ends[SEGS * n : SEGS * (n + 1), own],
            spread(dec_seg[n : n + 1, own]) * free[:, own],
            spread(back_enter[n : n + 1, own]),
        )
        for n in these
    ]

    def backward(t, held):
        carry, by_res, by_rate, by_skip = held
        i = seg - 1 - t
        place = tile(i)
        gg, one = gg_in[place, own], m1[place, :]
        gu = gg * q_in[place, own]
        s = [kept[i, n] for n in range(half)]
        lam = [carry[n] + gu for n in range(half)]
        terms = [r[n] * lam[n] for n in range(half)]
        if part == 0:
            terms.append(sk * gu)
            by_skip = by_skip + gu * z_in[place, own]
            gq[place, :] = gg * u_in[place, own]
        else:
            terms.append(gz[place, :])
        gz[place, :] = add_all(terms)
        by_res = [by_res[n] + gu * s[n] for n in range(half)]
        by_rate = [by_rate[n] + carry[n] * s[n] for n in range(half)]
        carry = [d[n] * (one * lam[n]) for n in range(half)]
        return (carry, by_res, by_rate, by_skip)

    _, by_res, by_rate, by_skip = lax.fori_loop(
        0, seg, backward, (carry, [zero] * half, [zero] * half, zero)
    )
    for k, n in enumerate(these):
        res_out[n : n + 1, own] = jnp.sum(by_res[k], axis=0, keepdims=True)
        rate_out[n : n + 1, own] = jnp.sum(by_rate[k], axis=0, keepdims=True)
    if part == 0:
        skip_out[:, own] = by_skip


def back_taps(b, v_in, k_in, p, halo, taps, m1, m2, gp_out, edge_out, conv_out, gq, gz):
    seg = p.shape[0] // SEGS
    own = lanes_of(b)
    cols = [lanes_of(3 * b, j) for j in range(3)]
    zero = jnp.zeros((SEGS, LANES), F32)
    c = tap_rows(taps, own)
    last = seg_rows() == SEGS - 1

    def short_grads(place):
        g = gz[place, :]
        return [gq[place, :], g * v_in[place, own], g * k_in[place, own]]

    def next_seg(value):
        return jnp.where(last, 0.0, pltpu.roll(value, SEGS - 1, 0))

    g0, g1 = short_grads(tile(0)), short_grads(tile(1))
    a1 = [m1[tile(0), :] * g for g in g0]
    b1 = [m2[tile(0), :] * g for g in g0]
    b2 = [m2[tile(1), :] * g for g in g1]
    for j in range(3):
        edge_out[0:8, cols[j]] = a1[j]
        edge_out[8:16, cols[j]] = b1[j]
        edge_out[16:24, cols[j]] = b2[j]

    def taps_back(t, held):
        late1, late2, later2, sums = held
        place = tile(seg - 1 - t)
        one, two = m1[place, :], m2[place, :]
        g = short_grads(place)
        new = []
        for j in range(3):
            value = p[place, cols[j]]
            gp_out[place, cols[j]] = c[0][j] * g[j] + c[1][j] * late1[j] + c[2][j] * later2[j]
            new += [
                sums[3 * j] + g[j] * value,
                sums[3 * j + 1] + late1[j] * value,
                sums[3 * j + 2] + later2[j] * value,
            ]
        return ([one * x for x in g], [two * x for x in g], late2, new)

    start = (
        [next_seg(x) for x in a1],
        [next_seg(x) for x in b1],
        [next_seg(x) for x in b2],
        [zero] * 9,
    )
    _, _, _, sums = lax.fori_loop(0, seg, taps_back, start)
    for j in range(3):
        old1, old2 = halo[15:16, cols[j]], halo[7:8, cols[j]]
        conv_out[j : j + 1, own] = jnp.sum(sums[3 * j], axis=0, keepdims=True)
        conv_out[3 + j : 4 + j, own] = jnp.sum(sums[3 * j + 1], axis=0, keepdims=True) + a1[j][:1] * old1
        conv_out[6 + j : 7 + j, own] = (
            jnp.sum(sums[3 * j + 2], axis=0, keepdims=True) + b1[j][:1] * old2 + b2[j][:1] * old1
        )


def mend_edges(b, taps, edge_in, gp_out):
    rows = gp_out.shape[0]
    own = lanes_of(b)
    cols = [lanes_of(3 * b, j) for j in range(3)]
    c = tap_rows(taps, own)
    last = seg_rows() == SEGS - 1
    for j in range(3):
        one = pltpu.roll(edge_in[0:8, cols[j]], SEGS - 1, 0)
        two = pltpu.roll(edge_in[8:16, cols[j]], SEGS - 1, 0)
        three = pltpu.roll(edge_in[16:24, cols[j]], SEGS - 1, 0)
        near, far = slice(rows - 8, rows), slice(rows - 16, rows - 8)
        gp_out[near, cols[j]] = gp_out[near, cols[j]] + jnp.where(last, c[1][j] * one + c[2][j] * three, 0.0)
        gp_out[far, cols[j]] = gp_out[far, cols[j]] + jnp.where(last, c[2][j] * two, 0.0)


class Links:
    def __init__(self, sends, recvs):
        self.sends, self.recvs, self.used, self.open = sends, recvs, 0, []
        self.x, self.y, self.c = lax.axis_index("x"), lax.axis_index("y"), lax.axis_index("c")
        self.zl, self.zh = lax.axis_index("zl"), lax.axis_index("zh")
        self.z = 2 * self.zh + self.zl

    def at_y(self, by):
        return lax.rem(self.y + by + 4, 4)

    def at_x(self, by):
        return lax.rem(self.x + by + 4, 4)

    def at_z(self, by):
        return lax.rem(self.z + by + 4, 4)

    def to_y(self, by):
        return {"y": self.at_y(by)}

    def to_x(self, by):
        return {"x": self.at_x(by)}

    def to_z(self, by):
        z = self.at_z(by)
        return {"zh": lax.div(z, 2), "zl": lax.rem(z, 2)}

    def sibling(self):
        return {"c": 1 - self.c}

    def send(self, src, dst, device):
        i = self.used
        self.used += 1
        copy = pltpu.make_async_remote_copy(
            src_ref=src,
            dst_ref=dst,
            send_sem=self.sends.at[i],
            recv_sem=self.recvs.at[i],
            device_id=device,
            device_id_type=pl.DeviceIdType.MESH,
        )
        copy.start()
        self.open.append(copy)
        return copy

    def local(self, src, dst):
        i = self.used
        self.used += 1
        copy = pltpu.make_async_copy(src, dst, self.sends.at[i])
        copy.start()
        return copy

    def greet(self, devices):
        barrier = pltpu.get_barrier_semaphore()
        for device in devices:
            pl.semaphore_signal(
                barrier, inc=1, device_id=device, device_id_type=pl.DeviceIdType.MESH
            )
        pl.semaphore_wait(barrier, len(devices))

    def settle(self):
        for copy in self.open:
            copy.wait_send()
        self.open = []


def arrived(copies):
    for copy in copies:
        copy.wait_recv()


def interleave(parts, order):
    for letter in order:
        next(parts[ord(letter) - ord("a")], None)
    finish(*parts)


def cut(count):
    upper = (count // 2 + 15) // 16 * 16
    return upper, count - upper


def owner_cols(y, c, b):
    return pl.ds(pl.multiple_of(b * 1024 + (2 * y + c) * LANES, LANES), LANES)


def gather_yc(links, src, dst, first=0, count=0):
    count = count or src.shape[0]
    top, low = cut(count)
    h0, h1 = pl.ds(first, top), pl.ds(first + top, low)
    full = pl.ds(first, count)

    def mine(part, b):
        return src.at[part, pl.ds(b * LANES, LANES)]

    def slot(y, c, part, b):
        return dst.at[part, owner_cols(y, c, b)]

    def push(y, part, device, own=False):
        c = links.c
        return [
            links.send(mine(part, b) if own else slot(y, c, part, b), slot(y, c, part, b), device)
            for b in range(2)
        ]

    y, up, down, far = links.y, links.at_y(1), links.at_y(-1), links.at_y(2)
    fwd, bwd, sib = links.to_y(1), links.to_y(-1), links.sibling()
    a0 = push(y, h0, fwd, True)
    b1 = push(y, h1, bwd, True)
    a1 = push(y, h1, fwd, True)
    b0 = push(y, h0, bwd, True)
    s = push(y, full, sib, True)
    keep = [links.local(mine(full, b), slot(y, links.c, full, b)) for b in range(2)]
    yield
    arrived(a0)
    f0 = push(down, h0, fwd)
    arrived(b1)
    f1 = push(up, h1, bwd)
    yield
    arrived(a1)
    s += push(down, full, sib)
    arrived(b0)
    s += push(up, full, sib)
    yield
    arrived(f0)
    s += push(far, h0, sib)
    arrived(f1)
    s += push(far, h1, sib)
    yield
    arrived(s)
    for copy in keep:
        copy.wait()


def fill(pairs, dst, place, cols):
    value = None
    for left, right in pairs:
        term = jnp.dot(left[place, :], right[:, cols], preferred_element_type=F32)
        value = term if value is None else value + term
    dst[place, cols] = value.astype(BF16)


def scatter_yc(links, pairs, out, src, sib_buf, half_buf, full_buf, begin=0, rows=0):
    rows = rows or src.shape[0]
    top, low = cut(rows)
    step = 64
    whole = pl.ds(begin, rows)
    order = [links.at_y(2), links.at_y(1), links.at_y(-1), links.y]
    fwd, bwd, sib = links.to_y(1), links.to_y(-1), links.sibling()
    mine, other = links.c, 1 - links.c
    got = []

    def produce(k):
        for b in range(2):
            fill(pairs, src, whole, pl.ds(pl.multiple_of(b * 1024 + order[k] * 256, 256), 256))
        got.append(
            [
                links.send(
                    src.at[whole, owner_cols(order[k], other, b)], sib_buf.at[k, whole, pl.ds(b * LANES, LANES)], sib
                )
                for b in range(2)
            ]
        )

    def total(k, place, b):
        lanes = slice(b * LANES, (b + 1) * LANES)
        return src[place, owner_cols(order[k], mine, b)].astype(F32) + sib_buf[k, place, lanes].astype(F32)

    def over(first, count, body):
        def run(i, _):
            body(pl.multiple_of(first + i * step, 16))
            return 0

        assert count % step == 0
        lax.fori_loop(0, count // step, run, 0)

    def put(k, first, count, more=None):
        def body(at):
            place = pl.ds(at, step)
            for b in range(2):
                lanes = slice(b * LANES, (b + 1) * LANES)
                value = total(k, place, b)
                if more is not None:
                    value = value + more[place, lanes].astype(F32)
                sib_buf[k, place, lanes] = value.astype(BF16)

        over(first, count, body)

    middle = begin + top
    t, l = pl.ds(begin, top), pl.ds(middle, low)
    produce(0)
    yield
    produce(1)
    arrived(got[0])
    put(0, begin, top)
    h0 = links.send(sib_buf.at[0, t, :], half_buf.at[t, :], fwd)
    put(0, middle, low)
    h1 = links.send(sib_buf.at[0, l, :], half_buf.at[l, :], bwd)
    yield
    produce(2)
    arrived(got[1])
    put(1, middle, low)
    p1 = links.send(sib_buf.at[1, l, :], full_buf.at[0, l, :], fwd)
    yield
    produce(3)
    arrived(got[2])
    put(2, begin, top)
    m1 = links.send(sib_buf.at[2, t, :], full_buf.at[1, t, :], bwd)
    yield
    h0.wait_recv()
    put(1, begin, top, half_buf)
    p0 = links.send(sib_buf.at[1, t, :], full_buf.at[0, t, :], fwd)
    h1.wait_recv()
    put(2, middle, low, half_buf)
    m0 = links.send(sib_buf.at[2, l, :], full_buf.at[1, l, :], bwd)
    yield
    arrived(got[3])
    arrived([p1, m1, p0, m0])

    def last(at):
        place = pl.ds(at, step)
        for b in range(2):
            lanes = slice(b * LANES, (b + 1) * LANES)
            out[place, lanes] = (
                total(3, place, b)
                + full_buf[0, place, lanes].astype(F32)
                + full_buf[1, place, lanes].astype(F32)
            )

    over(begin, rows, last)


def scatter_yc_scratch(rows):
    return [
        pltpu.VMEM((rows, 2048), BF16),
        pltpu.VMEM((4, rows, 256), BF16),
        pltpu.VMEM((rows, 256), BF16),
        pltpu.VMEM((2, rows, 256), BF16),
    ]


def yc_peers(links):
    return [
        {"y": links.at_y(dy), "c": lax.rem(links.c + dc, 2)}
        for dy in range(4)
        for dc in range(2)
        if (dy, dc) != (0, 0)
    ]


def sum_dots(links, src, out, buf):
    me = 2 * links.y + links.c
    copies = [links.send(src, buf.at[me], device) for device in yc_peers(links)]
    yield
    yield
    arrived(copies)
    total = src[...]
    for dy in range(4):
        for dc in range(2):
            if (dy, dc) != (0, 0):
                total = total + buf[2 * links.at_y(dy) + lax.rem(links.c + dc, 2)]
    out[...] = total


def xz_slot(dst, x, z, part):
    zh, zl = lax.div(z, 2), lax.rem(z, 2)
    rows = pl.ds(pl.multiple_of(zh * (dst.shape[0] // 2) + part.start, 16), part.size)
    return dst.at[rows, pl.ds(pl.multiple_of((2 * x + zl) * 256, 256), 256)]


AROUND = (2, 1, 3)


def xz_peers(links):
    return [links.to_x(by) for by in AROUND] + [links.to_z(by) for by in AROUND]


def gather_xz(links, src, dst, first=0):
    rows = src.shape[0]
    a, b = (first, rows - first) if first else cut(rows)
    keep = links.local(src, xz_slot(dst, links.x, links.z, pl.ds(0, rows)))
    upper, lower = pl.ds(0, a), pl.ds(a, b)

    def own(part, device):
        return links.send(src.at[part, :], xz_slot(dst, links.x, links.z, part), device)

    along_x = [(own(upper, links.to_x(by)), own(lower, links.to_x(by))) for by in AROUND]
    yield
    along_z = [(own(lower, links.to_z(by)), own(upper, links.to_z(by))) for by in AROUND]
    yield
    far = [pair[1] for pair in along_x + along_z]
    for by, (copy, _) in zip(AROUND, along_x):
        copy.wait_recv()
        piece = xz_slot(dst, links.at_x(-by), links.z, upper)
        far.extend(links.send(piece, piece, links.to_z(on)) for on in AROUND)
    for by, (copy, _) in zip(AROUND, along_z):
        copy.wait_recv()
        piece = xz_slot(dst, links.x, links.at_z(-by), lower)
        far.extend(links.send(piece, piece, links.to_x(on)) for on in AROUND)
    yield
    arrived(far)
    keep.wait()


def add_rows(count, terms, into):
    step = 16
    for size in (32, 48, 64, 80, 88, 96):
        if size % 16 == 0 and count % size == 0:
            step = size
    width = into[0].shape[-1]

    def pick(ref, first, lane, i):
        place = pl.ds(pl.multiple_of(first + i * step, 16), step)
        lanes = pl.ds(0 if lane is None else pl.multiple_of(lane, LANES), width)
        return place, lanes

    def body(i, _):
        value = None
        for ref, first, lane in terms:
            place, lanes = pick(ref, first, lane, i)
            term = ref[place, lanes].astype(F32)
            value = term if value is None else value + term
        ref, first, lane = into
        place, lanes = pick(ref, first, lane, i)
        ref[place, lanes] = value.astype(ref.dtype)
        return 0

    lax.fori_loop(0, count // step, body, 0)


def scatter_xz(links, src, out, near, near2):
    rows = out.shape[0]
    a, b = cut(rows)

    def by_xz(x, z):
        z = jnp.int32(z) if isinstance(z, int) else z
        return lax.div(z, 2), (2 * x + lax.rem(z, 2)) * 256

    halves = [
        (0, a, links.at_x, links.to_x, links.at_z, links.to_z, by_xz),
        (a, b, links.at_z, links.to_z, links.at_x, links.to_x, lambda z, x: by_xz(x, z)),
    ]
    came = []
    for which, (first, count, at1, to1, at2, to2, place_of) in enumerate(halves):
        copies = []
        for by in AROUND:
            for q in range(4):
                zh, lane = place_of(at1(by), q)
                part = src.at[
                    pl.ds(pl.multiple_of(zh * rows + first, 16), count), pl.ds(pl.multiple_of(lane, 256), 256)
                ]
                copies.append(links.send(part, near.at[which, by - 1, q, pl.ds(0, count), :], to1(by)))
        came.append(copies)
    yield
    last = []
    for which, (first, count, at1, to1, at2, to2, place_of) in enumerate(halves):
        arrived(came[which])
        for q in range(4):
            zh, lane = place_of(at1(0), q)
            add_rows(
                count,
                [(src, zh * rows + first, lane), *[(near.at[which, k, q], 0, None) for k in range(3)]],
                (near.at[which, 0, q], 0, None),
            )
        last.append(
            [
                links.send(
                    near.at[which, 0, at2(by), pl.ds(0, count), :], near2.at[which, by - 1, pl.ds(0, count), :], to2(by)
                )
                for by in AROUND
            ]
        )
    yield
    for which, (first, count, at1, to1, at2, to2, place_of) in enumerate(halves):
        arrived(last[which])
        add_rows(
            count,
            [(near.at[which, 0, at2(0)], 0, None), *[(near2.at[which, k], 0, None) for k in range(3)]],
            (out, first, None),
        )


def scatter_xz_scratch(rows):
    a, _ = cut(rows)
    return [pltpu.VMEM((2, 3, 4, a, 256), BF16), pltpu.VMEM((2, 3, a, 256), BF16)]


def scatter_grad(links, left, right, out, src, near, near2):
    rows = 2 * out.shape[0]
    for i in range(4):
        cols = slice(512 * i, 512 * (i + 1))
        value = lax.dot_general(
            left[...], right[:, cols], (((0,), (0,)), ((), ())), preferred_element_type=F32
        ).astype(BF16)
        src[0:rows, cols] = value
        yield
    yield from scatter_xz(links, src, out, near, near2)


def row_peers(links):
    peers = []
    for dx in range(4):
        for dz in range(4):
            if (dx, dz) != (0, 0):
                peers.append({"x": links.at_x(dx), **links.to_z(dz)})
    return peers


def block_of(links, dx, dz):
    z = links.at_z(dz)
    return links.at_x(dx) * 4 + lax.rem(z, 2) * 2 + lax.div(z, 2)


def exchange_rows(links, src, out):
    me = block_of(links, 0, 0)
    keep = links.local(src, out.at[me])
    copies = [links.send(src, out.at[me], device) for device in row_peers(links)]
    yield
    arrived(copies)
    keep.wait()


def sum_rows(links, src, out, buf):
    me = block_of(links, 0, 0)
    copies = []
    for dx in range(4):
        for dz in range(4):
            if (dx, dz) != (0, 0):
                device = {"x": links.at_x(dx), **links.to_z(dz)}
                lanes = pl.ds(pl.multiple_of(device["zh"] * LANES, LANES), LANES)
                copies.append(links.send(src.at[:, lanes], buf.at[me], device))
    yield
    arrived(copies)
    total = src[:, pl.ds(pl.multiple_of(links.zh * LANES, LANES), LANES)]
    for dx in range(4):
        for dz in range(4):
            if (dx, dz) != (0, 0):
                total = total + buf[block_of(links, dx, dz)]
    out[...] = total


def swap_pairs(links, ins, outs):
    lanes = pl.ds(pl.multiple_of(links.zh * LANES, LANES), LANES)
    keep, got = [], []
    for src, dst in zip(ins, outs):
        place = dst.at[pl.ds(0, src.shape[1]), lanes]
        got.append(links.send(src.at[1 - links.zh], place, links.to_z(2)))
    for src, dst in zip(ins, outs):
        place = dst.at[pl.ds(0, src.shape[1]), lanes]
        keep.append(links.local(src.at[links.zh], place))
    return got, keep


def unswap_pair(links, src, dst):
    mine = pl.ds(pl.multiple_of(links.zh * LANES, LANES), LANES)
    theirs = pl.ds(pl.multiple_of((1 - links.zh) * LANES, LANES), LANES)
    got = links.send(src.at[:, theirs], dst.at[links.zh], links.to_z(2))
    keep = links.local(src.at[:, mine], dst.at[links.zh])
    yield
    got.wait_recv()
    keep.wait()


def swap_only(links, src, dst):
    got, keep = swap_pairs(links, (src,), (dst,))
    for _ in range(4):
        yield
    arrived(got)
    for copy in keep:
        copy.wait()


def block_device(block):
    block = lax.rem(block + 16, 16)
    return {"x": lax.div(block, 4), "zl": lax.rem(lax.div(block, 2), 2), "zh": lax.rem(block, 2)}


def conv_backward(
    links, gg, u, q, z, k, v, p, halo, taps, m1, m2, ends, enter, free, dec, dec_seg, res, skip, rates, starts,
    gp, res_out, rate_out, skip_out, conv_out, edge, edge_in, back_ends, last, lasts, back_enter, kept, gq, gz,
):
    me = block_of(links, 0, 0)
    for b in range(2):
        back_first(b, gg, q, m1, free, dec, dec_seg, back_ends, last)
        if b == 0:
            yield
    going = exchange_rows(links, last, lasts)
    next(going)
    yield
    finish(going)
    total = jnp.zeros(last.shape, F32)
    for j in range(lasts.shape[0]):
        apart = (jnp.maximum(j - me - 1, 0) * p.shape[0]).astype(F32)
        after = (me < j).astype(F32)
        still = open_between(starts, (me + 1) * p.shape[0], j * p.shape[0])
        total = total + lasts[j] * (after * still * jnp.exp(-rates[...] * apart))
    back_enter[...] = total
    for b in range(2):
        for part in range(2):
            if (b, part) != (0, 0):
                keep_states(b, part, z, m1, ends, enter, free, dec, dec_seg, kept)
                yield
            back_poles(
                b, part, gg, u, q, z, m1, back_ends, back_enter, free, dec, dec_seg, res, skip,
                res_out, rate_out, skip_out, kept, gq, gz,
            )
            yield
        back_taps(b, v, k, p, halo, taps, m1, m2, gp, edge, conv_out, gq, gz)
        yield
    got = links.send(edge, edge_in, block_device(me - 1))
    yield
    got.wait_recv()
    for b in range(2):
        mend_edges(b, taps, edge_in, gp)


def shape(*dims, dtype=F32):
    return jax.ShapeDtypeStruct(dims, dtype)


def finish(*parts):
    for part in parts:
        for _ in part:
            pass


NT = (((1,), (1,)), ((), ()))


def open_between(starts, low, high):
    at = starts[...]
    hit = jnp.where((at >= low) & (at < high), 1.0, 0.0)
    return 1.0 - jnp.max(hit, axis=0, keepdims=True)


def write_masks(block, starts, m1, m2):
    rows = m1.shape[0]
    seg = rows // SEGS
    firsts = [jnp.broadcast_to(starts[j : j + 1, 0:LANES], (SEGS, LANES)) for j in range(DOCS)]
    base = block * rows + seg_rows() * seg

    def carries_on(place):
        hit = place == firsts[0]
        for first in firsts[1:]:
            hit = hit | (place == first)
        return jnp.where(hit, 0.0, 1.0)

    def step(i, earlier):
        one = carries_on(base + i)
        m1[tile(i), :] = one
        m2[tile(i), :] = one * earlier
        return one

    lax.fori_loop(0, seg, step, carries_on(base - 1))


def forward_half(
    links, tok, small, cot_pair, win_t, wout_t, wgate_t, starts, up_t, down,
    xg_out, win_out, wout_out, cs, p_out, q_out, z_out, k_out, v_out, xs_out, hg_out, wdown_out, hidden_out, gh_out,
    u, gated, halo, ends, free, enter, params, r1, m1, m2, acts, gg, gu, dots, r2, sum_down,
    xr, xs, sm, xg, gains, inv, inv_g2, win, p, q, z, k, v, dec, dec_seg, taps, res, skip, last, lasts,
    cot, wout, wgate, wup, wdown, own_dots, dots_buf, *held,
):
    rows, width = xg.shape
    poles = dec.shape[0]
    me = block_of(links, 0, 0)
    got, keep = swap_pairs(links, (small, tok), (sm, xr))
    win_in = gather_xz(links, win_t, win, win_t.shape[0] // 4)
    next(win_in)
    cot_swap = swap_only(links, cot_pair, cs)
    wout_in = gather_xz(links, wout_t, wout)
    wgate_in = gather_xz(links, wgate_t, wgate)
    write_masks(me, starts, m1, m2)
    arrived(got[:1])
    keep[0].wait()
    gain_rows = gather_yc(links, sm.at[pl.ds(0, 32), :], gains)
    next(gain_rows)
    values = sm[...].astype(F32)
    rate = jnp.exp(values[32:48])
    dec[...] = jnp.exp(-rate)
    dec_seg[...] = jnp.exp(-rate * (rows // SEGS))
    taps[...] = values[16:32]
    res[...] = values[48:64]
    skip[...] = jnp.broadcast_to(values[2:3], (SEGS, 2 * LANES))
    params[0:16, :] = values[0:16]
    params[16:32, :] = values[16:32]
    params[32:48, :] = rate
    params[48:64, :] = values[48:64]
    arrived(got[1:])
    keep[1].wait()

    def gained(i, _):
        place = pl.ds(pl.multiple_of(i * 64, 64), 64)
        xs[place, :] = (xr[place, :].astype(F32) * params[0:1, :]).astype(BF16)
        return 0

    lax.fori_loop(0, rows // 64, gained, 0)
    columns = gather_yc(links, xs, xg)
    next(columns)
    next(win_in)
    next(cot_swap)
    next(gain_rows)
    next(gain_rows)
    next(columns)
    next(win_in)
    next(columns)
    next(gain_rows)
    finish(columns)
    finish(gain_rows, win_in)
    inv[...] = 1.0 / gains[0:16, :].astype(F32)
    inv_g2[...] = inv[1:2, :]
    stores = [links.local(xg, xg_out), links.local(win, win_out), links.local(xr, xs_out)]
    step = 256

    def project(i, _):
        place = pl.ds(pl.multiple_of(i * step, step), step)
        r = rows_scale(xg, inv, place, width)
        r1[place, :] = jnp.broadcast_to(r, (step, LANES))
        p[place, :] = r * lax.dot_general(xg[place, :], win[...], NT, preferred_element_type=F32)
        return 0

    lax.fori_loop(0, rows // step, project, 0)
    stores.append(links.local(p, p_out))
    tail = links.send(p.at[pl.ds(rows - 16, 16), :], halo, block_device(me + 1))
    for part in (wgate_in, wout_in):
        next(part)
        next(part)
    finish(cot_swap)
    cot_in = gather_yc(links, cs, cot)
    next(cot_in)
    tail.wait_recv()
    for b in range(2):
        conv_first(b, p, halo, taps, m1, m2, dec, dec_seg, q, z, k, v, ends, free, last)
    going = exchange_rows(links, last, lasts)
    next(going)
    next(cot_in)
    next(wgate_in)
    next(wout_in)
    stores += [links.local(q, q_out), links.local(z, z_out), links.local(k, k_out), links.local(v, v_out)]
    finish(going)
    rates = params[32:48, :]
    total = jnp.zeros((poles, 2 * LANES), F32)
    for j in range(lasts.shape[0]):
        apart = (jnp.maximum(me - 1 - j, 0) * rows).astype(F32)
        before = (me > j).astype(F32)
        total = total + lasts[j] * (before * open_between(starts, (j + 1) * rows, me * rows) * jnp.exp(-rates * apart))
    enter[...] = total
    conv_second(0, q, z, m1, ends, free, enter, dec, dec_seg, res, skip, u, gated)
    next(cot_in)
    conv_second(1, q, z, m1, ends, free, enter, dec, dec_seg, res, skip, u, gated)
    finish(wout_in)
    for copy in stores:
        copy.wait()
    links.settle()
    one, two, held = held[:4], held[4:7], held[7:]
    mixer, hidden, gh = z, v, k
    beside = [gather_xz(links, up_t, wup, 128), gather_xz(links, down, wdown, 128)]
    for part in beside:
        next(part)
    steps = lambda part, count: [next(part, None) for _ in range(count)]
    sums = scatter_yc(links, [(gated, wout)], mixer, *one)
    steps(sums, 2)
    for part in beside:
        next(part)
    steps(sums, 3)
    for part in beside:
        next(part)
    finish(sums, cot_in)

    def residual(i, _):
        place = pl.ds(pl.multiple_of(i * 64, 64), 64)
        value = xr[place, :].astype(F32) + mixer[place, :]
        hidden[place, :] = value
        xs[place, :] = (value * params[1:2, :]).astype(BF16)
        return 0

    lax.fori_loop(0, rows // 64, residual, 0)
    finish(gather_yc(links, xs, xg), wgate_in, *beside)
    links.settle()
    kept = [links.local(wdown, wdown_out), links.local(xg, hg_out), links.local(wout, wout_out)]
    kept.append(links.local(hidden, hidden_out))
    step = 256

    def block(i, _):
        place = pl.ds(pl.multiple_of(i * step, step), step)
        r = rows_scale(xg, inv_g2, place, width)
        r2[place, :] = jnp.broadcast_to(r, (step, LANES))
        h = xg[place, :]
        gate = r * lax.dot_general(h, wgate[...], NT, preferred_element_type=F32)
        upper = r * lax.dot_general(h, wup[...], NT, preferred_element_type=F32)
        g_act = lax.dot_general(cot[place, :], wdown[...], NT, preferred_element_type=F32)
        sig = jax.nn.sigmoid(gate)
        acts[place, :] = (gate * sig * upper).astype(BF16)
        g_gate = g_act * upper * (sig * (1.0 + gate * (1.0 - sig)))
        g_upper = g_act * gate * sig
        gg[place, :] = (r * g_gate).astype(BF16)
        gu[place, :] = (r * g_upper).astype(BF16)
        both = (g_gate * gate + g_upper * upper).astype(BF16)
        own_dots[:, place] = lax.dot_general(
            jnp.ones((8, both.shape[1]), BF16), both, NT, preferred_element_type=F32
        )
        return 0

    lax.fori_loop(0, rows // step, block, 0)
    parts = [
        scatter_yc(links, [(gg, wgate), (gu, wup)], gh, one[0], *two),
        scatter_grad(links, acts, cot, sum_down, win, *held),
        sum_dots(links, own_dots, dots, dots_buf),
    ]
    interleave(parts, "bbbbbcaaaaabaa")
    kept.append(links.local(gh, gh_out))
    for copy in kept:
        copy.wait()


def rows_scale(x, gain, place, width):
    square = jnp.zeros((place.size, LANES), F32)
    for k in range(width // LANES):
        lanes = slice(LANES * k, LANES * (k + 1))
        plain = x[place, lanes].astype(F32) * gain[0:1, lanes]
        square = square + plain * plain
    return lax.rsqrt(jnp.sum(square, axis=1, keepdims=True) / width + EPS)


def dots_column(dots):
    line = lax.broadcasted_iota(jnp.int32, dots.shape, 0)
    value = dots[...]
    high = value.astype(BF16).astype(F32)
    pair = jnp.where(line == 0, high, jnp.where(line == 1, value - high, 0.0)).astype(BF16)
    return lax.dot_general(
        pair, jnp.ones((8, LANES), BF16), (((0,), (0,)), ((), ())), preferred_element_type=F32
    )


def mixer_back(
    links, gh_in, cs_in, r2_in, dots, params, wout, gated, acts, wdown, gg_low, gu_low, hg, hidden, u, q, z, k, v, p, halo, taps, m1, m2,
    ends, enter, free, dec, dec_seg, res, skip, rates, starts,
    g_hidden, gain2, gp, res_out, rate_out, skip_out, conv_out, mixed, sum_gate, sum_up, sum_out,
    g_mix, gg, mlp, mixed_half, edge, edge_in, back_ends, last, lasts, back_enter, kept, gq, gz, *held,
):
    rows = gg.shape[0]
    loads = [links.local(gh_in, mlp), links.local(cs_in, mixed_half), links.local(r2_in, gq)]
    for copy in loads:
        copy.wait()
    pull = gq[...] * gq[...] * dots_column(dots) / g_mix.shape[1]
    for b in range(2):
        lanes = lanes_of(b)
        back, h = mlp[:, lanes], hidden[:, lanes]
        value = mixed_half[:, lanes].astype(F32) + params[1:2, lanes] * back - h * pull
        gg[:, lanes] = value
        mixed_half[:, lanes] = value.astype(BF16)
        gain2[0:1, lanes] = jnp.sum(back * h, axis=0, keepdims=True)
    store = links.local(gg, g_hidden)
    columns = gather_yc(links, mixed_half, g_mix)
    gate = scatter_grad(links, gg_low, hg, sum_gate, *held[4:7])
    up = scatter_grad(links, gu_low, hg, sum_up, *held[7:10])
    out = scatter_grad(links, gated, g_mix, sum_out, *held[10:13])
    down = scatter_yc(links, [(acts, wdown)], mlp, *held[:4])
    steps = lambda part, count: [next(part, None) for _ in range(count)]
    steps(columns, 1)
    early, links.open = links.open, []
    steps(gate, 5)
    steps(columns, 1)
    steps(up, 5)
    steps(columns, 2)
    steps(down, 2)
    keep_states(0, 0, z, m1, ends, enter, free, dec, dec_seg, kept)
    finish(columns)
    store.wait()
    gg[...] = lax.dot_general(g_mix[...], wout[...], NT, preferred_element_type=F32)
    back = conv_backward(
        links, gg, u, q, z, k, v, p, halo, taps, m1, m2, ends, enter, free, dec, dec_seg, res, skip, rates, starts,
        gp, res_out, rate_out, skip_out, conv_out, edge, edge_in, back_ends, last, lasts, back_enter, kept, gq, gz,
    )
    steps(back, 2)
    steps(down, 2)
    steps(gate, 1)
    steps(up, 1)
    steps(back, 1)
    steps(down, 1)
    steps(out, 5)
    steps(back, 1)
    finish(gate)
    steps(back, 1)
    steps(down, 1)
    steps(out, 1)
    steps(back, 1)
    finish(up)
    steps(back, 1)
    finish(down)

    for copy in early:
        copy.wait_send()

    def mix(i, _):
        place = pl.ds(pl.multiple_of(i * 64, 64), 64)
        mixed_half[place, :] = (hidden[place, :] + mlp[place, :]).astype(BF16)
        return 0

    lax.fori_loop(0, rows // 64, mix, 0)
    swapped = unswap_pair(links, mixed_half, mixed)
    steps(swapped, 1)
    finish(back, out, swapped)


def input_back(
    links, gp, p, r1, xg, win, g_hidden, xs, g1, conv, rate_raw, res_raw, skip_raw, rate, res, gain2,
    sum_in, grad, tiny_out,
    gp_low, own_dots, dots, dots_buf, gx, grad_half, tiny, tiny_buf, *held,
):
    rows = gp.shape[0]
    width = xg.shape[1]
    step = 256

    def scale(i, _):
        place = pl.ds(pl.multiple_of(i * step, step), step)
        value = gp[place, :]
        both = (value * p[place, :]).astype(BF16)
        own_dots[:, place] = lax.dot_general(
            jnp.ones((8, both.shape[1]), BF16), both, NT, preferred_element_type=F32
        )
        gp_low[place, :] = (r1[place, 0:1] * value).astype(BF16)
        return 0

    lax.fori_loop(0, rows // step, scale, 0)
    parts = [
        scatter_yc(links, [(gp_low, win)], gx, *held[:4]),
        sum_dots(links, own_dots, dots, dots_buf),
        scatter_grad(links, gp_low, xg, sum_in, *held[4:]),
    ]
    for letter in "bcccccaaaaaca":
        next(parts[ord(letter) - ord("a")], None)
    finish(parts[0], parts[1])
    tiny[...] = jnp.zeros_like(tiny)
    pull = r1[...] * r1[...] * dots_column(dots) / width
    for b in range(2):
        lanes = lanes_of(b)
        x = xs[:, lanes].astype(F32)
        got = gx[:, lanes]
        grad_half[:, lanes] = (g_hidden[:, lanes] + g1[0:1, lanes] * got - x * pull).astype(BF16)
        tiny[0:1, lanes] = jnp.sum(got * x, axis=0, keepdims=True)
    tiny[1:2, :] = gain2[...]
    tiny[2:3, :] = jnp.sum(skip_raw[...], axis=0, keepdims=True)
    tiny[8:24, :] = conv[...]
    tiny[24:40, :] = -rate[...] * res[...] * rate_raw[...]
    tiny[40:56, :] = res_raw[...]
    swapped = unswap_pair(links, grad_half, grad)
    summed = sum_rows(links, tiny, tiny_out, tiny_buf)
    next(swapped)
    next(summed)
    finish(parts[2], summed, swapped)


def fused(number, maker, peers, inputs, outs, scratch, copies):
    vmem = pl.BlockSpec(memory_space=pltpu.VMEM)
    hbm = pl.BlockSpec(memory_space=pl.ANY)
    staged = [i for i, (_, kind) in enumerate(inputs) if kind == "s"]
    n_in, n_out = len(inputs), len(outs)

    def kernel(*refs):
        ins, results = list(refs[:n_in]), refs[n_in : n_in + n_out]
        held = refs[n_in + n_out : -2]
        links = Links(refs[-2], refs[-1])
        moves = []
        for i, buf in zip(staged, held):
            moves.append(links.local(ins[i], buf))
            ins[i] = buf
        met = []
        if "Y" in peers:
            met += yc_peers(links)
        elif "y" in peers:
            met += [links.to_y(1), links.to_y(-1), links.sibling()]
        if "r" in peers:
            met += row_peers(links)
        elif "x" in peers:
            met += xz_peers(links)
        links.greet(met)
        for move in moves:
            move.wait()
        maker(links, *ins, *results, *held[len(staged) :])
        links.settle()
        assert links.used <= copies

    return pl.pallas_call(
        kernel,
        in_specs=[vmem if kind == "v" else hbm for _, kind in inputs],
        out_specs=[vmem if kind == "v" else hbm for _, kind in outs],
        out_shape=[kept for kept, _ in outs],
        scratch_shapes=[
            *[pltpu.VMEM(inputs[i][0].shape, inputs[i][0].dtype) for i in staged],
            *scratch,
            pltpu.SemaphoreType.DMA((copies,)),
            pltpu.SemaphoreType.DMA((copies,)),
        ],
        compiler_params=pltpu.CompilerParams(
            collective_id=number, has_side_effects=True, vmem_limit_bytes=VMEM_LIMIT
        ),
    )(*[array for array, _ in inputs])


def grad_scratch(rows):
    return [pltpu.VMEM((2 * rows, 2048), BF16), *scatter_xz_scratch(rows)]


def shards(
    tokens, gain_first, gain_second, w_in, conv_w, log_rate, residue, skip,
    w_out, w_gate, w_up, w_down, cotangent, lengths,
):
    rows = tokens.shape[0] // 2
    width = 16 * LANES
    seg = rows // SEGS

    def stepped(value):
        return value.reshape(2, SEGS, seg, LANES).transpose(0, 2, 1, 3).reshape(2, rows, LANES)

    def unstepped(value):
        return value.reshape(2, seg, SEGS, LANES).transpose(0, 2, 1, 3).reshape(2 * rows, LANES)

    before = jnp.arange(DOCS)[:, None] < jnp.arange(DOCS)[None, :]
    starts = jnp.sum(jnp.where(before, lengths[:, None], 0), axis=0)
    starts = jnp.broadcast_to(starts[:, None], (DOCS, 2 * LANES))

    line = lax.broadcasted_iota(jnp.int32, (16, LANES), 0)
    singles = jnp.where(line == 0, gain_first, jnp.where(line == 1, gain_second, jnp.where(line == 2, skip, 0)))
    taps_own = jnp.pad(conv_w.reshape(9, LANES), ((0, 7), (0, 0)))
    small = jnp.concatenate([singles.astype(BF16), taps_own, log_rate, residue])
    hidden_units = w_gate.shape[1]
    half = (rows, 2 * LANES)
    weight = (2 * hidden_units, width)
    act = shape(*half)
    low = shape(*half, dtype=BF16)
    proj_shape = shape(rows, 6 * LANES)
    units = shape(rows, 2 * hidden_units, dtype=BF16)
    broad = shape(rows, width, dtype=BF16)
    sixteen = shape(16, 2 * LANES)
    vm = lambda kept: pltpu.VMEM(kept.shape, kept.dtype)
    (
        xg, win, wout, cs, proj, q, z, k, v, xs, hg, wdown, hidden, gh, u, gated, halo, seg_ends, free, enter, params,
        r1, mask1, mask2, acts, gg_low, gu_low, dot2, r2, sums_down,
    ) = fused(
        1,
        forward_half,
        "Yr",
        [
            (stepped(tokens), "h"), (jnp.broadcast_to(small[None], (2, 64, LANES)), "h"), (stepped(cotangent), "h"),
            (w_in.transpose(1, 2, 0).reshape(3 * LANES, 256), "h"), (w_out, "h"), (w_gate.T, "h"),
            (starts, "v"), (w_up.T, "h"), (w_down, "h"),
        ],
        [
            (broad, "h"), (shape(6 * LANES, width, dtype=BF16), "h"), (shape(2 * LANES, width, dtype=BF16), "h"),
            (low, "h"), (proj_shape, "h"), (act, "h"), (act, "h"), (act, "h"), (act, "h"), (low, "h"), (broad, "h"),
            (shape(*weight, dtype=BF16), "h"), (act, "h"), (act, "h"),
            (act, "v"), (low, "v"), (shape(16, 768), "v"), (shape(128, 256), "v"), (shape(8, 256), "v"),
            (sixteen, "v"), (shape(64, 256), "v"), (shape(rows, LANES), "v"), (shape(rows, LANES), "v"),
            (shape(rows, LANES), "v"), (units, "v"), (units, "v"), (units, "v"),
            (shape(8, rows), "v"), (shape(rows, LANES), "v"), (shape(hidden_units, 2 * LANES), "v"),
        ],
        [
            vm(low), vm(low), pltpu.VMEM((64, 256), BF16), vm(broad), pltpu.VMEM((32, width), BF16),
            pltpu.VMEM((16, width), F32), pltpu.VMEM((1, width), F32), pltpu.VMEM((6 * LANES, width), BF16),
            vm(proj_shape), *([vm(act)] * 4), vm(sixteen), vm(sixteen), vm(sixteen), vm(sixteen),
            pltpu.VMEM((8, 256), F32), vm(sixteen), pltpu.VMEM((16, 16, 256), F32),
            vm(broad), pltpu.VMEM((2 * LANES, width), BF16), *([pltpu.VMEM(weight, BF16)] * 3),
            pltpu.VMEM((8, rows), F32), pltpu.VMEM((8, 8, rows), F32),
            *scatter_yc_scratch(rows), *scatter_yc_scratch(rows)[1:], *scatter_xz_scratch(hidden_units),
        ],
        400,
    )
    g1 = params[0:1]
    skip8 = jnp.broadcast_to(params[2:3], (8, 2 * LANES))
    taps, rate, res = params[16:32], params[32:48], params[48:64]
    dec = jnp.exp(-rate)
    dec_seg = jnp.exp(-rate * seg)

    g_hidden, grad_gain2, g_proj, res_raw, rate_raw, skip_raw, conv_raw, mixed, sums_gate, sums_up, sums_out = fused(
        4,
        mixer_back,
        "yr",
        [
            (gh, "h"), (cs, "h"), (r2, "h"), (dot2, "v"), (params, "v"), (wout, "s"), (gated, "s"), (acts, "s"), (wdown, "s"), (gg_low, "s"),
            (gu_low, "s"), (hg, "s"), (hidden, "s"), (u, "s"), (q, "s"), (z, "s"), (k, "s"), (v, "s"), (proj, "s"),
            (halo, "v"), (taps, "v"), (mask1, "s"), (mask2, "s"), (seg_ends, "v"), (enter, "v"), (free, "v"),
            (dec, "v"), (dec_seg, "v"), (res, "v"), (skip8, "v"), (rate, "v"), (starts, "v"),
        ],
        [
            (act, "h"), (shape(1, 2 * LANES), "v"), (proj_shape, "v"), (sixteen, "v"), (sixteen, "v"), (shape(8, 2 * LANES), "v"), (sixteen, "v"),
            (shape(2, rows, LANES, dtype=BF16), "h"), *[(shape(hidden_units, 2 * LANES), "v")] * 2,
            (shape(LANES, 2 * LANES), "v"),
        ],
        [
            pltpu.VMEM((rows, width), BF16), pltpu.VMEM(half, F32), pltpu.VMEM(half, F32), pltpu.VMEM(half, BF16),
            pltpu.VMEM((24, 6 * LANES), F32), pltpu.VMEM((24, 6 * LANES), F32), pltpu.VMEM((128, 256), F32),
            pltpu.VMEM((16, 256), F32), pltpu.VMEM((16, 16, 256), F32), pltpu.VMEM((16, 256), F32),
            pltpu.VMEM((seg, 8, SEGS, LANES), F32), pltpu.VMEM((rows, LANES), F32), pltpu.VMEM((rows, LANES), F32),
            *scatter_yc_scratch(rows), *(grad_scratch(hidden_units) * 2), *grad_scratch(LANES),
        ],
        220,
    )
    sums_in, grad_tok, tiny = fused(
        5,
        input_back,
        "Yr",
        [
            (g_proj, "s"), (proj, "s"), (r1, "s"), (xg, "s"), (win, "s"), (g_hidden, "s"), (xs, "s"), (g1, "v"),
            (conv_raw, "v"), (rate_raw, "v"), (res_raw, "v"), (skip_raw, "v"), (rate, "v"), (res, "v"),
            (grad_gain2, "v"),
        ],
        [
            (shape(3 * LANES, 2 * LANES), "v"), (shape(2, rows, LANES, dtype=BF16), "h"), (shape(56, LANES), "v"),
        ],
        [
            pltpu.VMEM((rows, 6 * LANES), BF16), pltpu.VMEM((8, rows), F32), pltpu.VMEM((8, rows), F32),
            pltpu.VMEM((8, 8, rows), F32), pltpu.VMEM(half, F32), pltpu.VMEM(half, BF16), pltpu.VMEM((56, 256), F32),
            pltpu.VMEM((16, 56, LANES), F32), *scatter_yc_scratch(rows), *grad_scratch(3 * LANES),
        ],
        120,
    )
    return (
        unstepped(mixed),
        unstepped(grad_tok).astype(F32),
        tiny[0],
        tiny[1],
        sums_in.reshape(3, LANES, 256).transpose(2, 0, 1),
        tiny[8:17].reshape(3, 3, LANES),
        tiny[24:40],
        tiny[40:56],
        tiny[2],
        sums_out,
        sums_gate.T,
        sums_up.T,
        sums_down,
    )


def solution(mesh):
    cube = Mesh(mesh.devices.reshape(4, 2, 2, 4, 2), ("x", "zl", "zh", "y", "c"))
    seq, tp = ("x", "zl"), ("zh", "y", "c")
    return jax.shard_map(
        shards,
        mesh=cube,
        in_specs=(
            P(seq, tp), P(tp), P(tp), P(seq, None, tp), P(None, None, tp), P(None, tp), P(None, tp), P(tp),
            P(tp, seq), P(seq, tp), P(seq, tp), P(tp, seq), P(seq, tp), P(),
        ),
        out_specs=(
            P(seq, tp), P(seq, tp), P(tp), P(tp), P(seq, None, tp), P(None, None, tp), P(None, tp), P(None, tp), P(tp),
            P(tp, seq), P(seq, tp), P(seq, tp), P(tp, seq),
        ),
        check_vma=False,
    )
```

```python
import functools

import jax
import jax.numpy as jnp
from jax import lax
from jax.experimental import pallas as pl
from jax.experimental.pallas import tpu as pltpu
from jax.sharding import Mesh
from jax.sharding import PartitionSpec as P

EPS = 1e-06
DOCS = 8
ROW_AXES = ("x", "zl", "zh")
COL_AXES = ("y", "c")
F32 = jnp.float32
BF16 = jnp.bfloat16
VMEM_LIMIT = 61900 * 1024
SEGS = 8
LANES = 128


def spread(row):
    return jnp.broadcast_to(row, (SEGS, LANES))


def seg_rows():
    return lax.broadcasted_iota(jnp.int32, (SEGS, LANES), 0)


def tile(i):
    return pl.ds(pl.multiple_of(i * SEGS, SEGS), SEGS)


def lanes_of(b, j=0):
    return slice(LANES * (b + j), LANES * (b + j + 1))


def add_all(terms):
    while len(terms) > 1:
        terms = [sum(terms[i + 1 : i + 2], terms[i]) for i in range(0, len(terms), 2)]
    return terms[0]


def scan_up(ends, factor):
    rows = seg_rows()
    for by in (1, 2, 4):
        held = rows >= by
        ends = ends + factor * jnp.where(held, pltpu.roll(ends, by, 0), 0.0)
        factor = factor * jnp.where(held, pltpu.roll(factor, by, 0), 1.0)
    return ends


def scan_down(ends, factor):
    rows = seg_rows()
    for by in (1, 2, 4):
        held = rows < SEGS - by
        ends = ends + factor * jnp.where(held, pltpu.roll(ends, SEGS - by, 0), 0.0)
        factor = factor * jnp.where(held, pltpu.roll(factor, SEGS - by, 0), 1.0)
    return ends


def entering_up(ends, factor, enter):
    first = seg_rows() == 0
    whole = scan_up(ends + jnp.where(first, factor * enter, 0.0), factor)
    return jnp.where(first, enter, pltpu.roll(whole, 1, 0))


def entering_down(ends, factor, enter):
    last = seg_rows() == SEGS - 1
    whole = scan_down(ends + jnp.where(last, factor * enter, 0.0), factor)
    return jnp.where(last, enter, pltpu.roll(whole, SEGS - 1, 0))


def rows_of(ref, count, lanes):
    return [spread(ref[n : n + 1, lanes]) for n in range(count)]


def tap_rows(taps, lanes):
    return [[spread(taps[3 * i + j : 3 * i + j + 1, lanes]) for j in range(3)] for i in range(3)]


def conv_first(b, p, halo, taps, m1, m2, dec, dec_seg, q_out, z_out, k_out, v_out, ends_out, open_out, last_out):
    seg = p.shape[0] // SEGS
    poles = dec.shape[0]
    own = lanes_of(b)
    cols = [lanes_of(3 * b, j) for j in range(3)]
    first = seg_rows() == 0
    d = rows_of(dec, poles, own)
    c = tap_rows(taps, own)

    def before(j, back):
        mine = pltpu.roll(p[SEGS * (seg - back) : SEGS * (seg - back + 1), cols[j]], 1, 0)
        theirs = pltpu.roll(halo[SEGS * (2 - back) : SEGS * (3 - back), cols[j]], 1, 0)
        return jnp.where(first, theirs, mine)

    def step(i, carry):
        state, prev1, prev2, free = carry
        place = tile(i)
        one, two = m1[place, :], m2[place, :]
        cur = [p[place, cols[j]] for j in range(3)]
        q, k, v = [
            c[0][j] * cur[j] + c[1][j] * (one * prev1[j]) + c[2][j] * (two * prev2[j])
            for j in range(3)
        ]
        z = k * v
        q_out[place, own] = q
        k_out[place, own] = k
        v_out[place, own] = v
        z_out[place, own] = z
        state = [d[n] * (one * state[n]) + z for n in range(poles)]
        return (state, cur, prev1, free * one)

    zero = jnp.zeros((SEGS, LANES), F32)
    start = (
        [zero] * poles,
        [before(j, 1) for j in range(3)],
        [before(j, 2) for j in range(3)],
        zero + 1.0,
    )
    state, _, _, free = lax.fori_loop(0, seg, step, start)
    open_out[:, own] = free
    for n in range(poles):
        ends_out[SEGS * n : SEGS * (n + 1), own] = state[n]
        whole = scan_up(state[n], spread(dec_seg[n : n + 1, own]) * free)
        last_out[n : n + 1, own] = whole[SEGS - 1 :, :]


def conv_second(b, q_in, z_in, m1, ends, free, enter, dec, dec_seg, res, skip, u_out, gated_out):
    rows = q_in.shape[0]
    seg = rows // SEGS
    poles = dec.shape[0]
    own = lanes_of(b)
    d = rows_of(dec, poles, own)
    r = rows_of(res, poles, own)
    sk = spread(skip[0:1, own])
    start = [
        entering_up(
            ends[SEGS * n : SEGS * (n + 1), own],
            spread(dec_seg[n : n + 1, own]) * free[:, own],
            spread(enter[n : n + 1, own]),
        )
        for n in range(poles)
    ]

    def step(i, state):
        place = tile(i)
        one, z = m1[place, :], z_in[place, own]
        state = [d[n] * (one * state[n]) + z for n in range(poles)]
        u_out[place, own] = add_all([r[n] * state[n] for n in range(poles)] + [sk * z])
        return state

    lax.fori_loop(0, seg, step, start)

    def rounded(i, _):
        place = pl.ds(pl.multiple_of(i * 64, 64), 64)
        gated_out[place, own] = (q_in[place, own] * u_out[place, own]).astype(BF16)
        return 0

    lax.fori_loop(0, rows // 64, rounded, 0)


def back_first(b, gg_in, q_in, m1, free, dec, dec_seg, ends_out, last_out):
    seg = q_in.shape[0] // SEGS
    poles = dec.shape[0]
    own = lanes_of(b)
    d = rows_of(dec, poles, own)

    def step(t, carry):
        place = tile(seg - 1 - t)
        gu = gg_in[place, own] * q_in[place, own]
        one = m1[place, :]
        return [d[n] * (one * (carry[n] + gu)) for n in range(poles)]

    zero = jnp.zeros((SEGS, LANES), F32)
    carry = lax.fori_loop(0, seg, step, [zero] * poles)
    for n in range(poles):
        ends_out[SEGS * n : SEGS * (n + 1), own] = carry[n]
        whole = scan_down(carry[n], spread(dec_seg[n : n + 1, own]) * free[:, own])
        last_out[n : n + 1, own] = whole[:1, :]


def keep_states(b, part, z_in, m1, ends, enter, free, dec, dec_seg, kept):
    seg = z_in.shape[0] // SEGS
    half = dec.shape[0] // 2
    own = lanes_of(b)
    these = range(half * part, half * (part + 1))
    d = [spread(dec[n : n + 1, own]) for n in these]
    start = [
        entering_up(
            ends[SEGS * n : SEGS * (n + 1), own],
            spread(dec_seg[n : n + 1, own]) * free[:, own],
            spread(enter[n : n + 1, own]),
        )
        for n in these
    ]

    def forward(i, state):
        place = tile(i)
        one, z = m1[place, :], z_in[place, own]
        state = [d[n] * (one * state[n]) + z for n in range(half)]
        for n in range(half):
            kept[i, n] = state[n]
        return state

    lax.fori_loop(0, seg, forward, start)


def back_poles(
    b, part, gg_in, u_in, q_in, z_in, m1, back_ends, back_enter, free, dec, dec_seg, res, skip,
    res_out, rate_out, skip_out, kept, gq, gz,
):
    seg = q_in.shape[0] // SEGS
    half = dec.shape[0] // 2
    own = lanes_of(b)
    zero = jnp.zeros((SEGS, LANES), F32)
    sk = spread(skip[0:1, own])
    these = range(half * part, half * (part + 1))
    d = [spread(dec[n : n + 1, own]) for n in these]
    r = [spread(res[n : n + 1, own]) for n in these]
    carry = [
        entering_down(
            back_ends[SEGS * n : SEGS * (n + 1), own],
            spread(dec_seg[n : n + 1, own]) * free[:, own],
            spread(back_enter[n : n + 1, own]),
        )
        for n in these
    ]

    def backward(t, held):
        carry, by_res, by_rate, by_skip = held
        i = seg - 1 - t
        place = tile(i)
        gg, one = gg_in[place, own], m1[place, :]
        gu = gg * q_in[place, own]
        s = [kept[i, n] for n in range(half)]
        lam = [carry[n] + gu for n in range(half)]
        terms = [r[n] * lam[n] for n in range(half)]
        if part == 0:
            terms.append(sk * gu)
            by_skip = by_skip + gu * z_in[place, own]
            gq[place, :] = gg * u_in[place, own]
        else:
            terms.append(gz[place, :])
        gz[place, :] = add_all(terms)
        by_res = [by_res[n] + gu * s[n] for n in range(half)]
        by_rate = [by_rate[n] + carry[n] * s[n] for n in range(half)]
        carry = [d[n] * (one * lam[n]) for n in range(half)]
        return (carry, by_res, by_rate, by_skip)

    _, by_res, by_rate, by_skip = lax.fori_loop(
        0, seg, backward, (carry, [zero] * half, [zero] * half, zero)
    )
    for k, n in enumerate(these):
        res_out[n : n + 1, own] = jnp.sum(by_res[k], axis=0, keepdims=True)
        rate_out[n : n + 1, own] = jnp.sum(by_rate[k], axis=0, keepdims=True)
    if part == 0:
        skip_out[:, own] = by_skip


def back_taps(b, v_in, k_in, p, halo, taps, m1, m2, gp_out, edge_out, conv_out, gq, gz):
    seg = p.shape[0] // SEGS
    own = lanes_of(b)
    cols = [lanes_of(3 * b, j) for j in range(3)]
    zero = jnp.zeros((SEGS, LANES), F32)
    c = tap_rows(taps, own)
    last = seg_rows() == SEGS - 1

    def short_grads(place):
        g = gz[place, :]
        return [gq[place, :], g * v_in[place, own], g * k_in[place, own]]

    def next_seg(value):
        return jnp.where(last, 0.0, pltpu.roll(value, SEGS - 1, 0))

    g0, g1 = short_grads(tile(0)), short_grads(tile(1))
    a1 = [m1[tile(0), :] * g for g in g0]
    b1 = [m2[tile(0), :] * g for g in g0]
    b2 = [m2[tile(1), :] * g for g in g1]
    for j in range(3):
        edge_out[0:8, cols[j]] = a1[j]
        edge_out[8:16, cols[j]] = b1[j]
        edge_out[16:24, cols[j]] = b2[j]

    def taps_back(t, held):
        late1, late2, later2, sums = held
        place = tile(seg - 1 - t)
        one, two = m1[place, :], m2[place, :]
        g = short_grads(place)
        new = []
        for j in range(3):
            value = p[place, cols[j]]
            gp_out[place, cols[j]] = c[0][j] * g[j] + c[1][j] * late1[j] + c[2][j] * later2[j]
            new += [
                sums[3 * j] + g[j] * value,
                sums[3 * j + 1] + late1[j] * value,
                sums[3 * j + 2] + later2[j] * value,
            ]
        return ([one * x for x in g], [two * x for x in g], late2, new)

    start = (
        [next_seg(x) for x in a1],
        [next_seg(x) for x in b1],
        [next_seg(x) for x in b2],
        [zero] * 9,
    )
    _, _, _, sums = lax.fori_loop(0, seg, taps_back, start)
    for j in range(3):
        old1, old2 = halo[15:16, cols[j]], halo[7:8, cols[j]]
        conv_out[j : j + 1, own] = jnp.sum(sums[3 * j], axis=0, keepdims=True)
        conv_out[3 + j : 4 + j, own] = jnp.sum(sums[3 * j + 1], axis=0, keepdims=True) + a1[j][:1] * old1
        conv_out[6 + j : 7 + j, own] = (
            jnp.sum(sums[3 * j + 2], axis=0, keepdims=True) + b1[j][:1] * old2 + b2[j][:1] * old1
        )


def mend_edges(b, taps, edge_in, gp_out):
    rows = gp_out.shape[0]
    own = lanes_of(b)
    cols = [lanes_of(3 * b, j) for j in range(3)]
    c = tap_rows(taps, own)
    last = seg_rows() == SEGS - 1
    for j in range(3):
        one = pltpu.roll(edge_in[0:8, cols[j]], SEGS - 1, 0)
        two = pltpu.roll(edge_in[8:16, cols[j]], SEGS - 1, 0)
        three = pltpu.roll(edge_in[16:24, cols[j]], SEGS - 1, 0)
        near, far = slice(rows - 8, rows), slice(rows - 16, rows - 8)
        gp_out[near, cols[j]] = gp_out[near, cols[j]] + jnp.where(last, c[1][j] * one + c[2][j] * three, 0.0)
        gp_out[far, cols[j]] = gp_out[far, cols[j]] + jnp.where(last, c[2][j] * two, 0.0)


class Links:
    def __init__(self, sends, recvs):
        self.sends, self.recvs, self.used, self.open = sends, recvs, 0, []
        self.x, self.y, self.c = lax.axis_index("x"), lax.axis_index("y"), lax.axis_index("c")
        self.zl, self.zh = lax.axis_index("zl"), lax.axis_index("zh")
        self.z = 2 * self.zh + self.zl

    def at_y(self, by):
        return lax.rem(self.y + by + 4, 4)

    def at_x(self, by):
        return lax.rem(self.x + by + 4, 4)

    def at_z(self, by):
        return lax.rem(self.z + by + 4, 4)

    def to_y(self, by):
        return {"y": self.at_y(by)}

    def to_x(self, by):
        return {"x": self.at_x(by)}

    def to_z(self, by):
        z = self.at_z(by)
        return {"zh": lax.div(z, 2), "zl": lax.rem(z, 2)}

    def sibling(self):
        return {"c": 1 - self.c}

    def send(self, src, dst, device):
        i = self.used
        self.used += 1
        copy = pltpu.make_async_remote_copy(
            src_ref=src,
            dst_ref=dst,
            send_sem=self.sends.at[i],
            recv_sem=self.recvs.at[i],
            device_id=device,
            device_id_type=pl.DeviceIdType.MESH,
        )
        copy.start()
        self.open.append(copy)
        return copy

    def local(self, src, dst):
        i = self.used
        self.used += 1
        copy = pltpu.make_async_copy(src, dst, self.sends.at[i])
        copy.start()
        return copy

    def greet(self, devices):
        barrier = pltpu.get_barrier_semaphore()
        for device in devices:
            pl.semaphore_signal(
                barrier, inc=1, device_id=device, device_id_type=pl.DeviceIdType.MESH
            )
        pl.semaphore_wait(barrier, len(devices))

    def settle(self):
        for copy in self.open:
            copy.wait_send()
        self.open = []


def arrived(copies):
    for copy in copies:
        copy.wait_recv()


def interleave(parts, order):
    for letter in order:
        next(parts[ord(letter) - ord("a")], None)
    finish(*parts)


def cut(count):
    upper = (count // 2 + 15) // 16 * 16
    return upper, count - upper


def owner_cols(y, c, b):
    return pl.ds(pl.multiple_of(b * 1024 + (2 * y + c) * LANES, LANES), LANES)


def gather_yc(links, src, dst, first=0, count=0):
    count = count or src.shape[0]
    top, low = cut(count)
    h0, h1 = pl.ds(first, top), pl.ds(first + top, low)
    full = pl.ds(first, count)

    def mine(part, b):
        return src.at[part, pl.ds(b * LANES, LANES)]

    def slot(y, c, part, b):
        return dst.at[part, owner_cols(y, c, b)]

    def push(y, part, device, own=False):
        c = links.c
        return [
            links.send(mine(part, b) if own else slot(y, c, part, b), slot(y, c, part, b), device)
            for b in range(2)
        ]

    y, up, down, far = links.y, links.at_y(1), links.at_y(-1), links.at_y(2)
    fwd, bwd, sib = links.to_y(1), links.to_y(-1), links.sibling()
    a0 = push(y, h0, fwd, True)
    b1 = push(y, h1, bwd, True)
    a1 = push(y, h1, fwd, True)
    b0 = push(y, h0, bwd, True)
    s = push(y, full, sib, True)
    keep = [links.local(mine(full, b), slot(y, links.c, full, b)) for b in range(2)]
    yield
    arrived(a0)
    f0 = push(down, h0, fwd)
    arrived(b1)
    f1 = push(up, h1, bwd)
    yield
    arrived(a1)
    s += push(down, full, sib)
    arrived(b0)
    s += push(up, full, sib)
    yield
    arrived(f0)
    s += push(far, h0, sib)
    arrived(f1)
    s += push(far, h1, sib)
    yield
    arrived(s)
    for copy in keep:
        copy.wait()


def fill(pairs, dst, place, cols):
    value = None
    for left, right in pairs:
        term = jnp.dot(left[place, :], right[:, cols], preferred_element_type=F32)
        value = term if value is None else value + term
    dst[place, cols] = value.astype(BF16)


def scatter_yc(links, pairs, out, src, sib_buf, half_buf, full_buf, begin=0, rows=0):
    rows = rows or src.shape[0]
    top, low = cut(rows)
    step = 64
    whole = pl.ds(begin, rows)
    order = [links.at_y(2), links.at_y(1), links.at_y(-1), links.y]
    fwd, bwd, sib = links.to_y(1), links.to_y(-1), links.sibling()
    mine, other = links.c, 1 - links.c
    got = []

    def produce(k):
        for b in range(2):
            fill(pairs, src, whole, pl.ds(pl.multiple_of(b * 1024 + order[k] * 256, 256), 256))
        got.append(
            [
                links.send(
                    src.at[whole, owner_cols(order[k], other, b)], sib_buf.at[k, whole, pl.ds(b * LANES, LANES)], sib
                )
                for b in range(2)
            ]
        )

    def total(k, place, b):
        lanes = slice(b * LANES, (b + 1) * LANES)
        return src[place, owner_cols(order[k], mine, b)].astype(F32) + sib_buf[k, place, lanes].astype(F32)

    def over(first, count, body):
        def run(i, _):
            body(pl.multiple_of(first + i * step, 16))
            return 0

        assert count % step == 0
        lax.fori_loop(0, count // step, run, 0)

    def put(k, first, count, more=None):
        def body(at):
            place = pl.ds(at, step)
            for b in range(2):
                lanes = slice(b * LANES, (b + 1) * LANES)
                value = total(k, place, b)
                if more is not None:
                    value = value + more[place, lanes].astype(F32)
                sib_buf[k, place, lanes] = value.astype(BF16)

        over(first, count, body)

    middle = begin + top
    t, l = pl.ds(begin, top), pl.ds(middle, low)
    produce(0)
    yield
    produce(1)
    arrived(got[0])
    put(0, begin, top)
    h0 = links.send(sib_buf.at[0, t, :], half_buf.at[t, :], fwd)
    put(0, middle, low)
    h1 = links.send(sib_buf.at[0, l, :], half_buf.at[l, :], bwd)
    yield
    produce(2)
    arrived(got[1])
    put(1, middle, low)
    p1 = links.send(sib_buf.at[1, l, :], full_buf.at[0, l, :], fwd)
    yield
    produce(3)
    arrived(got[2])
    put(2, begin, top)
    m1 = links.send(sib_buf.at[2, t, :], full_buf.at[1, t, :], bwd)
    yield
    h0.wait_recv()
    put(1, begin, top, half_buf)
    p0 = links.send(sib_buf.at[1, t, :], full_buf.at[0, t, :], fwd)
    h1.wait_recv()
    put(2, middle, low, half_buf)
    m0 = links.send(sib_buf.at[2, l, :], full_buf.at[1, l, :], bwd)
    yield
    arrived(got[3])
    arrived([p1, m1, p0, m0])

    def last(at):
        place = pl.ds(at, step)
        for b in range(2):
            lanes = slice(b * LANES, (b + 1) * LANES)
            out[place, lanes] = (
                total(3, place, b)
                + full_buf[0, place, lanes].astype(F32)
                + full_buf[1, place, lanes].astype(F32)
            )

    over(begin, rows, last)


def scatter_yc_scratch(rows):
    return [
        pltpu.VMEM((rows, 2048), BF16),
        pltpu.VMEM((4, rows, 256), BF16),
        pltpu.VMEM((rows, 256), BF16),
        pltpu.VMEM((2, rows, 256), BF16),
    ]


def yc_peers(links):
    return [
        {"y": links.at_y(dy), "c": lax.rem(links.c + dc, 2)}
        for dy in range(4)
        for dc in range(2)
        if (dy, dc) != (0, 0)
    ]


def sum_dots(links, src, out, buf):
    me = 2 * links.y + links.c
    copies = [links.send(src, buf.at[me], device) for device in yc_peers(links)]
    yield
    yield
    arrived(copies)
    total = src[...]
    for dy in range(4):
        for dc in range(2):
            if (dy, dc) != (0, 0):
                total = total + buf[2 * links.at_y(dy) + lax.rem(links.c + dc, 2)]
    out[...] = total


def xz_slot(dst, x, z, part):
    zh, zl = lax.div(z, 2), lax.rem(z, 2)
    rows = pl.ds(pl.multiple_of(zh * (dst.shape[0] // 2) + part.start, 16), part.size)
    return dst.at[rows, pl.ds(pl.multiple_of((2 * x + zl) * 256, 256), 256)]


AROUND = (2, 1, 3)


def xz_peers(links):
    return [links.to_x(by) for by in AROUND] + [links.to_z(by) for by in AROUND]


def gather_xz(links, src, dst, first=0):
    rows = src.shape[0]
    a, b = (first, rows - first) if first else cut(rows)
    keep = links.local(src, xz_slot(dst, links.x, links.z, pl.ds(0, rows)))
    upper, lower = pl.ds(0, a), pl.ds(a, b)

    def own(part, device):
        return links.send(src.at[part, :], xz_slot(dst, links.x, links.z, part), device)

    along_x = [(own(upper, links.to_x(by)), own(lower, links.to_x(by))) for by in AROUND]
    yield
    along_z = [(own(lower, links.to_z(by)), own(upper, links.to_z(by))) for by in AROUND]
    yield
    far = [pair[1] for pair in along_x + along_z]
    for by, (copy, _) in zip(AROUND, along_x):
        copy.wait_recv()
        piece = xz_slot(dst, links.at_x(-by), links.z, upper)
        far.extend(links.send(piece, piece, links.to_z(on)) for on in AROUND)
    for by, (copy, _) in zip(AROUND, along_z):
        copy.wait_recv()
        piece = xz_slot(dst, links.x, links.at_z(-by), lower)
        far.extend(links.send(piece, piece, links.to_x(on)) for on in AROUND)
    yield
    arrived(far)
    keep.wait()


def add_rows(count, terms, into):
    step = 16
    for size in (32, 48, 64, 80, 88, 96):
        if size % 16 == 0 and count % size == 0:
            step = size
    width = into[0].shape[-1]

    def pick(ref, first, lane, i):
        place = pl.ds(pl.multiple_of(first + i * step, 16), step)
        lanes = pl.ds(0 if lane is None else pl.multiple_of(lane, LANES), width)
        return place, lanes

    def body(i, _):
        value = None
        for ref, first, lane in terms:
            place, lanes = pick(ref, first, lane, i)
            term = ref[place, lanes].astype(F32)
            value = term if value is None else value + term
        ref, first, lane = into
        place, lanes = pick(ref, first, lane, i)
        ref[place, lanes] = value.astype(ref.dtype)
        return 0

    lax.fori_loop(0, count // step, body, 0)


def scatter_xz(links, src, out, near, near2):
    rows = out.shape[0]
    a, b = cut(rows)

    def by_xz(x, z):
        z = jnp.int32(z) if isinstance(z, int) else z
        return lax.div(z, 2), (2 * x + lax.rem(z, 2)) * 256

    halves = [
        (0, a, links.at_x, links.to_x, links.at_z, links.to_z, by_xz),
        (a, b, links.at_z, links.to_z, links.at_x, links.to_x, lambda z, x: by_xz(x, z)),
    ]
    came = []
    for which, (first, count, at1, to1, at2, to2, place_of) in enumerate(halves):
        copies = []
        for by in AROUND:
            for q in range(4):
                zh, lane = place_of(at1(by), q)
                part = src.at[
                    pl.ds(pl.multiple_of(zh * rows + first, 16), count), pl.ds(pl.multiple_of(lane, 256), 256)
                ]
                copies.append(links.send(part, near.at[which, by - 1, q, pl.ds(0, count), :], to1(by)))
        came.append(copies)
    yield
    last = []
    for which, (first, count, at1, to1, at2, to2, place_of) in enumerate(halves):
        arrived(came[which])
        for q in range(4):
            zh, lane = place_of(at1(0), q)
            add_rows(
                count,
                [(src, zh * rows + first, lane), *[(near.at[which, k, q], 0, None) for k in range(3)]],
                (near.at[which, 0, q], 0, None),
            )
        last.append(
            [
                links.send(
                    near.at[which, 0, at2(by), pl.ds(0, count), :], near2.at[which, by - 1, pl.ds(0, count), :], to2(by)
                )
                for by in AROUND
            ]
        )
    yield
    for which, (first, count, at1, to1, at2, to2, place_of) in enumerate(halves):
        arrived(last[which])
        add_rows(
            count,
            [(near.at[which, 0, at2(0)], 0, None), *[(near2.at[which, k], 0, None) for k in range(3)]],
            (out, first, None),
        )


def scatter_xz_scratch(rows):
    a, _ = cut(rows)
    return [pltpu.VMEM((2, 3, 4, a, 256), BF16), pltpu.VMEM((2, 3, a, 256), BF16)]


def scatter_grad(links, left, right, out, src, near, near2):
    rows = 2 * out.shape[0]
    for i in range(4):
        cols = slice(512 * i, 512 * (i + 1))
        value = lax.dot_general(
            left[...], right[:, cols], (((0,), (0,)), ((), ())), preferred_element_type=F32
        ).astype(BF16)
        src[0:rows, cols] = value
        yield
    yield from scatter_xz(links, src, out, near, near2)


def row_peers(links):
    peers = []
    for dx in range(4):
        for dz in range(4):
            if (dx, dz) != (0, 0):
                peers.append({"x": links.at_x(dx), **links.to_z(dz)})
    return peers


def block_of(links, dx, dz):
    z = links.at_z(dz)
    return links.at_x(dx) * 4 + lax.rem(z, 2) * 2 + lax.div(z, 2)


def exchange_rows(links, src, out):
    me = block_of(links, 0, 0)
    keep = links.local(src, out.at[me])
    copies = [links.send(src, out.at[me], device) for device in row_peers(links)]
    yield
    arrived(copies)
    keep.wait()


def sum_rows(links, src, out, buf):
    me = block_of(links, 0, 0)
    copies = []
    for dx in range(4):
        for dz in range(4):
            if (dx, dz) != (0, 0):
                device = {"x": links.at_x(dx), **links.to_z(dz)}
                lanes = pl.ds(pl.multiple_of(device["zh"] * LANES, LANES), LANES)
                copies.append(links.send(src.at[:, lanes], buf.at[me], device))
    yield
    arrived(copies)
    total = src[:, pl.ds(pl.multiple_of(links.zh * LANES, LANES), LANES)]
    for dx in range(4):
        for dz in range(4):
            if (dx, dz) != (0, 0):
                total = total + buf[block_of(links, dx, dz)]
    out[...] = total


def swap_pairs(links, ins, outs):
    lanes = pl.ds(pl.multiple_of(links.zh * LANES, LANES), LANES)
    keep, got = [], []
    for src, dst in zip(ins, outs):
        place = dst.at[pl.ds(0, src.shape[1]), lanes]
        got.append(links.send(src.at[1 - links.zh], place, links.to_z(2)))
    for src, dst in zip(ins, outs):
        place = dst.at[pl.ds(0, src.shape[1]), lanes]
        keep.append(links.local(src.at[links.zh], place))
    return got, keep


def unswap_pair(links, src, dst):
    mine = pl.ds(pl.multiple_of(links.zh * LANES, LANES), LANES)
    theirs = pl.ds(pl.multiple_of((1 - links.zh) * LANES, LANES), LANES)
    got = links.send(src.at[:, theirs], dst.at[links.zh], links.to_z(2))
    keep = links.local(src.at[:, mine], dst.at[links.zh])
    yield
    got.wait_recv()
    keep.wait()


def swap_only(links, src, dst):
    got, keep = swap_pairs(links, (src,), (dst,))
    for _ in range(4):
        yield
    arrived(got)
    for copy in keep:
        copy.wait()


def block_device(block):
    block = lax.rem(block + 16, 16)
    return {"x": lax.div(block, 4), "zl": lax.rem(lax.div(block, 2), 2), "zh": lax.rem(block, 2)}


def conv_backward(
    links, gg, u, q, z, k, v, p, halo, taps, m1, m2, ends, enter, free, dec, dec_seg, res, skip, rates, starts,
    gp, res_out, rate_out, skip_out, conv_out, edge, edge_in, back_ends, last, lasts, back_enter, kept, gq, gz,
):
    me = block_of(links, 0, 0)
    for b in range(2):
        back_first(b, gg, q, m1, free, dec, dec_seg, back_ends, last)
        if b == 0:
            yield
    going = exchange_rows(links, last, lasts)
    next(going)
    yield
    finish(going)
    total = jnp.zeros(last.shape, F32)
    for j in range(lasts.shape[0]):
        apart = (jnp.maximum(j - me - 1, 0) * p.shape[0]).astype(F32)
        after = (me < j).astype(F32)
        still = open_between(starts, (me + 1) * p.shape[0], j * p.shape[0])
        total = total + lasts[j] * (after * still * jnp.exp(-rates[...] * apart))
    back_enter[...] = total
    for b in range(2):
        for part in range(2):
            if (b, part) != (0, 0):
                keep_states(b, part, z, m1, ends, enter, free, dec, dec_seg, kept)
                yield
            back_poles(
                b, part, gg, u, q, z, m1, back_ends, back_enter, free, dec, dec_seg, res, skip,
                res_out, rate_out, skip_out, kept, gq, gz,
            )
            yield
        back_taps(b, v, k, p, halo, taps, m1, m2, gp, edge, conv_out, gq, gz)
        yield
    got = links.send(edge, edge_in, block_device(me - 1))
    yield
    got.wait_recv()
    for b in range(2):
        mend_edges(b, taps, edge_in, gp)


def shape(*dims, dtype=F32):
    return jax.ShapeDtypeStruct(dims, dtype)


def finish(*parts):
    for part in parts:
        for _ in part:
            pass


NT = (((1,), (1,)), ((), ()))


def open_between(starts, low, high):
    at = starts[...]
    hit = jnp.where((at >= low) & (at < high), 1.0, 0.0)
    return 1.0 - jnp.max(hit, axis=0, keepdims=True)


def write_masks(block, starts, m1, m2):
    rows = m1.shape[0]
    seg = rows // SEGS
    firsts = [jnp.broadcast_to(starts[j : j + 1, 0:LANES], (SEGS, LANES)) for j in range(DOCS)]
    base = block * rows + seg_rows() * seg

    def carries_on(place):
        hit = place == firsts[0]
        for first in firsts[1:]:
            hit = hit | (place == first)
        return jnp.where(hit, 0.0, 1.0)

    def step(i, earlier):
        one = carries_on(base + i)
        m1[tile(i), :] = one
        m2[tile(i), :] = one * earlier
        return one

    lax.fori_loop(0, seg, step, carries_on(base - 1))


def forward_half(
    links, tok, small, cot_pair, win_t, wout_t, wgate_t, starts, up_t, down,
    xg_out, win_out, wout_out, cs, p_out, q_out, z_out, k_out, v_out, xs_out, hg_out, wdown_out, hidden_out, gh_out,
    u, gated, halo, ends, free, enter, params, r1, m1, m2, acts, gg, gu, dots, r2, sum_down,
    xr, xs, sm, xg, gains, inv, inv_g2, win, p, q, z, k, v, dec, dec_seg, taps, res, skip, last, lasts,
    cot, wout, wgate, wup, wdown, own_dots, dots_buf, *held,
):
    rows, width = xg.shape
    poles = dec.shape[0]
    me = block_of(links, 0, 0)
    got, keep = swap_pairs(links, (small, tok), (sm, xr))
    win_in = gather_xz(links, win_t, win, win_t.shape[0] // 3)
    next(win_in)
    cot_swap = swap_only(links, cot_pair, cs)
    wout_in = gather_xz(links, wout_t, wout)
    wgate_in = gather_xz(links, wgate_t, wgate)
    write_masks(me, starts, m1, m2)
    arrived(got[:1])
    keep[0].wait()
    gain_rows = gather_yc(links, sm.at[pl.ds(0, 32), :], gains)
    next(gain_rows)
    values = sm[...].astype(F32)
    rate = jnp.exp(values[32:48])
    dec[...] = jnp.exp(-rate)
    dec_seg[...] = jnp.exp(-rate * (rows // SEGS))
    taps[...] = values[16:32]
    res[...] = values[48:64]
    skip[...] = jnp.broadcast_to(values[2:3], (SEGS, 2 * LANES))
    params[0:16, :] = values[0:16]
    params[16:32, :] = values[16:32]
    params[32:48, :] = rate
    params[48:64, :] = values[48:64]
    arrived(got[1:])
    keep[1].wait()

    def gained(i, _):
        place = pl.ds(pl.multiple_of(i * 64, 64), 64)
        xs[place, :] = (xr[place, :].astype(F32) * params[0:1, :]).astype(BF16)
        return 0

    lax.fori_loop(0, rows // 64, gained, 0)
    columns = gather_yc(links, xs, xg)
    next(columns)
    next(win_in)
    next(cot_swap)
    next(gain_rows)
    next(gain_rows)
    next(columns)
    next(win_in)
    next(columns)
    next(gain_rows)
    finish(columns)
    finish(gain_rows, win_in)
    inv[...] = 1.0 / gains[0:16, :].astype(F32)
    inv_g2[...] = inv[1:2, :]
    stores = [links.local(xg, xg_out), links.local(win, win_out), links.local(xr, xs_out)]
    step = 256

    def project(i, _):
        place = pl.ds(pl.multiple_of(i * step, step), step)
        r = rows_scale(xg, inv, place, width)
        r1[place, :] = jnp.broadcast_to(r, (step, LANES))
        p[place, :] = r * lax.dot_general(xg[place, :], win[...], NT, preferred_element_type=F32)
        return 0

    lax.fori_loop(0, rows // step, project, 0)
    stores.append(links.local(p, p_out))
    tail = links.send(p.at[pl.ds(rows - 16, 16), :], halo, block_device(me + 1))
    for part in (wgate_in, wout_in):
        next(part)
        next(part)
    finish(cot_swap)
    cot_in = gather_yc(links, cs, cot)
    next(cot_in)
    tail.wait_recv()
    for b in range(2):
        conv_first(b, p, halo, taps, m1, m2, dec, dec_seg, q, z, k, v, ends, free, last)
    going = exchange_rows(links, last, lasts)
    next(going)
    next(cot_in)
    next(wgate_in)
    next(wout_in)
    stores += [links.local(q, q_out), links.local(z, z_out), links.local(k, k_out), links.local(v, v_out)]
    finish(going)
    rates = params[32:48, :]
    total = jnp.zeros((poles, 2 * LANES), F32)
    for j in range(lasts.shape[0]):
        apart = (jnp.maximum(me - 1 - j, 0) * rows).astype(F32)
        before = (me > j).astype(F32)
        total = total + lasts[j] * (before * open_between(starts, (j + 1) * rows, me * rows) * jnp.exp(-rates * apart))
    enter[...] = total
    conv_second(0, q, z, m1, ends, free, enter, dec, dec_seg, res, skip, u, gated)
    next(cot_in)
    conv_second(1, q, z, m1, ends, free, enter, dec, dec_seg, res, skip, u, gated)
    finish(wout_in)
    for copy in stores:
        copy.wait()
    links.settle()
    one, two, held = held[:4], held[4:7], held[7:]
    mixer, hidden, gh = z, v, k
    beside = [gather_xz(links, up_t, wup, 128), gather_xz(links, down, wdown, 128)]
    for part in beside:
        next(part)
    steps = lambda part, count: [next(part, None) for _ in range(count)]
    sums = scatter_yc(links, [(gated, wout)], mixer, *one)
    steps(sums, 2)
    for part in beside:
        next(part)
    steps(sums, 3)
    for part in beside:
        next(part)
    finish(sums, cot_in)

    def residual(i, _):
        place = pl.ds(pl.multiple_of(i * 64, 64), 64)
        value = xr[place, :].astype(F32) + mixer[place, :]
        hidden[place, :] = value
        xs[place, :] = (value * params[1:2, :]).astype(BF16)
        return 0

    lax.fori_loop(0, rows // 64, residual, 0)
    finish(gather_yc(links, xs, xg), wgate_in, *beside)
    links.settle()
    kept = [links.local(wdown, wdown_out), links.local(xg, hg_out), links.local(wout, wout_out)]
    kept.append(links.local(hidden, hidden_out))
    step = 256

    def block(i, _):
        place = pl.ds(pl.multiple_of(i * step, step), step)
        r = rows_scale(xg, inv_g2, place, width)
        r2[place, :] = jnp.broadcast_to(r, (step, LANES))
        h = xg[place, :]
        gate = r * lax.dot_general(h, wgate[...], NT, preferred_element_type=F32)
        upper = r * lax.dot_general(h, wup[...], NT, preferred_element_type=F32)
        g_act = lax.dot_general(cot[place, :], wdown[...], NT, preferred_element_type=F32)
        sig = jax.nn.sigmoid(gate)
        acts[place, :] = (gate * sig * upper).astype(BF16)
        g_gate = g_act * upper * (sig * (1.0 + gate * (1.0 - sig)))
        g_upper = g_act * gate * sig
        gg[place, :] = (r * g_gate).astype(BF16)
        gu[place, :] = (r * g_upper).astype(BF16)
        both = (g_gate * gate + g_upper * upper).astype(BF16)
        own_dots[:, place] = lax.dot_general(
            jnp.ones((8, both.shape[1]), BF16), both, NT, preferred_element_type=F32
        )
        return 0

    lax.fori_loop(0, rows // step, block, 0)
    parts = [
        scatter_yc(links, [(gg, wgate), (gu, wup)], gh, one[0], *two),
        scatter_grad(links, acts, cot, sum_down, win, *held),
        sum_dots(links, own_dots, dots, dots_buf),
    ]
    interleave(parts, "bbbbbcaaaaabaa")
    kept.append(links.local(gh, gh_out))
    for copy in kept:
        copy.wait()


def rows_scale(x, gain, place, width):
    square = jnp.zeros((place.size, LANES), F32)
    for k in range(width // LANES):
        lanes = slice(LANES * k, LANES * (k + 1))
        plain = x[place, lanes].astype(F32) * gain[0:1, lanes]
        square = square + plain * plain
    return lax.rsqrt(jnp.sum(square, axis=1, keepdims=True) / width + EPS)


def dots_column(dots):
    line = lax.broadcasted_iota(jnp.int32, dots.shape, 0)
    value = dots[...]
    high = value.astype(BF16).astype(F32)
    pair = jnp.where(line == 0, high, jnp.where(line == 1, value - high, 0.0)).astype(BF16)
    return lax.dot_general(
        pair, jnp.ones((8, LANES), BF16), (((0,), (0,)), ((), ())), preferred_element_type=F32
    )


def mixer_back(
    links, gh_in, cs_in, r2_in, dots, params, wout, gated, acts, wdown, gg_low, gu_low, hg, hidden, u, q, z, k, v, p, halo, taps, m1, m2,
    ends, enter, free, dec, dec_seg, res, skip, rates, starts,
    g_hidden, gain2, gp, res_out, rate_out, skip_out, conv_out, mixed, sum_gate, sum_up, sum_out,
    g_mix, gg, mlp, mixed_half, edge, edge_in, back_ends, last, lasts, back_enter, kept, gq, gz, *held,
):
    rows = gg.shape[0]
    loads = [links.local(gh_in, mlp), links.local(cs_in, mixed_half), links.local(r2_in, gq)]
    for copy in loads:
        copy.wait()
    pull = gq[...] * gq[...] * dots_column(dots) / g_mix.shape[1]
    for b in range(2):
        lanes = lanes_of(b)
        back, h = mlp[:, lanes], hidden[:, lanes]
        value = mixed_half[:, lanes].astype(F32) + params[1:2, lanes] * back - h * pull
        gg[:, lanes] = value
        mixed_half[:, lanes] = value.astype(BF16)
        gain2[0:1, lanes] = jnp.sum(back * h, axis=0, keepdims=True)
    store = links.local(gg, g_hidden)
    columns = gather_yc(links, mixed_half, g_mix)
    gate = scatter_grad(links, gg_low, hg, sum_gate, *held[4:7])
    up = scatter_grad(links, gu_low, hg, sum_up, *held[7:10])
    out = scatter_grad(links, gated, g_mix, sum_out, *held[10:13])
    down = scatter_yc(links, [(acts, wdown)], mlp, *held[:4])
    steps = lambda part, count: [next(part, None) for _ in range(count)]
    steps(columns, 1)
    early, links.open = links.open, []
    steps(gate, 5)
    steps(columns, 1)
    steps(up, 5)
    steps(columns, 2)
    steps(down, 2)
    keep_states(0, 0, z, m1, ends, enter, free, dec, dec_seg, kept)
    finish(columns)
    store.wait()
    gg[...] = lax.dot_general(g_mix[...], wout[...], NT, preferred_element_type=F32)
    back = conv_backward(
        links, gg, u, q, z, k, v, p, halo, taps, m1, m2, ends, enter, free, dec, dec_seg, res, skip, rates, starts,
        gp, res_out, rate_out, skip_out, conv_out, edge, edge_in, back_ends, last, lasts, back_enter, kept, gq, gz,
    )
    steps(back, 2)
    steps(down, 2)
    steps(gate, 1)
    steps(up, 1)
    steps(back, 1)
    steps(down, 1)
    steps(out, 5)
    steps(back, 1)
    finish(gate)
    steps(back, 1)
    steps(down, 1)
    steps(out, 1)
    steps(back, 1)
    finish(up)
    steps(back, 1)
    finish(down)

    for copy in early:
        copy.wait_send()

    def mix(i, _):
        place = pl.ds(pl.multiple_of(i * 64, 64), 64)
        mixed_half[place, :] = (hidden[place, :] + mlp[place, :]).astype(BF16)
        return 0

    lax.fori_loop(0, rows // 64, mix, 0)
    swapped = unswap_pair(links, mixed_half, mixed)
    steps(swapped, 1)
    finish(back, out, swapped)


def input_back(
    links, gp, p, r1, xg, win, g_hidden, xs, g1, conv, rate_raw, res_raw, skip_raw, rate, res, gain2,
    sum_in, grad, tiny_out,
    gp_low, own_dots, dots, dots_buf, gx, grad_half, tiny, tiny_buf, *held,
):
    rows = gp.shape[0]
    width = xg.shape[1]
    step = 256

    def scale(i, _):
        place = pl.ds(pl.multiple_of(i * step, step), step)
        value = gp[place, :]
        both = (value * p[place, :]).astype(BF16)
        own_dots[:, place] = lax.dot_general(
            jnp.ones((8, both.shape[1]), BF16), both, NT, preferred_element_type=F32
        )
        gp_low[place, :] = (r1[place, 0:1] * value).astype(BF16)
        return 0

    lax.fori_loop(0, rows // step, scale, 0)
    parts = [
        scatter_yc(links, [(gp_low, win)], gx, *held[:4]),
        sum_dots(links, own_dots, dots, dots_buf),
        scatter_grad(links, gp_low, xg, sum_in, *held[4:]),
    ]
    for letter in "bcccccaaaaaca":
        next(parts[ord(letter) - ord("a")], None)
    finish(parts[0], parts[1])
    tiny[...] = jnp.zeros_like(tiny)
    pull = r1[...] * r1[...] * dots_column(dots) / width
    for b in range(2):
        lanes = lanes_of(b)
        x = xs[:, lanes].astype(F32)
        got = gx[:, lanes]
        grad_half[:, lanes] = (g_hidden[:, lanes] + g1[0:1, lanes] * got - x * pull).astype(BF16)
        tiny[0:1, lanes] = jnp.sum(got * x, axis=0, keepdims=True)
    tiny[1:2, :] = gain2[...]
    tiny[2:3, :] = jnp.sum(skip_raw[...], axis=0, keepdims=True)
    tiny[8:24, :] = conv[...]
    tiny[24:40, :] = -rate[...] * res[...] * rate_raw[...]
    tiny[40:56, :] = res_raw[...]
    swapped = unswap_pair(links, grad_half, grad)
    summed = sum_rows(links, tiny, tiny_out, tiny_buf)
    next(swapped)
    next(summed)
    finish(parts[2], summed, swapped)


def fused(number, maker, peers, inputs, outs, scratch, copies):
    vmem = pl.BlockSpec(memory_space=pltpu.VMEM)
    hbm = pl.BlockSpec(memory_space=pl.ANY)
    staged = [i for i, (_, kind) in enumerate(inputs) if kind == "s"]
    n_in, n_out = len(inputs), len(outs)

    def kernel(*refs):
        ins, results = list(refs[:n_in]), refs[n_in : n_in + n_out]
        held = refs[n_in + n_out : -2]
        links = Links(refs[-2], refs[-1])
        moves = []
        for i, buf in zip(staged, held):
            moves.append(links.local(ins[i], buf))
            ins[i] = buf
        met = []
        if "Y" in peers:
            met += yc_peers(links)
        elif "y" in peers:
            met += [links.to_y(1), links.to_y(-1), links.sibling()]
        if "r" in peers:
            met += row_peers(links)
        elif "x" in peers:
            met += xz_peers(links)
        links.greet(met)
        for move in moves:
            move.wait()
        maker(links, *ins, *results, *held[len(staged) :])
        links.settle()
        assert links.used <= copies

    return pl.pallas_call(
        kernel,
        in_specs=[vmem if kind == "v" else hbm for _, kind in inputs],
        out_specs=[vmem if kind == "v" else hbm for _, kind in outs],
        out_shape=[kept for kept, _ in outs],
        scratch_shapes=[
            *[pltpu.VMEM(inputs[i][0].shape, inputs[i][0].dtype) for i in staged],
            *scratch,
            pltpu.SemaphoreType.DMA((copies,)),
            pltpu.SemaphoreType.DMA((copies,)),
        ],
        compiler_params=pltpu.CompilerParams(
            collective_id=number, has_side_effects=True, vmem_limit_bytes=VMEM_LIMIT
        ),
    )(*[array for array, _ in inputs])


def grad_scratch(rows):
    return [pltpu.VMEM((2 * rows, 2048), BF16), *scatter_xz_scratch(rows)]


def shards(
    tokens, gain_first, gain_second, w_in, conv_w, log_rate, residue, skip,
    w_out, w_gate, w_up, w_down, cotangent, lengths,
):
    rows = tokens.shape[0] // 2
    width = 16 * LANES
    seg = rows // SEGS

    def stepped(value):
        return value.reshape(2, SEGS, seg, LANES).transpose(0, 2, 1, 3).reshape(2, rows, LANES)

    def unstepped(value):
        return value.reshape(2, seg, SEGS, LANES).transpose(0, 2, 1, 3).reshape(2 * rows, LANES)

    before = jnp.arange(DOCS)[:, None] < jnp.arange(DOCS)[None, :]
    starts = jnp.sum(jnp.where(before, lengths[:, None], 0), axis=0)
    starts = jnp.broadcast_to(starts[:, None], (DOCS, 2 * LANES))

    line = lax.broadcasted_iota(jnp.int32, (16, LANES), 0)
    singles = jnp.where(line == 0, gain_first, jnp.where(line == 1, gain_second, jnp.where(line == 2, skip, 0)))
    taps_own = jnp.pad(conv_w.reshape(9, LANES), ((0, 7), (0, 0)))
    small = jnp.concatenate([singles.astype(BF16), taps_own, log_rate, residue])
    hidden_units = w_gate.shape[1]
    half = (rows, 2 * LANES)
    weight = (2 * hidden_units, width)
    act = shape(*half)
    low = shape(*half, dtype=BF16)
    proj_shape = shape(rows, 6 * LANES)
    units = shape(rows, 2 * hidden_units, dtype=BF16)
    broad = shape(rows, width, dtype=BF16)
    sixteen = shape(16, 2 * LANES)
    vm = lambda kept: pltpu.VMEM(kept.shape, kept.dtype)
    (
        xg, win, wout, cs, proj, q, z, k, v, xs, hg, wdown, hidden, gh, u, gated, halo, seg_ends, free, enter, params,
        r1, mask1, mask2, acts, gg_low, gu_low, dot2, r2, sums_down,
    ) = fused(
        1,
        forward_half,
        "Yr",
        [
            (stepped(tokens), "h"), (jnp.broadcast_to(small[None], (2, 64, LANES)), "h"), (stepped(cotangent), "h"),
            (w_in.transpose(1, 2, 0).reshape(3 * LANES, 256), "h"), (w_out, "h"), (w_gate.T, "h"),
            (starts, "v"), (w_up.T, "h"), (w_down, "h"),
        ],
        [
            (broad, "h"), (shape(6 * LANES, width, dtype=BF16), "h"), (shape(2 * LANES, width, dtype=BF16), "h"),
            (low, "h"), (proj_shape, "h"), (act, "h"), (act, "h"), (act, "h"), (act, "h"), (low, "h"), (broad, "h"),
            (shape(*weight, dtype=BF16), "h"), (act, "h"), (act, "h"),
            (act, "v"), (low, "v"), (shape(16, 768), "v"), (shape(128, 256), "v"), (shape(8, 256), "v"),
            (sixteen, "v"), (shape(64, 256), "v"), (shape(rows, LANES), "v"), (shape(rows, LANES), "v"),
            (shape(rows, LANES), "v"), (units, "v"), (units, "v"), (units, "v"),
            (shape(8, rows), "v"), (shape(rows, LANES), "v"), (shape(hidden_units, 2 * LANES), "v"),
        ],
        [
            vm(low), vm(low), pltpu.VMEM((64, 256), BF16), vm(broad), pltpu.VMEM((32, width), BF16),
            pltpu.VMEM((16, width), F32), pltpu.VMEM((1, width), F32), pltpu.VMEM((6 * LANES, width), BF16),
            vm(proj_shape), *([vm(act)] * 4), vm(sixteen), vm(sixteen), vm(sixteen), vm(sixteen),
            pltpu.VMEM((8, 256), F32), vm(sixteen), pltpu.VMEM((16, 16, 256), F32),
            vm(broad), pltpu.VMEM((2 * LANES, width), BF16), *([pltpu.VMEM(weight, BF16)] * 3),
            pltpu.VMEM((8, rows), F32), pltpu.VMEM((8, 8, rows), F32),
            *scatter_yc_scratch(rows), *scatter_yc_scratch(rows)[1:], *scatter_xz_scratch(hidden_units),
        ],
        400,
    )
    g1 = params[0:1]
    skip8 = jnp.broadcast_to(params[2:3], (8, 2 * LANES))
    taps, rate, res = params[16:32], params[32:48], params[48:64]
    dec = jnp.exp(-rate)
    dec_seg = jnp.exp(-rate * seg)

    g_hidden, grad_gain2, g_proj, res_raw, rate_raw, skip_raw, conv_raw, mixed, sums_gate, sums_up, sums_out = fused(
        4,
        mixer_back,
        "yr",
        [
            (gh, "h"), (cs, "h"), (r2, "h"), (dot2, "v"), (params, "v"), (wout, "s"), (gated, "s"), (acts, "s"), (wdown, "s"), (gg_low, "s"),
            (gu_low, "s"), (hg, "s"), (hidden, "s"), (u, "s"), (q, "s"), (z, "s"), (k, "s"), (v, "s"), (proj, "s"),
            (halo, "v"), (taps, "v"), (mask1, "s"), (mask2, "s"), (seg_ends, "v"), (enter, "v"), (free, "v"),
            (dec, "v"), (dec_seg, "v"), (res, "v"), (skip8, "v"), (rate, "v"), (starts, "v"),
        ],
        [
            (act, "h"), (shape(1, 2 * LANES), "v"), (proj_shape, "v"), (sixteen, "v"), (sixteen, "v"), (shape(8, 2 * LANES), "v"), (sixteen, "v"),
            (shape(2, rows, LANES, dtype=BF16), "h"), *[(shape(hidden_units, 2 * LANES), "v")] * 2,
            (shape(LANES, 2 * LANES), "v"),
        ],
        [
            pltpu.VMEM((rows, width), BF16), pltpu.VMEM(half, F32), pltpu.VMEM(half, F32), pltpu.VMEM(half, BF16),
            pltpu.VMEM((24, 6 * LANES), F32), pltpu.VMEM((24, 6 * LANES), F32), pltpu.VMEM((128, 256), F32),
            pltpu.VMEM((16, 256), F32), pltpu.VMEM((16, 16, 256), F32), pltpu.VMEM((16, 256), F32),
            pltpu.VMEM((seg, 8, SEGS, LANES), F32), pltpu.VMEM((rows, LANES), F32), pltpu.VMEM((rows, LANES), F32),
            *scatter_yc_scratch(rows), *(grad_scratch(hidden_units) * 2), *grad_scratch(LANES),
        ],
        220,
    )
    sums_in, grad_tok, tiny = fused(
        5,
        input_back,
        "Yr",
        [
            (g_proj, "s"), (proj, "s"), (r1, "s"), (xg, "s"), (win, "s"), (g_hidden, "s"), (xs, "s"), (g1, "v"),
            (conv_raw, "v"), (rate_raw, "v"), (res_raw, "v"), (skip_raw, "v"), (rate, "v"), (res, "v"),
            (grad_gain2, "v"),
        ],
        [
            (shape(3 * LANES, 2 * LANES), "v"), (shape(2, rows, LANES, dtype=BF16), "h"), (shape(56, LANES), "v"),
        ],
        [
            pltpu.VMEM((rows, 6 * LANES), BF16), pltpu.VMEM((8, rows), F32), pltpu.VMEM((8, rows), F32),
            pltpu.VMEM((8, 8, rows), F32), pltpu.VMEM(half, F32), pltpu.VMEM(half, BF16), pltpu.VMEM((56, 256), F32),
            pltpu.VMEM((16, 56, LANES), F32), *scatter_yc_scratch(rows), *grad_scratch(3 * LANES),
        ],
        120,
    )
    return (
        unstepped(mixed),
        unstepped(grad_tok).astype(F32),
        tiny[0],
        tiny[1],
        sums_in.reshape(3, LANES, 256).transpose(2, 0, 1),
        tiny[8:17].reshape(3, 3, LANES),
        tiny[24:40],
        tiny[40:56],
        tiny[2],
        sums_out,
        sums_gate.T,
        sums_up.T,
        sums_down,
    )


def solution(mesh):
    cube = Mesh(mesh.devices.reshape(4, 2, 2, 4, 2), ("x", "zl", "zh", "y", "c"))
    seq, tp = ("x", "zl"), ("zh", "y", "c")
    return jax.shard_map(
        shards,
        mesh=cube,
        in_specs=(
            P(seq, tp), P(tp), P(tp), P(seq, None, tp), P(None, None, tp), P(None, tp), P(None, tp), P(tp),
            P(tp, seq), P(seq, tp), P(seq, tp), P(tp, seq), P(seq, tp), P(),
        ),
        out_specs=(
            P(seq, tp), P(seq, tp), P(tp), P(tp), P(seq, None, tp), P(None, None, tp), P(None, tp), P(None, tp), P(tp),
            P(tp, seq), P(seq, tp), P(seq, tp), P(tp, seq),
        ),
        check_vma=False,
    )
```
